32 devices in a mesh: site: 4 (over y, x), fsdp: 8 (over z, core).
Axes of the slice: x: 2, y: 2, z: 4, core: 2. Of those that a mesh axis runs over, the one named last changes fastest.
Arguments:
- held_input: bfloat16 [4, 4096, 1536], P('site', 'fsdp'), may hold values from -6 to 6
- held_cotangent: bfloat16 [4, 4096, 1536], P('site', 'fsdp'), may hold values from -6 to 6
- proj_weight: bfloat16 [1536, 1536], P('fsdp'), may hold values from -0.15625 to 0.15625
- stem_weight: bfloat16 [3, 512, 1536], P(None, 'fsdp'), may hold values from -0.15625 to 0.15625
- seg_counts: int32 [4, 8], P('site'), may hold values from 1 to 128, 512 in all within a row
Outputs:
- stem_grad: bfloat16 [4, 16384, 512], P('site', 'fsdp')
- weight_grad: float32 [1536, 1536], P('fsdp')
The draws below stay inside these ranges and needn't reach their ends.
Inputs may be any that keep to these rules, and one draw needn't show every extreme that they name: `seg_counts`: in every group the 8 counts sum to 512, so that every holder slot is used; one owner has exactly 128, and a holder keeps at most 16 segments of one owner, a bound reached in every draw.
All inputs are finite; a program needn't handle non-finite values.
Results may differ from the reference program's by a relative error of at most 0.0049.
Values may be sent and summed in bfloat16 or wider, within the bound.
No kernel may reach another device: no remote copies, remote signals or barrier semaphores. Data moves between devices by JAX's collectives and lax.ppermute only.
A program may use at most 128 MiB of HBM per device.

```python
import math
import jax
import jax.numpy as jnp
import numpy as np
from jax import lax

D = 1536
CS = 512
SEG = 8
HOLD = 64
OWN_SEG = 128
N_SITE = 4
N_FSDP = 8


def with_spikes(values, key, source, target, shards_of, factor):
    def block_of(position):
        return (jnp.arange(values.shape[position]) // (values.shape[position] // shards_of)).reshape((-1,) + (1,) * (values.ndim - 1 - position))

    near = jax.random.permutation(key, shards_of)[block_of(target)]
    second = (block_of(target) + shards_of // 2) % shards_of
    return jnp.where((block_of(source) == near) | (block_of(source) == second), factor * values, values)


def block_levels(own_key, extent, pieces, smallest, high):
    gain = 1.0
    for position, parts in pieces:
        draws = jax.random.uniform(jax.random.fold_in(jax.random.fold_in(own_key, 6), position), (parts,), jnp.float32, smallest / len(pieces), high / len(pieces))
        gain = gain * jnp.repeat(jnp.exp(draws), extent[position] // parts).reshape((-1,) + (1,) * (len(extent) - 1 - position))
    return gain


def length_profile(amount, total, bound, lean):
    weights = [(1 << 20) // math.isqrt(rank ** lean) + 1 for rank in range(2, amount + 1)]
    surplus, holding = total - bound - (amount - 1), [1] * (amount - 1)
    while surplus > 0:
        candidates = [i for i in range(amount - 1) if holding[i] < bound]
        mass, budget = sum([weights[i] for i in candidates]), surplus
        for i in candidates:
            more = min(bound - holding[i], max(1, budget * weights[i] // mass), surplus)
            holding[i] = holding[i] + more
            surplus = surplus - more
    return np.array([bound] + holding)


def uneven_parts(rng, count, total, limit, lean):
    if count == 2:
        one = jax.random.randint(rng, (), max(1, total - limit), min(limit, total - 1) + 1)
        return jnp.stack([one, total - one])
    sizes = jnp.asarray(length_profile(count, total, limit, lean), jnp.int32)
    couples = (count - 1) // 2
    donor, sink = sizes[1:1 + 2 * couples:2], sizes[2:2 + 2 * couples:2]
    slack = jnp.minimum(donor - 1, limit - sink)
    moved = jax.random.randint(jax.random.fold_in(rng, 1), (couples,), 0, 1 << 20) % (slack + 1)
    sizes = sizes.at[1:1 + 2 * couples:2].set(donor - moved).at[2:2 + 2 * couples:2].set(sink + moved)
    return sizes[jax.random.permutation(jax.random.fold_in(rng, 2), count)]


def gaussian(rng, extent, spread, bound, split=(), held_as=jnp.bfloat16):
    loudness = block_levels(rng, extent, split, -0.22, 0.18) if split else 1.0
    result = jax.random.normal(rng, extent, jnp.float32) * spread * loudness
    return jnp.minimum(jnp.maximum(result, -bound), bound).astype(held_as)


def heavy_noise(stream_key, dims, spread, bound, shards, heavy, kind=jnp.bfloat16):
    entries = spread * jax.random.normal(stream_key, dims, jnp.float32)
    if shards:
        entries = entries * block_levels(stream_key, dims, shards, -0.22, 0.18)
    return jnp.clip(with_spikes(entries, jax.random.fold_in(stream_key, 3), *heavy), -bound, bound).astype(kind)


def setup_inputs(seed: int = 0) -> dict:
    key_list = jax.random.split(jax.random.key(seed), 6)
    held_input = heavy_noise(key_list[0], (N_SITE, N_FSDP * HOLD * SEG, D), 1.0, 6.0, ((0, 4), (1, 8)), (1, 2, 8, 2.0))
    held_cotangent = gaussian(key_list[1], (N_SITE, N_FSDP * HOLD * SEG, D), 1.0, 6.0, ((0, 4), (1, 8)))
    proj_weight = gaussian(key_list[2], (D, D), D ** -0.5, 0.15625, ((0, 8),))
    stem_weight = gaussian(key_list[3], (3, CS, D), (3 * CS) ** -0.5, 0.15625, ((1, 8),))
    seg_counts = jax.vmap(lambda own: uneven_parts(own, N_FSDP, N_FSDP * HOLD, OWN_SEG, 2))(jax.random.split(key_list[4], N_SITE)).reshape((N_SITE, N_FSDP)).astype(jnp.int32)
    return dict(held_input=held_input, held_cotangent=held_cotangent, proj_weight=proj_weight, stem_weight=stem_weight, seg_counts=seg_counts)


EPSILON = 1e-05

def owner_grad_rows(input_grad, counts):
    group_size = N_FSDP
    starts = jnp.cumsum(counts) - counts
    segment = jnp.arange(OWN_SEG, dtype=jnp.int32)
    item_index = starts[:, None] + segment[None, :]
    is_live = segment[None, :] < counts[:, None]
    holder = item_index // 2 % group_size
    slot_ids = 2 * (item_index // (2 * group_size)) + item_index % 2
    row_index = jnp.where(is_live, holder * HOLD + slot_ids, 0).astype(jnp.int32)
    blocks_all = input_grad.reshape(group_size * HOLD, SEG, D)
    picked = jnp.take(blocks_all, row_index.reshape(-1), axis=0).reshape(group_size, OWN_SEG * SEG, D)
    mask_rows = jnp.repeat(is_live, SEG, axis=1)
    return jnp.where(mask_rows[:, :, None], picked, jnp.zeros((), jnp.bfloat16))

def stem_backward(frames, stem_weight):
    tap_terms = [jnp.dot(frames, stem_weight[tap_id].T, preferred_element_type=jnp.float32) for tap_id in range(3)]
    shifted = jnp.concatenate([tap_terms[0][1:], jnp.zeros((1, CS), jnp.float32)], 0)
    odd_rows = tap_terms[2] + shifted
    return jnp.stack([tap_terms[1], odd_rows], 1).reshape(2 * frames.shape[0], CS).astype(jnp.bfloat16)

def reference(held_input, held_cotangent, proj_weight, stem_weight, seg_counts):
    grad_total = jnp.zeros((D, D), jnp.float32)
    stem_list = []
    for group_id in range(N_SITE):
        inputs = held_input[group_id].astype(jnp.float32)
        cotangent = held_cotangent[group_id]
        row_mean = lax.optimization_barrier(jnp.mean(inputs, axis=-1, keepdims=True))
        centered = inputs - row_mean
        variance = lax.optimization_barrier(jnp.mean(centered * centered, axis=-1, keepdims=True))
        inverse = lax.rsqrt(variance + EPSILON)
        normed = centered * inverse
        normed_bf = normed.astype(jnp.bfloat16)
        grad_total = grad_total + jnp.dot(normed_bf.T, cotangent, preferred_element_type=jnp.float32)
        proj_back = jnp.dot(cotangent, proj_weight.T, preferred_element_type=jnp.float32)
        input_grad = cotangent.astype(jnp.float32) + inverse * (proj_back - lax.optimization_barrier(jnp.mean(proj_back, axis=-1, keepdims=True)) - normed * lax.optimization_barrier(jnp.mean(proj_back * normed, axis=-1, keepdims=True)))
        input_grad = input_grad.astype(jnp.bfloat16)
        owner_frames = owner_grad_rows(input_grad, seg_counts[group_id])
        stems = lax.map(lambda frames: stem_backward(frames, stem_weight), owner_frames)
        stem_list.append(stems.reshape(N_FSDP * 2 * OWN_SEG * SEG, CS))
    stem_grad = jnp.stack(stem_list, 0)
    weight_grad = grad_total / math.sqrt(N_SITE * N_FSDP * HOLD * SEG)
    return (stem_grad, weight_grad)
```

```python
import math

import jax
import jax.numpy as jnp
from jax import lax
from jax.experimental import pallas as pl
from jax.experimental.pallas import tpu as pltpu
from jax.sharding import PartitionSpec as P

D = 1536
SEG = 8
HOLD = 64
OWN_SEG = 128
N_SITE = 4
N_FSDP = 8
N_Z = N_FSDP // 2
QUARTER = D // N_SITE
CAP = OWN_SEG // N_FSDP
CS = 512
ROWS = HOLD * SEG
BLOCK = 128
LANES = 128
VMEM_LIMIT = 40 * 1024 * 1024

EPSILON = 1e-05
F32 = jnp.float32
BF16 = jnp.bfloat16


def swap_core(value):
    return lax.ppermute(value, "fsdp", [(i, i ^ 1) for i in range(N_FSDP)])


def swap_z(value, distance):
    return lax.ppermute(value, "fsdp", [(i, i ^ (2 * distance)) for i in range(N_FSDP)])


def swap_site(value, distance):
    return lax.ppermute(value, "site", [(i, i ^ distance) for i in range(N_SITE)])


def gather_parts(shard, site):
    quarter = lax.dynamic_slice_in_dim(shard, site * QUARTER, QUARTER, 2)
    others = jnp.stack([swap_z(quarter, distance) for distance in (1, 2, 3)])
    parts = [shard, others] + [swap_site(others, distance) for distance in (1, 2, 3)]
    return parts + [swap_core(part) for part in parts]


def call(kernel, name, out_shape, grid, in_specs, out_specs, scratch, flops, moved):
    return pl.pallas_call(
        kernel,
        name=name,
        out_shape=out_shape,
        grid_spec=pltpu.PrefetchScalarGridSpec(
            num_scalar_prefetch=1,
            grid=grid,
            in_specs=in_specs,
            out_specs=out_specs,
            scratch_shapes=scratch,
        ),
        compiler_params=pltpu.CompilerParams(
            dimension_semantics=("arbitrary",) * len(grid), vmem_limit_bytes=VMEM_LIMIT
        ),
        cost_estimate=pl.CostEstimate(flops=flops, bytes_accessed=moved, transcendentals=0),
    )


ANY = pl.BlockSpec(memory_space=pl.ANY)


def whole(shape):
    return pl.BlockSpec(shape, lambda i, scalars: (0,) * len(shape))


def row_block(rows, columns):
    return pl.BlockSpec((rows, columns), lambda i, scalars: (i, 0))


def shape(dims, dtype):
    return jax.ShapeDtypeStruct(dims, dtype)


def dot_nt(a, b):
    return lax.dot_general(a, b, (((1,), (1,)), ((), ())), preferred_element_type=F32)


def normalise(inputs):
    inputs = inputs.astype(F32)
    centered = inputs - jnp.mean(inputs, axis=-1, keepdims=True)
    variance = jnp.mean(centered * centered, axis=-1, keepdims=True)
    inverse = lax.rsqrt(variance + EPSILON)
    return centered * inverse, inverse


def norm_kernel(scalars, x_ref, own_ref, other_ref, turned):
    core = scalars[1] % 2
    normed, _ = normalise(x_ref[...])
    turned[...] = normed.astype(BF16).T
    shard = D // N_FSDP
    for z in range(N_Z):
        rows = pl.ds(z * shard, shard)
        mine = pl.multiple_of((2 * z + core) * shard, shard)
        theirs = pl.multiple_of((2 * z + 1 - core) * shard, shard)
        own_ref[rows, :] = turned[pl.ds(mine, shard), :]
        other_ref[rows, :] = turned[pl.ds(theirs, shard), :]


def norm_halves(scalars, inputs):
    half = shape((D // 2, ROWS), BF16)
    out = pl.BlockSpec((D // 2, BLOCK), lambda i, scalars: (0, i))
    return call(
        norm_kernel, "norm_halves", (half, half), (ROWS // BLOCK,), [row_block(BLOCK, D)],
        (out, out), [pltpu.VMEM((D, BLOCK), BF16)], 10 * ROWS * D, 4 * ROWS * D,
    )(scalars, inputs)


def outer_kernel(scalars, na_ref, nb_ref, ca_ref, cb_ref, own_ref, p1_ref, p2_ref, p3_ref):
    step = pl.program_id(0)
    total = jnp.dot(na_ref[...], ca_ref[...], preferred_element_type=F32)
    total = total + jnp.dot(nb_ref[...], cb_ref[...], preferred_element_type=F32)

    @pl.when(step == 3)
    def _():
        own_ref[...] = total

    for at, ref in enumerate((p1_ref, p2_ref, p3_ref)):

        @pl.when(step == at)
        def _(ref=ref):
            ref[...] = total.astype(BF16)


def outer_pieces(scalars, normed_a, normed_b, cotangent_a, cotangent_b):
    dims = (D // 2, QUARTER)
    column = pl.BlockSpec(
        (ROWS, QUARTER), lambda i, scalars: (0, lax.bitwise_xor(scalars[0], lax.rem(i + 1, 4)))
    )
    return call(
        outer_kernel, "outer_pieces", (shape(dims, F32),) + (shape(dims, BF16),) * 3, (N_SITE,),
        [whole((D // 2, ROWS))] * 2 + [column] * 2, (whole(dims),) * 4, [],
        2 * ROWS * D * D, 6 * ROWS * D + 3 * D * D,
    )(scalars, normed_a, normed_b, cotangent_a, cotangent_b)


def site_sum_kernel(scalars, own_ref, a_ref, b_ref, c_ref, o0_ref, o1_ref, o2_ref, o3_ref):
    shard = D // N_FSDP
    z = scalars[1] // 2
    for distance, ref in enumerate((o0_ref, o1_ref, o2_ref, o3_ref)):
        rows = pl.ds(pl.multiple_of(lax.bitwise_xor(z, distance) * shard, shard), shard)
        total = own_ref[rows, :]
        for part in (a_ref, b_ref, c_ref):
            total = total + part[rows, :].astype(F32)
        ref[...] = total.astype(ref.dtype)


def site_sum(scalars, own, parts):
    dims, out = (D // 2, QUARTER), (D // N_FSDP, QUARTER)
    return call(
        site_sum_kernel, "site_sum", (shape(out, F32),) + (shape(out, BF16),) * 3, (1,),
        [whole(dims)] * 4, (whole(out),) * 4, [], 4 * dims[0] * dims[1], 14 * dims[0] * dims[1],
    )(scalars, own, *parts)


def z_sum_kernel(scale, scalars, own_ref, a_ref, b_ref, c_ref, out_ref):
    total = own_ref[...]
    for part in (a_ref, b_ref, c_ref):
        total = total + part[...].astype(F32)
    out_ref[...] = total * scale


def z_sum(scalars, own, parts, scale):
    dims = (D // N_FSDP, QUARTER)
    return call(
        lambda *refs: z_sum_kernel(scale, *refs), "z_sum", shape(dims, F32), (1,),
        [whole(dims)] * 4, whole(dims), [], 4 * dims[0] * dims[1], 14 * dims[0] * dims[1],
    )(scalars, own, *parts)


def lay_columns_kernel(scalars, a_ref, b_ref, c_ref, d_ref, out_ref):
    for distance, ref in enumerate((a_ref, b_ref, c_ref, d_ref)):
        at = pl.multiple_of(lax.bitwise_xor(scalars[0], distance) * QUARTER, QUARTER)
        out_ref[:, pl.ds(at, QUARTER)] = ref[...]


def lay_columns(scalars, parts):
    dims = (D // N_FSDP, QUARTER)
    out = (D // N_FSDP, D)
    return call(
        lay_columns_kernel, "lay_columns", shape(out, F32), (1,), [whole(dims)] * 4, whole(out),
        [], 0, 8 * out[0] * out[1],
    )(scalars, *parts)


def weight_copies(scalars, parts, weight, sem):
    site, index = scalars[0], scalars[1]
    rows = weight.shape[1] // N_FSDP
    copies = []

    def add(source, at, columns):
        place = weight.at[:, pl.ds(pl.multiple_of(at * rows, rows), rows), columns]
        copies.append(pltpu.make_async_copy(source, place, sem))

    for swapped in (0, 1):
        core_index = lax.bitwise_xor(index, swapped)
        shard, *quarters = parts[5 * swapped : 5 * swapped + 5]
        add(shard, core_index, pl.ds(0, D))
        for distance, ref in enumerate(quarters):
            at = pl.multiple_of(lax.bitwise_xor(site, distance) * QUARTER, QUARTER)
            for z in (1, 2, 3):
                add(ref.at[z - 1], lax.bitwise_xor(core_index, 2 * z), pl.ds(at, QUARTER))
    return copies


def fetch_weight(scalars, parts, weight, sem):
    @pl.when(pl.program_id(0) == 0)
    def _():
        copies = weight_copies(scalars, parts, weight, sem)
        for copy in copies:
            copy.start()
        for copy in copies:
            copy.wait()


def input_grad_kernel(scalars, *refs):
    parts, (x_ref, cot_ref, out_ref, weight, sem) = refs[:10], refs[10:]
    fetch_weight(scalars, parts, weight, sem)
    cotangent = cot_ref[...]
    back = dot_nt(cotangent, weight[0])
    normed, inverse = normalise(x_ref[...])
    inner = back - jnp.mean(back, axis=-1, keepdims=True)
    inner = inner - normed * jnp.mean(back * normed, axis=-1, keepdims=True)
    out_ref[...] = (cotangent.astype(F32) + inverse * inner).astype(BF16)


def input_gradient(scalars, parts, inputs, cotangent):
    return call(
        input_grad_kernel, "input_gradient", shape((ROWS, D), BF16), (ROWS // BLOCK,),
        [ANY] * 10 + [row_block(BLOCK, D)] * 2, row_block(BLOCK, D),
        [pltpu.VMEM((1, D, D), BF16), pltpu.SemaphoreType.DMA], 2 * ROWS * D * D,
        2 * D * D + 6 * ROWS * D,
    )(scalars, *parts, inputs, cotangent)


def starts_of(scalars):
    starts = [jnp.int32(0)]
    for owner in range(N_FSDP):
        starts.append(starts[-1] + scalars[2 + owner])
    return starts


def held_before(start, holder):
    return 2 * (start // (2 * N_FSDP)) + jnp.clip(start % (2 * N_FSDP) - 2 * holder, 0, 2)


def stem_kernel(scalars, *refs):
    parts, grad_ref, outs = refs[:10], refs[10], refs[11:19]
    weight, mixed, packed, firsts, sem, out_sem = refs[19:]
    fetch_weight(scalars, parts, weight, sem)
    step = pl.program_id(0)
    index = scalars[1]
    grad = grad_ref[...]
    even = dot_nt(grad, weight[1])
    leading = dot_nt(grad, weight[0])
    row = lax.broadcasted_iota(jnp.int32, leading.shape, 0)
    following = pltpu.roll(leading, BLOCK - 1, 0)
    following = jnp.where(row % SEG == SEG - 1, 0.0, following)
    odd = dot_nt(grad, weight[2]) + following
    for lane in range(CS // LANES):
        mixed[lane, pl.ds(0, BLOCK, stride=2), :] = even[:, lane * LANES : (lane + 1) * LANES]
        mixed[lane, pl.ds(1, BLOCK, stride=2), :] = odd[:, lane * LANES : (lane + 1) * LANES]
    starts = starts_of(scalars)
    segments = BLOCK // SEG
    for local in range(segments):
        slot = step * segments + local
        item = 2 * (slot // 2 * N_FSDP + index) + slot % 2
        owner = jnp.int32(0)
        start = jnp.int32(0)
        for other in range(1, N_FSDP):
            passed = item >= starts[other]
            owner = jnp.where(passed, other, owner)
            start = jnp.where(passed, starts[other], start)
        rank = slot - held_before(start, index)
        place = lax.bitwise_xor(owner, index)
        for lane in range(CS // LANES):
            rows = mixed[lane, pl.ds(2 * SEG * local, 2 * SEG), :]
            packed[place, rank, :, pl.ds(lane * LANES, LANES)] = rows.astype(BF16)
        firsts[pl.ds(place * CAP + rank, 1), :] = leading[SEG * local : SEG * local + 1, :]

    @pl.when(step == pl.num_programs(0) - 1)
    def _():
        packed[:, CAP] = firsts[...].reshape(N_FSDP, CAP, CS).astype(BF16)
        copies = [
            pltpu.make_async_copy(packed.at[place], outs[place], out_sem.at[place])
            for place in range(N_FSDP)
        ]
        for copy in copies:
            copy.start()
        for copy in copies:
            copy.wait()


def stem_payloads(scalars, parts, grad):
    payload = (CAP + 1, 2 * SEG, CS)
    return call(
        stem_kernel, "stem_payloads", (shape(payload, BF16),) * N_FSDP, (ROWS // BLOCK,),
        [ANY] * 10 + [row_block(BLOCK, D)], (ANY,) * N_FSDP,
        [
            pltpu.VMEM((3, CS, D), BF16),
            pltpu.VMEM((CS // LANES, 2 * BLOCK, LANES), F32),
            pltpu.VMEM((N_FSDP,) + payload, BF16),
            pltpu.VMEM((N_FSDP * CAP, CS), F32),
            pltpu.SemaphoreType.DMA,
            pltpu.SemaphoreType.DMA((N_FSDP,)),
        ],
        6 * ROWS * D * CS, 6 * CS * D + 2 * ROWS * D + 2 * N_FSDP * math.prod(payload),
    )(scalars, *parts, grad)


def owner_kernel(scalars, *refs):
    payloads, out_ref = refs[:N_FSDP], refs[N_FSDP]
    packed, firsts, sem = refs[N_FSDP + 1 :]
    step = pl.program_id(0)
    index = scalars[1]

    @pl.when(step == 0)
    def _():
        copies = [
            pltpu.make_async_copy(payloads[place], packed.at[place], sem.at[place])
            for place in range(N_FSDP)
        ]
        for copy in copies:
            copy.start()
        for copy in copies:
            copy.wait()
        firsts[...] = packed[:, CAP].astype(F32).reshape(N_FSDP * CAP, CS)

    start = jnp.int32(0)
    for owner in range(N_FSDP):
        start = start + jnp.where(owner < index, scalars[2 + owner], 0)
    count = scalars[2 + index]

    def place_of(segment):
        item = start + segment
        holder = item // 2 % N_FSDP
        slot = 2 * (item // (2 * N_FSDP)) + item % 2
        return lax.bitwise_xor(holder, index), slot - held_before(start, holder)

    per_step = OWN_SEG // 4
    last_row = lax.broadcasted_iota(jnp.int32, (2 * SEG, CS), 0) == 2 * SEG - 1

    def one(local, carry):
        segment = step * per_step + local
        rows = pl.ds(pl.multiple_of(local * 2 * SEG, 2 * SEG), 2 * SEG)

        @pl.when(segment < count)
        def _():
            place, rank = place_of(segment)
            follows = segment + 1 < count
            next_place, next_rank = place_of(jnp.where(follows, segment + 1, segment))
            first = firsts[pl.ds(next_place * CAP + next_rank, 1), :]
            extra = jnp.where(last_row & follows, jnp.broadcast_to(first, (2 * SEG, CS)), 0.0)
            out_ref[rows, :] = (packed[place, rank].astype(F32) + extra).astype(BF16)

        @pl.when(segment >= count)
        def _():
            out_ref[rows, :] = jnp.zeros((2 * SEG, CS), BF16)

        return carry

    lax.fori_loop(0, per_step, one, 0)


def owner_rows(scalars, payloads):
    payload = (CAP + 1, 2 * SEG, CS)
    rows = 2 * OWN_SEG * SEG
    return call(
        owner_kernel, "owner_rows", shape((rows, CS), BF16), (4,), [ANY] * N_FSDP,
        row_block(rows // 4, CS),
        [
            pltpu.VMEM((N_FSDP,) + payload, BF16),
            pltpu.VMEM((N_FSDP * CAP, CS), F32),
            pltpu.SemaphoreType.DMA((N_FSDP,)),
        ],
        4 * rows * CS, 2 * rows * CS + 2 * N_FSDP * math.prod(payload),
    )(scalars, *payloads)


def body(held_input, held_cotangent, proj_weight, stem_weight, seg_counts):
    site, index = lax.axis_index("site"), lax.axis_index("fsdp")
    scalars = jnp.concatenate([jnp.stack([site, index]).astype(jnp.int32), seg_counts[0]])
    inputs, cotangent = held_input[0], held_cotangent[0]

    proj_parts = gather_parts(proj_weight[None], site)
    stem_parts = gather_parts(stem_weight, site)

    normed_own, normed_other = norm_halves(scalars, inputs)
    own, *pieces = outer_pieces(
        scalars, normed_own, swap_core(normed_other), cotangent, swap_core(cotangent)
    )
    own, *pieces = site_sum(scalars, own, [swap_site(p, d + 1) for d, p in enumerate(pieces)])
    scale = 1.0 / math.sqrt(N_SITE * N_FSDP * ROWS)
    quarter = z_sum(scalars, own, [swap_z(p, d + 1) for d, p in enumerate(pieces)], scale)
    weight_grad = lay_columns(scalars, [quarter] + [swap_site(quarter, d) for d in (1, 2, 3)])

    grad = input_gradient(scalars, proj_parts, inputs, cotangent)
    payloads = stem_payloads(scalars, stem_parts, grad)
    received = [payloads[0]] + [
        lax.ppermute(payloads[d], "fsdp", [(i, i ^ d) for i in range(N_FSDP)])
        for d in range(1, N_FSDP)
    ]
    stem_grad = owner_rows(scalars, received)
    return (stem_grad[None], weight_grad)


def plain_body(held_input, held_cotangent, proj_weight, stem_weight, seg_counts):
    group_size = lax.axis_size("fsdp")
    capacity = 2 * ((OWN_SEG + 2 * group_size - 1) // (2 * group_size))
    my_index = lax.axis_index("fsdp")
    cotangent = held_cotangent[0]
    normed, inverse = normalise(held_input[0])
    normed_bf = normed.astype(jnp.bfloat16)
    proj_back = dot_nt(cotangent, lax.all_gather(proj_weight, "fsdp", axis=0, tiled=True))
    input_grad = cotangent.astype(jnp.float32) + inverse * (
        proj_back
        - jnp.mean(proj_back, axis=-1, keepdims=True)
        - normed * jnp.mean(proj_back * normed, axis=-1, keepdims=True)
    )
    input_grad = input_grad.astype(jnp.bfloat16)
    counts = seg_counts[0]
    endings = jnp.cumsum(counts)
    starts = endings - counts
    slot_ids = jnp.arange(HOLD, dtype=jnp.int32)
    item_index = 2 * (slot_ids // 2 * group_size + my_index) + slot_ids % 2
    owner_ids = jnp.sum((item_index[:, None] >= endings[None, :]).astype(jnp.int32), axis=1)
    earlier = (slot_ids[None, :] < slot_ids[:, None]) & (owner_ids[None, :] == owner_ids[:, None])
    rank_ids = jnp.sum(earlier.astype(jnp.int32), axis=1)
    target = owner_ids * capacity + rank_ids
    positions = jnp.arange(group_size * capacity, dtype=jnp.int32)
    matched = target[None, :] == positions[:, None]
    filled = jnp.any(matched, axis=1)
    source = jnp.sum(jnp.where(matched, slot_ids[None, :], 0), axis=1)
    owner_hit = jnp.arange(group_size, dtype=jnp.int32) == my_index
    my_count = jnp.sum(jnp.where(owner_hit, counts, 0))
    my_start = jnp.sum(jnp.where(owner_hit, starts, 0))
    segment = jnp.arange(OWN_SEG, dtype=jnp.int32)
    is_live = segment < my_count
    holder = (my_start + segment) // 2 % group_size
    before = (
        (segment[None, :] < segment[:, None])
        & (holder[None, :] == holder[:, None])
        & is_live[None, :]
    )
    holder_rank = jnp.sum(before.astype(jnp.int32), axis=1)
    row_index = jnp.where(is_live, holder * capacity + holder_rank, 0)
    held_segments = input_grad.reshape(HOLD, SEG, D)
    zero_bf = jnp.zeros((), jnp.bfloat16)
    send_rows = jnp.where(filled[:, None, None], jnp.take(held_segments, source, axis=0), zero_bf)
    received = lax.all_to_all(
        send_rows.reshape(group_size, capacity, SEG, D), "fsdp", split_axis=0, concat_axis=0, tiled=True
    )
    picked = jnp.take(received.reshape(group_size * capacity, SEG, D), row_index, axis=0)
    frames = jnp.where(is_live[:, None, None], picked, zero_bf).reshape(OWN_SEG * SEG, D)
    tap_terms = jnp.einsum(
        "rd,kcd->krc",
        frames,
        lax.all_gather(stem_weight, "fsdp", axis=1, tiled=True),
        preferred_element_type=jnp.float32,
    )
    shifted = jnp.concatenate(
        [tap_terms[0][1:], jnp.zeros((1, tap_terms.shape[2]), jnp.float32)], 0
    )
    stem_rows = (
        jnp.stack([tap_terms[1], tap_terms[2] + shifted], 1)
        .reshape(2 * OWN_SEG * SEG, tap_terms.shape[2])
        .astype(jnp.bfloat16)
    )
    shard_sum = lax.psum_scatter(
        lax.dot_general(
            normed_bf, cotangent, (((0,), (0,)), ((), ())), preferred_element_type=jnp.float32
        ),
        "fsdp",
        scatter_dimension=0,
        tiled=True,
    )
    shard_sum = lax.psum(shard_sum, "site")
    weight_grad = shard_sum / math.sqrt(lax.axis_size("site") * group_size * ROWS)
    return (stem_rows[None], weight_grad)


def solution(mesh):
    placed = (
        P("site", "fsdp", None),
        P("site", "fsdp", None),
        P("fsdp", None),
        P(None, "fsdp", None),
        P("site", None),
    )
    fits = (mesh.shape["site"], mesh.shape["fsdp"]) == (N_SITE, N_FSDP)
    return jax.shard_map(
        body if fits else plain_body,
        mesh=mesh,
        in_specs=placed,
        out_specs=(P("site", "fsdp", None), P("fsdp", None)),
        check_vma=False,
    )
```

```python
import math

import jax
import jax.numpy as jnp
from jax import lax
from jax.experimental import pallas as pl
from jax.experimental.pallas import tpu as pltpu
from jax.sharding import PartitionSpec as P

D = 1536
SEG = 8
HOLD = 64
OWN_SEG = 128
N_SITE = 4
N_FSDP = 8
N_Z = N_FSDP // 2
QUARTER = D // N_SITE
CAP = OWN_SEG // N_FSDP
CS = 512
ROWS = HOLD * SEG
BLOCK = 128
LANES = 128
COLUMNS = 256
PAYLOAD_ORDER = (0, 4, 5, 6, 7, 2, 3, 1)
MIB = 1024 * 1024

EPSILON = 1e-05
F32 = jnp.float32
BF16 = jnp.bfloat16


def swap_core(value):
    return lax.ppermute(value, "fsdp", [(i, i ^ 1) for i in range(N_FSDP)])


def swap_z(value, distance):
    return lax.ppermute(value, "fsdp", [(i, i ^ (2 * distance)) for i in range(N_FSDP)])


def swap_site(value, distance):
    return lax.ppermute(value, "site", [(i, i ^ distance) for i in range(N_SITE)])


def hold(value, *first):
    return pl.pallas_call(
        lambda *refs: None,
        name="hold",
        out_shape=shape(value.shape, value.dtype),
        in_specs=[HBM] + [ANY] * len(first),
        out_specs=HBM,
        input_output_aliases={0: 0},
        cost_estimate=pl.CostEstimate(flops=0, bytes_accessed=0, transcendentals=0),
    )(value, *first)


Z_ORDER = (2, 1, 3)
HALF = D // N_FSDP // 2
STEM_ROWS = CS // N_FSDP
TAPS = 3
QUARTER_TAPS = (0, 2)
WHOLE_TAP = 1
UNITS = len(QUARTER_TAPS) + N_SITE


def half_places(site, low):
    return [(0, z, ("xor", site), low, HALF) for z in Z_ORDER]


def unit_places(site):
    return [(tap, z, ("xor", site), 0, STEM_ROWS) for z in Z_ORDER for tap in QUARTER_TAPS]


def all_places():
    whole_tap = [(WHOLE_TAP, ("abs", j)) for j in range(N_SITE)]
    columns = [(tap, ("xor", 0)) for tap in QUARTER_TAPS] + whole_tap
    return [(tap, z, kind, 0, STEM_ROWS) for z in Z_ORDER for tap, kind in columns]


def shard_places(tap, count):
    return [(tap, 0, ("abs", j), 0, count) for j in range(N_SITE)]


def rows_of(value):
    return value.reshape(-1, QUARTER)


def call(kernel, name, out_shape, grid, in_specs, out_specs, scratch, vmem=16):
    return pl.pallas_call(
        kernel,
        name=name,
        out_shape=out_shape,
        grid_spec=pltpu.PrefetchScalarGridSpec(
            num_scalar_prefetch=1,
            grid=grid,
            in_specs=in_specs,
            out_specs=out_specs,
            scratch_shapes=scratch,
        ),
        compiler_params=pltpu.CompilerParams(
            dimension_semantics=("arbitrary",) * len(grid), vmem_limit_bytes=vmem * MIB
        ),
        cost_estimate=pl.CostEstimate(flops=0, bytes_accessed=0, transcendentals=0),
    )


ANY = pl.BlockSpec(memory_space=pl.ANY)
HBM = pl.BlockSpec(memory_space=pltpu.HBM)


def whole(shape):
    return pl.BlockSpec(shape, lambda i, scalars: (0,) * len(shape))


def row_block(rows, columns):
    return pl.BlockSpec((rows, columns), lambda i, scalars: (i, 0))


def shape(dims, dtype):
    return jax.ShapeDtypeStruct(dims, dtype)


def dot_nt(a, b):
    return lax.dot_general(a, b, (((1,), (1,)), ((), ())), preferred_element_type=F32)


def join(kernel, name, out_dims, values, first=(), scratch=()):
    n = len(values)

    def wrapped(*refs):
        kernel(*refs[:n], *refs[n + len(first) :])

    out = tuple(shape(dims, BF16) for dims in out_dims)
    vmem = pl.BlockSpec(memory_space=pltpu.VMEM)
    return pl.pallas_call(
        wrapped,
        name=name,
        out_shape=out,
        in_specs=[vmem] * n + [ANY] * len(first),
        out_specs=(vmem,) * len(out),
        compiler_params=pltpu.CompilerParams(vmem_limit_bytes=8 * MIB),
        cost_estimate=pl.CostEstimate(flops=0, bytes_accessed=0, transcendentals=0),
    )(*values, *first)


def cut_proj_kernel(shard, out):
    at = pl.multiple_of(lax.axis_index("site") * QUARTER, QUARTER)
    out[...] = shard[:, pl.ds(at, QUARTER)]


def cut_stem_kernel(shard, out):
    at = pl.multiple_of(lax.axis_index("site") * QUARTER, QUARTER)
    for i, tap in enumerate(QUARTER_TAPS):
        out[i] = shard[tap, :, pl.ds(at, QUARTER)]
    for i in range(N_SITE):
        out[len(QUARTER_TAPS) + i] = shard[WHOLE_TAP, :, i * QUARTER : (i + 1) * QUARTER]


def pair_kernel(a, b, out):
    out[0] = a[...]
    out[1] = b[...]


def halves_kernel(pair, near, a, b):
    for i, piece in enumerate((pair.at[1], near.at[0], near.at[1])):
        a[i] = piece[:HALF, :]
        b[i] = piece[HALF:, :]


def pack_rows(out, pieces):
    at = 0
    for piece in pieces:
        out[at : at + piece.shape[0], :] = piece
        at += piece.shape[0]


def column_pieces(shard):
    return [shard[:, i * QUARTER : (i + 1) * QUARTER] for i in range(N_SITE)]


def site_step_kernel(shard, stem, a0, b0, a1, b1, quarter, far, a, b, packed, pair):
    pair[0], pair[1] = quarter[...], far[...]
    a[0], a[1], b[0], b[1] = a0[...], a1[...], b0[...], b1[...]
    pieces = column_pieces(shard[...])
    for tap in range(stem.shape[0]):
        pieces += column_pieces(stem[tap])
    pack_rows(packed, pieces + [ref[i] for ref in (a0, b0, a1, b1) for i in range(3)])


def collect_kernel(a, b, c, out):
    out[0], out[1], out[2] = a[...], b[...], c[...]


def three_kernel(pair, near, a2, b2, quarters, units, packed):
    pieces = [ref[j, i] for ref in (a2, b2) for j in range(2) for i in range(3)]
    for i, piece in enumerate((pair[1], near[0], near[1])):
        quarters[i] = piece[: len(QUARTER_TAPS)]
        units[i] = piece
        pieces += [piece[j] for j in range(UNITS)]
    pack_rows(packed, pieces)


def normalise(inputs):
    inputs = inputs.astype(F32)
    centered = inputs - jnp.mean(inputs, axis=-1, keepdims=True)
    variance = jnp.mean(centered * centered, axis=-1, keepdims=True)
    inverse = lax.rsqrt(variance + EPSILON)
    return centered * inverse, inverse


def norm_kernel(scalars, x_ref, out_ref, turned):
    core = scalars[1] % 2
    normed, _ = normalise(x_ref[...])
    turned[...] = normed.astype(BF16).T
    shard = D // N_FSDP
    for z in range(N_Z):
        rows = pl.ds(pl.multiple_of((2 * z + core) * shard, shard), shard)
        out_ref[pl.ds(z * shard, shard), :] = turned[rows, :]


def norm_half(scalars, inputs):
    return call(
        norm_kernel, "norm_half", shape((D // 2, ROWS), BF16), (ROWS // BLOCK,),
        [row_block(BLOCK, D)], pl.BlockSpec((D // 2, BLOCK), lambda i, scalars: (0, i)),
        [pltpu.VMEM((D, BLOCK), BF16)],
    )(scalars, inputs)


OUTER_PLACES = (((0, 0), (0, 0)), ((1, 0), (0, 1)), ((0, 1), (1, 0)), ((1, 1), (1, 1)))


def outer_kernel(scalars, na_ref, nb_ref, ca_ref, cb_ref, ka_ref, sa_ref, kb_ref, sb_ref):
    step = pl.program_id(0)
    total = jnp.dot(na_ref[...], ca_ref[...], preferred_element_type=F32)
    total = total + jnp.dot(nb_ref[...], cb_ref[...], preferred_element_type=F32)
    low, high = total[: D // 4, :], total[D // 4 :, :]
    for at, (a, b) in enumerate(OUTER_PLACES):

        @pl.when(step == at)
        def _(a=a, b=b):
            for (ref, i), value in (((ka_ref, sa_ref)[a[0]], a[1]), low), (((kb_ref, sb_ref)[b[0]], b[1]), high):
                ref[i] = value.astype(ref.dtype)


def outer_pieces(scalars, normed_a, normed_b, cotangent_a, cotangent_b):
    dims = (2, D // 4, QUARTER)
    column = pl.BlockSpec((ROWS, QUARTER), lambda i, scalars: (0, lax.bitwise_xor(scalars[0], i)))
    return call(
        outer_kernel, "outer_pieces", (shape(dims, F32), shape(dims, BF16)) * 2, (N_SITE,),
        [whole((D // 2, ROWS))] * 2 + [column] * 2, (whole(dims),) * 4, [],
    )(scalars, normed_a, normed_b, cotangent_a, cotangent_b)


def half_sum_kernel(scalars, ka_ref, ra_ref, kb_ref, rb_ref, oa_ref, sa_ref, ob_ref, sb_ref):
    for kept, came, own, sent in ((ka_ref, ra_ref, oa_ref, sa_ref), (kb_ref, rb_ref, ob_ref, sb_ref)):
        own[...] = kept[0] + came[0].astype(F32)
        sent[...] = (kept[1] + came[1].astype(F32)).astype(BF16)


def half_sum(scalars, *values):
    dims, out = (2, D // 4, QUARTER), (D // 4, QUARTER)
    return call(
        half_sum_kernel, "half_sum", (shape(out, F32), shape(out, BF16)) * 2, (1,),
        [whole(dims)] * 4, (whole(out),) * 4, [],
    )(scalars, *values)


def site_sum_kernel(scalars, oa_ref, ra_ref, ob_ref, rb_ref, kept_ref, sent_ref, total):
    shard = D // N_FSDP
    z = scalars[1] // 2
    total[: D // 4, :] = oa_ref[...] + ra_ref[...].astype(F32)
    total[D // 4 :, :] = ob_ref[...] + rb_ref[...].astype(F32)
    for distance, (ref, i) in enumerate(((kept_ref, 0), (sent_ref, 0), (kept_ref, 1), (sent_ref, 1))):
        rows = pl.ds(pl.multiple_of(lax.bitwise_xor(z, distance) * shard, shard), shard)
        ref[i] = total[rows, :].astype(ref.dtype)


def site_sum(scalars, *values):
    dims, out = (D // 4, QUARTER), (2, D // N_FSDP, QUARTER)
    return call(
        site_sum_kernel, "site_sum", (shape(out, F32), shape(out, BF16)), (1,),
        [whole(dims)] * 4, (whole(out),) * 2, [pltpu.VMEM((D // 2, QUARTER), F32)],
    )(scalars, *values)


def near_sum_kernel(scalars, kept_ref, came_ref, *refs):
    own_ref, sent_ref = refs[-2:]
    own_ref[...] = kept_ref[0] + came_ref[0].astype(F32)
    sent_ref[...] = (kept_ref[1] + came_ref[1].astype(F32)).astype(BF16)


def near_sum(scalars, kept, came, first):
    dims, out = (2, D // N_FSDP, QUARTER), (D // N_FSDP, QUARTER)
    return call(
        near_sum_kernel, "near_sum", (shape(out, F32), shape(out, BF16)), (1,),
        [whole(dims)] * 2 + [ANY] * len(first), (whole(out),) * 2, [],
    )(scalars, kept, came, *first)


def far_sum_kernel(scale, scalars, own_ref, came_ref, *refs):
    refs[-1][...] = (own_ref[...] + came_ref[...].astype(F32)) * scale


def far_sum(scalars, own, came, scale, first):
    dims = (D // N_FSDP, QUARTER)
    return call(
        lambda *refs: far_sum_kernel(scale, *refs), "far_sum", shape(dims, F32), (1,),
        [whole(dims)] * 2 + [ANY] * len(first), whole(dims), [],
    )(scalars, own, came, *first)


def lay_columns_kernel(scalars, a_ref, b_ref, c_ref, d_ref, out_ref):
    for distance, ref in enumerate((a_ref, b_ref, c_ref, d_ref)):
        at = pl.multiple_of(lax.bitwise_xor(scalars[0], distance) * QUARTER, QUARTER)
        out_ref[:, pl.ds(at, QUARTER)] = ref[...]


def lay_columns(scalars, parts):
    out = (D // N_FSDP, D)
    return call(
        lay_columns_kernel, "lay_columns", shape(out, F32), (1,), [whole(parts[0].shape)] * N_SITE,
        whole(out), [],
    )(scalars, *parts)


def weight_copies(tables, scalars, refs, weight, sem):
    site, index = scalars[0], scalars[1]
    shard = weight.shape[1] // N_FSDP
    copies = []
    for (places, swapped), ref in zip(tables, refs, strict=True):
        at = 0
        for place in places:
            if isinstance(place, int):
                at += place
                continue
            tap, z, (kind, quarter), low, count = place
            start = lax.bitwise_xor(index, 2 * z + swapped) * shard + low
            rows = pl.ds(pl.multiple_of(start, math.gcd(shard, low)), count)
            columns = pl.ds(quarter * QUARTER, QUARTER)
            if kind == "all":
                columns = pl.ds(0, D)
            elif kind == "xor":
                column = lax.bitwise_xor(site, quarter) * QUARTER
                columns = pl.ds(pl.multiple_of(column, QUARTER), QUARTER)
            source = ref.at[pl.ds(at, count), :]
            copies.append(pltpu.make_async_copy(source, weight.at[tap, rows, columns], sem))
            at += count
        assert at == ref.shape[0]
    return copies


def input_grad_kernel(tables, scalars, *refs):
    n = len(tables)
    parts, (x_ref, cot_ref, out_ref, weight, normed, inverse, back, sem) = refs[:n], refs[n:]
    copies = weight_copies(tables, scalars, parts, weight, sem)
    for copy in copies:
        copy.start()

    @pl.loop(0, ROWS // BLOCK)
    def _(i):
        rows = pl.ds(pl.multiple_of(i * BLOCK, BLOCK), BLOCK)
        normed[rows, :], inverse[rows, :] = normalise(x_ref[rows, :])

    for copy in copies:
        copy.wait()

    @pl.loop(0, D // COLUMNS)
    def _(i):
        rows = pl.ds(pl.multiple_of(i * COLUMNS, COLUMNS), COLUMNS)
        back[:, rows] = dot_nt(cot_ref[...], weight[0, rows, :])

    @pl.loop(0, ROWS // BLOCK)
    def _(i):
        rows = pl.ds(pl.multiple_of(i * BLOCK, BLOCK), BLOCK)
        term, row_normed = back[rows, :], normed[rows, :]
        inner = term - jnp.mean(term, axis=-1, keepdims=True)
        inner = inner - row_normed * jnp.mean(term * row_normed, axis=-1, keepdims=True)
        out_ref[rows, :] = (cot_ref[rows, :].astype(F32) + inverse[rows, :] * inner).astype(BF16)


def split_parts(parts):
    return [(places, swapped) for _, places, swapped in parts], [value for value, _, _ in parts]


def input_gradient(scalars, parts, inputs, cotangent):
    tables, values = split_parts(parts)
    return call(
        lambda *refs: input_grad_kernel(tables, *refs), "input_gradient", shape((ROWS, D), BF16),
        (1,), [ANY] * len(values) + [whole((ROWS, D))] * 2, whole((ROWS, D)),
        [
            pltpu.VMEM((1, D, D), BF16),
            pltpu.VMEM((ROWS, D), F32),
            pltpu.VMEM((ROWS, 1), F32),
            pltpu.VMEM((ROWS, D), F32),
            pltpu.SemaphoreType.DMA,
        ],
        vmem=32,
    )(scalars, *values, inputs, cotangent)


def starts_of(scalars):
    starts = [jnp.int32(0)]
    for owner in range(N_FSDP):
        starts.append(starts[-1] + scalars[2 + owner])
    return starts


def held_before(start, holder):
    return 2 * (start // (2 * N_FSDP)) + jnp.clip(start % (2 * N_FSDP) - 2 * holder, 0, 2)


def stem_kernel(tables, scalars, *refs):
    n = len(tables)
    parts, grad_ref, outs = refs[:n], refs[n], refs[n + 1 : n + 1 + N_FSDP]
    weight, mixed, leading, packed, firsts, sem, out_sem = refs[n + 1 + N_FSDP :]
    copies = weight_copies(tables, scalars, parts, weight, sem)
    for copy in copies:
        copy.start()
    for copy in copies:
        copy.wait()
    index = scalars[1]
    for lane in range(0, CS, COLUMNS):
        span = pl.ds(lane, COLUMNS)
        even = dot_nt(grad_ref[...], weight[1, span, :])
        first = dot_nt(grad_ref[...], weight[0, span, :])
        leading[:, span] = first
        row = lax.broadcasted_iota(jnp.int32, first.shape, 0)
        following = jnp.where(row % SEG == SEG - 1, 0.0, pltpu.roll(first, ROWS - 1, 0))
        odd = dot_nt(grad_ref[...], weight[2, span, :]) + following
        for part in range(COLUMNS // LANES):
            at = lane // LANES + part
            columns = slice(part * LANES, (part + 1) * LANES)
            mixed[at, pl.ds(0, ROWS, stride=2), :] = even[:, columns]
            mixed[at, pl.ds(1, ROWS, stride=2), :] = odd[:, columns]
    starts = starts_of(scalars)

    @pl.loop(0, HOLD, unroll=4)
    def _(slot):
        item = 2 * (slot // 2 * N_FSDP + index) + slot % 2
        owner = jnp.int32(0)
        start = jnp.int32(0)
        for other in range(1, N_FSDP):
            passed = item >= starts[other]
            owner = jnp.where(passed, other, owner)
            start = jnp.where(passed, starts[other], start)
        rank = slot - held_before(start, index)
        place = lax.bitwise_xor(owner, index)
        rows = pl.ds(pl.multiple_of(slot * 2 * SEG, 2 * SEG), 2 * SEG)
        for lane in range(CS // LANES):
            packed[place, rank, :, pl.ds(lane * LANES, LANES)] = mixed[lane, rows, :].astype(BF16)
        firsts[pl.ds(place * CAP + rank, 1), :] = leading[pl.ds(slot * SEG, 1), :]

    packed[:, CAP] = firsts[...].reshape(N_FSDP, CAP, CS).astype(BF16)
    copies = [
        pltpu.make_async_copy(packed.at[place], outs[place], out_sem.at[place])
        for place in range(N_FSDP)
    ]
    for copy in copies:
        copy.start()
    for copy in copies:
        copy.wait()


def stem_payloads(scalars, parts, grad):
    tables, values = split_parts(parts)
    payload = (CAP + 1, 2 * SEG, CS)
    return call(
        lambda *refs: stem_kernel(tables, *refs), "stem_payloads",
        (shape(payload, BF16),) * N_FSDP, (1,),
        [ANY] * len(values) + [whole((ROWS, D))], (HBM,) * N_FSDP,
        [
            pltpu.VMEM((3, CS, D), BF16),
            pltpu.VMEM((CS // LANES, 2 * ROWS, LANES), F32),
            pltpu.VMEM((ROWS, CS), F32),
            pltpu.VMEM((N_FSDP,) + payload, BF16),
            pltpu.VMEM((N_FSDP * CAP, CS), F32),
            pltpu.SemaphoreType.DMA,
            pltpu.SemaphoreType.DMA((N_FSDP,)),
        ],
        vmem=32,
    )(scalars, *values, grad)


def owner_kernel(scalars, *refs):
    payloads, out_ref = refs[:N_FSDP], refs[N_FSDP]
    packed, firsts, sem = refs[N_FSDP + 1 :]
    step = pl.program_id(0)
    index = scalars[1]

    @pl.when(step == 0)
    def _():
        copies = [
            pltpu.make_async_copy(payloads[i], packed.at[place], sem.at[place])
            for i, place in enumerate(PAYLOAD_ORDER)
        ]
        for copy in copies:
            copy.start()
        for copy in copies:
            copy.wait()
        firsts[...] = packed[:, CAP].astype(F32).reshape(N_FSDP * CAP, CS)

    start = jnp.int32(0)
    for owner in range(N_FSDP):
        start = start + jnp.where(owner < index, scalars[2 + owner], 0)
    count = scalars[2 + index]

    def place_of(segment):
        item = start + segment
        holder = item // 2 % N_FSDP
        slot = 2 * (item // (2 * N_FSDP)) + item % 2
        return lax.bitwise_xor(holder, index), slot - held_before(start, holder)

    per_step = OWN_SEG // 4
    last_row = lax.broadcasted_iota(jnp.int32, (2 * SEG, CS), 0) == 2 * SEG - 1

    def one(local, carry):
        segment = step * per_step + local
        rows = pl.ds(pl.multiple_of(local * 2 * SEG, 2 * SEG), 2 * SEG)

        @pl.when(segment < count)
        def _():
            place, rank = place_of(segment)
            follows = segment + 1 < count
            next_place, next_rank = place_of(jnp.where(follows, segment + 1, segment))
            first = firsts[pl.ds(next_place * CAP + next_rank, 1), :]
            extra = jnp.where(last_row & follows, jnp.broadcast_to(first, (2 * SEG, CS)), 0.0)
            out_ref[rows, :] = (packed[place, rank].astype(F32) + extra).astype(BF16)

        @pl.when(segment >= count)
        def _():
            out_ref[rows, :] = jnp.zeros((2 * SEG, CS), BF16)

        return carry

    lax.fori_loop(0, per_step, one, 0)


def owner_rows(scalars, payloads):
    payload = (CAP + 1, 2 * SEG, CS)
    rows = 2 * OWN_SEG * SEG
    return call(
        owner_kernel, "owner_rows", shape((rows, CS), BF16), (4,), [ANY] * N_FSDP,
        row_block(rows // 4, CS),
        [
            pltpu.VMEM((N_FSDP,) + payload, BF16),
            pltpu.VMEM((N_FSDP * CAP, CS), F32),
            pltpu.SemaphoreType.DMA((N_FSDP,)),
        ],
    )(scalars, *payloads)


def body(held_input, held_cotangent, proj_weight, stem_weight, seg_counts):
    site, index = lax.axis_index("site"), lax.axis_index("fsdp")
    scalars = jnp.concatenate([jnp.stack([site, index]).astype(jnp.int32), seg_counts[0]])
    inputs, cotangent = held_input[0], held_cotangent[0]

    piece = (D // N_FSDP, QUARTER)
    half = (3, HALF, QUARTER)
    units = (UNITS, STEM_ROWS, QUARTER)
    quarters = (len(QUARTER_TAPS), STEM_ROWS, QUARTER)

    normed_own = norm_half(scalars, inputs)
    normed_theirs = norm_half(scalars, swap_core(inputs))
    kept_a, sent_a, kept_b, sent_b = outer_pieces(
        scalars, normed_own, normed_theirs, cotangent, swap_core(cotangent)
    )
    (proj_quarter,) = join(cut_proj_kernel, "cut_proj", [piece], [proj_weight], [normed_own])
    far = swap_z(proj_quarter, 2)
    (pair,) = join(pair_kernel, "pair", [(2, *piece)], [proj_quarter, far], [sent_a])

    near = swap_z(pair, 1)
    came_a, came_b = swap_site(sent_a, 1), swap_site(sent_b, 2)
    a0, b0 = join(halves_kernel, "halves", [half, half], [pair, near])

    a1, b1 = swap_site(a0, 1), swap_site(b0, 2)
    own_a, sent_a, own_b, sent_b = half_sum(scalars, kept_a, came_a, kept_b, came_b)
    (stem_quarter,) = join(cut_stem_kernel, "cut_stem", [units], [stem_weight], [near])
    far = swap_z(stem_quarter, 2)
    kept, sent = site_sum(scalars, own_a, swap_site(sent_a, 2), own_b, swap_site(sent_b, 1))
    a, b, packed, stem_pair = join(
        site_step_kernel, "site_step", [(2, *half)] * 2 + [(D // 2 + TAPS * N_SITE * STEM_ROWS + 12 * HALF, QUARTER), (2, *units)],
        [proj_weight, stem_weight, a0, b0, a1, b1, stem_quarter, far], [kept],
    )

    a2, b2 = swap_site(a, 2), swap_site(b, 1)
    near = swap_z(stem_pair, 1)
    packed = swap_core(packed)
    n = 3 * UNITS * STEM_ROWS
    others, all_others, late = join(
        three_kernel, "three", [(3, *quarters), (3, *units), (12 * HALF + n, QUARTER)],
        [stem_pair, near, a2, b2], [packed],
    )

    over = [swap_site(others, distance) for distance in (1, 2, 3)]
    late = swap_core(late)
    whole_proj = [(0, 0, ("all", 0), 0, D // N_FSDP)]
    first = [half_places(0, 0), half_places(0, HALF), half_places(1, 0), half_places(2, HALF)]
    last = [half_places(2, 0) + half_places(3, 0), half_places(1, HALF) + half_places(3, HALF)]
    proj_parts = [
        (proj_weight, whole_proj, 0),
        (rows_of(a0), first[0], 0), (rows_of(b0), first[1], 0),
        (rows_of(a1), first[2], 0), (rows_of(b1), first[3], 0),
        (rows_of(a2), last[0], 0), (rows_of(b2), last[1], 0),
        (packed, shard_places(0, D // N_FSDP) + [TAPS * N_SITE * STEM_ROWS] + sum(first, []), 1),
        (late, sum(last, []) + [n], 1),
    ]
    grad = input_gradient(scalars, proj_parts, inputs, cotangent)
    own, sent = near_sum(scalars, kept, swap_z(hold(sent, others), 1), [grad])
    (over,) = join(collect_kernel, "collect", [(3, 3, *quarters)], over, [grad, sent])
    over = rows_of(over)
    last = sum((unit_places(d) for d in (1, 2, 3)), [])
    stem_parts = [
        (stem_weight.reshape(-1, D), [(tap, 0, ("all", 0), 0, STEM_ROWS) for tap in range(TAPS)], 0),
        (rows_of(all_others), all_places(), 0),
        (over, last, 0),
        (
            packed,
            [D // 2] + sum((shard_places(tap, STEM_ROWS) for tap in range(TAPS)), []) + [12 * HALF],
            1,
        ),
        (late, [12 * HALF] + all_places(), 1),
        (swap_core(over), last, 1),
    ]

    payloads = stem_payloads(scalars, stem_parts, grad)
    received = {0: payloads[0]}
    for d in PAYLOAD_ORDER[1:]:
        received[d] = lax.ppermute(payloads[d], "fsdp", [(i, i ^ d) for i in range(N_FSDP)])
    scale = 1.0 / math.sqrt(N_SITE * N_FSDP * ROWS)
    first = [received[d] for d in (4, 5, 2, 3)]
    terms = far_sum(scalars, own, swap_z(sent, 2), scale, first)
    weight_grad = lay_columns(scalars, [terms] + [swap_site(terms, d) for d in (1, 2, 3)])
    stem_grad = owner_rows(scalars, [received[d] for d in PAYLOAD_ORDER])
    return (stem_grad[None], weight_grad)


def plain_body(held_input, held_cotangent, proj_weight, stem_weight, seg_counts):
    group_size = lax.axis_size("fsdp")
    capacity = 2 * ((OWN_SEG + 2 * group_size - 1) // (2 * group_size))
    my_index = lax.axis_index("fsdp")
    cotangent = held_cotangent[0]
    normed, inverse = normalise(held_input[0])
    normed_bf = normed.astype(jnp.bfloat16)
    proj_back = dot_nt(cotangent, lax.all_gather(proj_weight, "fsdp", axis=0, tiled=True))
    input_grad = cotangent.astype(jnp.float32) + inverse * (
        proj_back
        - jnp.mean(proj_back, axis=-1, keepdims=True)
        - normed * jnp.mean(proj_back * normed, axis=-1, keepdims=True)
    )
    input_grad = input_grad.astype(jnp.bfloat16)
    counts = seg_counts[0]
    endings = jnp.cumsum(counts)
    starts = endings - counts
    slot_ids = jnp.arange(HOLD, dtype=jnp.int32)
    item_index = 2 * (slot_ids // 2 * group_size + my_index) + slot_ids % 2
    owner_ids = jnp.sum((item_index[:, None] >= endings[None, :]).astype(jnp.int32), axis=1)
    earlier = (slot_ids[None, :] < slot_ids[:, None]) & (owner_ids[None, :] == owner_ids[:, None])
    rank_ids = jnp.sum(earlier.astype(jnp.int32), axis=1)
    target = owner_ids * capacity + rank_ids
    positions = jnp.arange(group_size * capacity, dtype=jnp.int32)
    matched = target[None, :] == positions[:, None]
    filled = jnp.any(matched, axis=1)
    source = jnp.sum(jnp.where(matched, slot_ids[None, :], 0), axis=1)
    owner_hit = jnp.arange(group_size, dtype=jnp.int32) == my_index
    my_count = jnp.sum(jnp.where(owner_hit, counts, 0))
    my_start = jnp.sum(jnp.where(owner_hit, starts, 0))
    segment = jnp.arange(OWN_SEG, dtype=jnp.int32)
    is_live = segment < my_count
    holder = (my_start + segment) // 2 % group_size
    before = (
        (segment[None, :] < segment[:, None])
        & (holder[None, :] == holder[:, None])
        & is_live[None, :]
    )
    holder_rank = jnp.sum(before.astype(jnp.int32), axis=1)
    row_index = jnp.where(is_live, holder * capacity + holder_rank, 0)
    held_segments = input_grad.reshape(HOLD, SEG, D)
    zero_bf = jnp.zeros((), jnp.bfloat16)
    send_rows = jnp.where(filled[:, None, None], jnp.take(held_segments, source, axis=0), zero_bf)
    received = lax.all_to_all(
        send_rows.reshape(group_size, capacity, SEG, D), "fsdp", split_axis=0, concat_axis=0, tiled=True
    )
    picked = jnp.take(received.reshape(group_size * capacity, SEG, D), row_index, axis=0)
    frames = jnp.where(is_live[:, None, None], picked, zero_bf).reshape(OWN_SEG * SEG, D)
    tap_terms = jnp.einsum(
        "rd,kcd->krc",
        frames,
        lax.all_gather(stem_weight, "fsdp", axis=1, tiled=True),
        preferred_element_type=jnp.float32,
    )
    shifted = jnp.concatenate(
        [tap_terms[0][1:], jnp.zeros((1, tap_terms.shape[2]), jnp.float32)], 0
    )
    stem_rows = (
        jnp.stack([tap_terms[1], tap_terms[2] + shifted], 1)
        .reshape(2 * OWN_SEG * SEG, tap_terms.shape[2])
        .astype(jnp.bfloat16)
    )
    shard_sum = lax.psum_scatter(
        lax.dot_general(
            normed_bf, cotangent, (((0,), (0,)), ((), ())), preferred_element_type=jnp.float32
        ),
        "fsdp",
        scatter_dimension=0,
        tiled=True,
    )
    shard_sum = lax.psum(shard_sum, "site")
    weight_grad = shard_sum / math.sqrt(lax.axis_size("site") * group_size * ROWS)
    return (stem_rows[None], weight_grad)


def solution(mesh):
    placed = (
        P("site", "fsdp", None),
        P("site", "fsdp", None),
        P("fsdp", None),
        P(None, "fsdp", None),
        P("site", None),
    )
    fits = (mesh.shape["site"], mesh.shape["fsdp"]) == (N_SITE, N_FSDP)
    return jax.shard_map(
        body if fits else plain_body,
        mesh=mesh,
        in_specs=placed,
        out_specs=(P("site", "fsdp", None), P("fsdp", None)),
        check_vma=False,
    )
```

```python
import math

import jax
import jax.numpy as jnp
from jax import lax
from jax.experimental import pallas as pl
from jax.experimental.pallas import tpu as pltpu
from jax.sharding import PartitionSpec as P

D = 1536
SEG = 8
HOLD = 64
OWN_SEG = 128
N_SITE = 4
N_FSDP = 8
N_Z = N_FSDP // 2
QUARTER = D // N_SITE
CAP = OWN_SEG // N_FSDP
CS = 512
ROWS = HOLD * SEG
BLOCK = 128
LANES = 128
COLUMNS = 768
PAYLOAD_ORDER = (0, 4, 5, 2, 3, 6, 7, 1)
MIB = 1024 * 1024

EPSILON = 1e-05
F32 = jnp.float32
BF16 = jnp.bfloat16


def swap_core(value):
    return lax.ppermute(value, "fsdp", [(i, i ^ 1) for i in range(N_FSDP)])


def swap_z(value, distance):
    return lax.ppermute(value, "fsdp", [(i, i ^ (2 * distance)) for i in range(N_FSDP)])


def swap_site(value, distance):
    return lax.ppermute(value, "site", [(i, i ^ distance) for i in range(N_SITE)])


def hold(value, *first):
    return pl.pallas_call(
        lambda *refs: None,
        name="hold",
        out_shape=shape(value.shape, value.dtype),
        in_specs=[HBM] + [ANY] * len(first),
        out_specs=HBM,
        input_output_aliases={0: 0},
        cost_estimate=pl.CostEstimate(flops=0, bytes_accessed=0, transcendentals=0),
    )(value, *first)


Z_ORDER = (2, 1, 3)
HALF = D // N_FSDP // 2
STEM_ROWS = CS // N_FSDP
TAPS = 3
QUARTER_TAPS = (1,)
WHOLE_TAPS = (0, 2)
UNITS = len(QUARTER_TAPS) + len(WHOLE_TAPS) * N_SITE


def half_places(site, low):
    return [(0, z, ("xor", site), low, HALF) for z in Z_ORDER]


def unit_places(site):
    return [(tap, z, ("xor", site), 0, STEM_ROWS) for z in Z_ORDER for tap in QUARTER_TAPS]


def all_places():
    whole_tap = [(tap, ("abs", j)) for tap in WHOLE_TAPS for j in range(N_SITE)]
    columns = [(tap, ("xor", 0)) for tap in QUARTER_TAPS] + whole_tap
    return [(tap, z, kind, 0, STEM_ROWS) for z in Z_ORDER for tap, kind in columns]


def shard_places(tap, count):
    return [(tap, 0, ("abs", j), 0, count) for j in range(N_SITE)]


def rows_of(value):
    return value.reshape(-1, QUARTER)


def call(kernel, name, out_shape, grid, in_specs, out_specs, scratch, vmem=16):
    return pl.pallas_call(
        kernel,
        name=name,
        out_shape=out_shape,
        grid_spec=pltpu.PrefetchScalarGridSpec(
            num_scalar_prefetch=1,
            grid=grid,
            in_specs=in_specs,
            out_specs=out_specs,
            scratch_shapes=scratch,
        ),
        compiler_params=pltpu.CompilerParams(
            dimension_semantics=("arbitrary",) * len(grid), vmem_limit_bytes=vmem * MIB
        ),
        cost_estimate=pl.CostEstimate(flops=0, bytes_accessed=0, transcendentals=0),
    )


ANY = pl.BlockSpec(memory_space=pl.ANY)
HBM = pl.BlockSpec(memory_space=pltpu.HBM)


def whole(shape):
    return pl.BlockSpec(shape, lambda i, scalars: (0,) * len(shape))


def row_block(rows, columns):
    return pl.BlockSpec((rows, columns), lambda i, scalars: (i, 0))


def shape(dims, dtype):
    return jax.ShapeDtypeStruct(dims, dtype)


def dot_nt(a, b):
    return lax.dot_general(a, b, (((1,), (1,)), ((), ())), preferred_element_type=F32)


def join(kernel, name, out_dims, values, first=(), wide_dims=()):
    n = len(values)

    def wrapped(*refs):
        kernel(*refs[:n], *refs[n + len(first) :])

    out = tuple(shape(dims, BF16) for dims in out_dims) + tuple(shape(dims, F32) for dims in wide_dims)
    vmem = pl.BlockSpec(memory_space=pltpu.VMEM)
    return pl.pallas_call(
        wrapped,
        name=name,
        out_shape=out,
        in_specs=[vmem] * n + [ANY] * len(first),
        out_specs=(vmem,) * len(out),
        compiler_params=pltpu.CompilerParams(vmem_limit_bytes=16 * MIB),
        cost_estimate=pl.CostEstimate(flops=0, bytes_accessed=0, transcendentals=0),
    )(*values, *first)


def cut_proj_kernel(shard, out):
    at = pl.multiple_of(lax.axis_index("site") * QUARTER, QUARTER)
    out[...] = shard[:, pl.ds(at, QUARTER)]


def pair_kernel(a, b, out):
    out[0] = a[...]
    out[1] = b[...]


def halves_kernel(pair, near, sent_a, sent_b, stem, a, b, out_a, out_b, units):
    out_a[...], out_b[...] = sent_a[...], sent_b[...]
    for i, piece in enumerate((pair.at[1], near.at[0], near.at[1])):
        a[i] = piece[:HALF, :]
        b[i] = piece[HALF:, :]
    at = pl.multiple_of(lax.axis_index("site") * QUARTER, QUARTER)
    for i, tap in enumerate(QUARTER_TAPS):
        units[i] = stem[tap, :, pl.ds(at, QUARTER)]
    for i, tap in enumerate(WHOLE_TAPS):
        for j in range(N_SITE):
            columns = slice(j * QUARTER, (j + 1) * QUARTER)
            units[len(QUARTER_TAPS) + N_SITE * i + j] = stem[tap, :, columns]


def pack_rows(out, pieces):
    at = 0
    for piece in pieces:
        out[at : at + piece.shape[0], :] = piece
        at += piece.shape[0]


def site_step_kernel(
    a0, b0, a1, b1, units, far, kept_a, came_a, kept_b, came_b, a, b, pair, sent_a, sent_b, own_a, own_b
):
    pair[0], pair[1] = units[...], far[...]
    a[0], a[1], b[0], b[1] = a0[...], a1[...], b0[...], b1[...]
    for kept, came, own, sent in ((kept_a, came_a, own_a, sent_a), (kept_b, came_b, own_b, sent_b)):
        own[...] = kept[0] + came[0].astype(F32)
        sent[...] = (kept[1] + came[1].astype(F32)).astype(BF16)


def collect_kernel(a, b, c, out):
    out[0], out[1], out[2] = a[...], b[...], c[...]


def three_kernel(pair, near, a, b, a2, b2, quarters, units, packed):
    pieces = [ref[j, i] for ref in (a, b, a2, b2) for j in range(2) for i in range(3)]
    for i, piece in enumerate((pair[1], near[0], near[1])):
        quarters[i] = piece[: len(QUARTER_TAPS)]
        units[i] = piece
        pieces += [piece[j] for j in range(UNITS)]
    pack_rows(packed, pieces)


def normalise(inputs):
    inputs = inputs.astype(F32)
    centered = inputs - jnp.mean(inputs, axis=-1, keepdims=True)
    variance = jnp.mean(centered * centered, axis=-1, keepdims=True)
    inverse = lax.rsqrt(variance + EPSILON)
    return centered * inverse, inverse


def norm_kernel(scalars, x_ref, *refs):
    out_ref, turned = refs[-2:]
    core = scalars[1] % 2
    normed, _ = normalise(x_ref[...])
    turned[...] = normed.astype(BF16).T
    shard = D // N_FSDP
    for z in range(N_Z):
        rows = pl.ds(pl.multiple_of((2 * z + core) * shard, shard), shard)
        out_ref[pl.ds(z * shard, shard), :] = turned[rows, :]


def norm_half(scalars, inputs, first=()):
    return call(
        norm_kernel, "norm_half", shape((D // 2, ROWS), BF16), (ROWS // BLOCK,),
        [row_block(BLOCK, D)] + [ANY] * len(first),
        pl.BlockSpec((D // 2, BLOCK), lambda i, scalars: (0, i)), [pltpu.VMEM((D, BLOCK), BF16)],
    )(scalars, inputs, *first)


OUTER_PLACES = (((0, 0), (0, 0)), ((1, 0), (0, 1)), ((0, 1), (1, 0)), ((1, 1), (1, 1)))


def outer_kernel(scalars, na_ref, nb_ref, ca_ref, cb_ref, _, ka_ref, sa_ref, kb_ref, sb_ref):
    step = pl.program_id(0)
    total = jnp.dot(na_ref[...], ca_ref[...], preferred_element_type=F32)
    total = total + jnp.dot(nb_ref[...], cb_ref[...], preferred_element_type=F32)
    low, high = total[: D // 4, :], total[D // 4 :, :]
    for at, (a, b) in enumerate(OUTER_PLACES):

        @pl.when(step == at)
        def _(a=a, b=b):
            for (ref, i), value in (((ka_ref, sa_ref)[a[0]], a[1]), low), (((kb_ref, sb_ref)[b[0]], b[1]), high):
                ref[i] = value.astype(ref.dtype)


def outer_pieces(scalars, normed_a, normed_b, cotangent_a, cotangent_b, first):
    dims = (2, D // 4, QUARTER)
    column = pl.BlockSpec((ROWS, QUARTER), lambda i, scalars: (0, lax.bitwise_xor(scalars[0], i)))
    return call(
        outer_kernel, "outer_pieces", (shape(dims, F32), shape(dims, BF16)) * 2, (N_SITE,),
        [whole((D // 2, ROWS))] * 2 + [column] * 2 + [ANY], (whole(dims),) * 4, [],
    )(scalars, normed_a, normed_b, cotangent_a, cotangent_b, first)


def site_sum_kernel(scalars, oa_ref, ra_ref, ob_ref, rb_ref, kept_ref, sent_ref, total):
    shard = D // N_FSDP
    z = scalars[1] // 2
    total[: D // 4, :] = oa_ref[...] + ra_ref[...].astype(F32)
    total[D // 4 :, :] = ob_ref[...] + rb_ref[...].astype(F32)
    for distance, (ref, i) in enumerate(((kept_ref, 0), (sent_ref, 0), (kept_ref, 1), (sent_ref, 1))):
        rows = pl.ds(pl.multiple_of(lax.bitwise_xor(z, distance) * shard, shard), shard)
        ref[i] = total[rows, :].astype(ref.dtype)


def site_sum(scalars, *values):
    dims, out = (D // 4, QUARTER), (2, D // N_FSDP, QUARTER)
    return call(
        site_sum_kernel, "site_sum", (shape(out, F32), shape(out, BF16)), (1,),
        [whole(dims)] * 4, (whole(out),) * 2, [pltpu.VMEM((D // 2, QUARTER), F32)],
    )(scalars, *values)


def near_sum_kernel(scalars, kept_ref, came_ref, *refs):
    own_ref, sent_ref = refs[-2:]
    own_ref[...] = kept_ref[0] + came_ref[0].astype(F32)
    sent_ref[...] = (kept_ref[1] + came_ref[1].astype(F32)).astype(BF16)


def near_sum(scalars, kept, came, first):
    dims, out = (2, D // N_FSDP, QUARTER), (D // N_FSDP, QUARTER)
    return call(
        near_sum_kernel, "near_sum", (shape(out, F32), shape(out, BF16)), (1,),
        [whole(dims)] * 2 + [ANY] * len(first), (whole(out),) * 2, [],
    )(scalars, kept, came, *first)


def far_sum_kernel(scale, scalars, own_ref, came_ref, *refs):
    refs[-1][...] = (own_ref[...] + came_ref[...].astype(F32)) * scale


def far_sum(scalars, own, came, scale, first):
    dims = (D // N_FSDP, QUARTER)
    return call(
        lambda *refs: far_sum_kernel(scale, *refs), "far_sum", shape(dims, F32), (1,),
        [whole(dims)] * 2 + [ANY] * len(first), whole(dims), [],
    )(scalars, own, came, *first)


def lay_columns_kernel(scalars, a_ref, b_ref, c_ref, d_ref, out_ref):
    for distance, ref in enumerate((a_ref, b_ref, c_ref, d_ref)):
        at = pl.multiple_of(lax.bitwise_xor(scalars[0], distance) * QUARTER, QUARTER)
        out_ref[:, pl.ds(at, QUARTER)] = ref[...]


def lay_columns(scalars, parts):
    out = (D // N_FSDP, D)
    return call(
        lay_columns_kernel, "lay_columns", shape(out, F32), (1,), [whole(parts[0].shape)] * N_SITE,
        whole(out), [],
    )(scalars, *parts)


def weight_copies(tables, scalars, refs, weight, sem):
    site, index = scalars[0], scalars[1]
    shard = weight.shape[1] // N_FSDP
    copies = []
    for (places, swapped), ref in zip(tables, refs, strict=True):
        at = 0
        for place in places:
            if isinstance(place, int):
                at += place
                continue
            tap, z, (kind, quarter), low, count = place
            start = lax.bitwise_xor(index, 2 * z + swapped) * shard + low
            rows = pl.ds(pl.multiple_of(start, math.gcd(shard, low)), count)
            columns = pl.ds(quarter * QUARTER, QUARTER)
            if kind == "all":
                columns = pl.ds(0, D)
            elif kind == "xor":
                column = lax.bitwise_xor(site, quarter) * QUARTER
                columns = pl.ds(pl.multiple_of(column, QUARTER), QUARTER)
            source = ref.at[pl.ds(at, count), :]
            copies.append(pltpu.make_async_copy(source, weight.at[tap, rows, columns], sem))
            at += count
        assert at == ref.shape[0]
    return copies


def fetch(source, target, sem):
    copy = pltpu.make_async_copy(source, target, sem)
    copy.start()
    return copy


def input_grad_kernel(tables, scalars, *refs):
    n = len(tables)
    parts, (x_hbm, cot_hbm, out_ref) = refs[:n], refs[n : n + 3]
    x_ref, cot_ref, weight, normed, inverse, back, sems, sem = refs[n + 3 :]
    x_copy = fetch(x_hbm, x_ref, sems.at[0])
    cot_copy = fetch(cot_hbm, cot_ref, sems.at[1])
    copies = weight_copies(tables, scalars, parts, weight, sem)
    for copy in copies:
        copy.start()
    x_copy.wait()

    @pl.loop(0, ROWS // BLOCK)
    def _(i):
        rows = pl.ds(pl.multiple_of(i * BLOCK, BLOCK), BLOCK)
        normed[rows, :], inverse[rows, :] = normalise(x_ref[rows, :])

    cot_copy.wait()
    for copy in copies:
        copy.wait()

    @pl.loop(0, D // COLUMNS)
    def _(i):
        rows = pl.ds(pl.multiple_of(i * COLUMNS, COLUMNS), COLUMNS)
        back[:, rows] = dot_nt(cot_ref[...], weight[0, rows, :])

    @pl.loop(0, ROWS // BLOCK)
    def _(i):
        rows = pl.ds(pl.multiple_of(i * BLOCK, BLOCK), BLOCK)
        term, row_normed = back[rows, :], normed[rows, :]
        inner = term - jnp.mean(term, axis=-1, keepdims=True)
        inner = inner - row_normed * jnp.mean(term * row_normed, axis=-1, keepdims=True)
        out_ref[rows, :] = (cot_ref[rows, :].astype(F32) + inverse[rows, :] * inner).astype(BF16)


def split_parts(parts):
    return [(places, swapped) for _, places, swapped in parts], [value for value, _, _ in parts]


def input_gradient(scalars, parts, inputs, cotangent):
    tables, values = split_parts(parts)
    return call(
        lambda *refs: input_grad_kernel(tables, *refs), "input_gradient", shape((ROWS, D), BF16),
        (1,), [HBM] * (len(values) + 2), whole((ROWS, D)),
        [
            pltpu.VMEM((ROWS, D), BF16),
            pltpu.VMEM((ROWS, D), BF16),
            pltpu.VMEM((1, D, D), BF16),
            pltpu.VMEM((ROWS, D), F32),
            pltpu.VMEM((ROWS, 1), F32),
            pltpu.VMEM((ROWS, D), F32),
            pltpu.SemaphoreType.DMA((2,)),
            pltpu.SemaphoreType.DMA,
        ],
        vmem=22,
    )(scalars, *values, inputs, cotangent)


def held_before(start, holder):
    return 2 * (start // (2 * N_FSDP)) + jnp.clip(start % (2 * N_FSDP) - 2 * holder, 0, 2)


SLOTS_AT = 2
SEGMENTS_AT = SLOTS_AT + HOLD
COUNT_AT = SEGMENTS_AT + OWN_SEG


def plan_kernel(scalars, plan):
    site, index = scalars[0], scalars[1]
    plan[0], plan[1] = site, index
    starts = [jnp.int32(0)]
    for owner in range(N_FSDP):
        starts.append(starts[-1] + scalars[2 + owner])

    @pl.loop(0, HOLD)
    def _(slot):
        item = 2 * (slot // 2 * N_FSDP + index) + slot % 2
        owner = jnp.int32(0)
        start = jnp.int32(0)
        for other in range(1, N_FSDP):
            passed = item >= starts[other]
            owner = jnp.where(passed, other, owner)
            start = jnp.where(passed, starts[other], start)
        plan[SLOTS_AT + slot] = lax.bitwise_xor(owner, index) * CAP + slot - held_before(start, index)

    start = jnp.int32(0)
    for owner in range(N_FSDP):
        start = start + jnp.where(owner < index, scalars[2 + owner], 0)
    count = scalars[2 + index]
    plan[COUNT_AT] = count

    @pl.loop(0, OWN_SEG)
    def _(segment):
        item = start + jnp.minimum(segment, count - 1)
        holder = item // 2 % N_FSDP
        rank = 2 * (item // (2 * N_FSDP)) + item % 2 - held_before(start, holder)
        plan[SEGMENTS_AT + segment] = lax.bitwise_xor(holder, index) * CAP + rank


def plan_of(scalars):
    return call(
        plan_kernel, "plan", shape((COUNT_AT + 1,), jnp.int32), (1,), [],
        pl.BlockSpec(memory_space=pltpu.SMEM), [],
    )(scalars)


def stem_kernel(tables, scalars, *refs):
    n = len(tables)
    parts, grad_ref, outs = refs[:n], refs[n], refs[n + 1 : n + 1 + N_FSDP]
    weight, mixed, leading, packed, firsts, sem, out_sem = refs[n + 1 + N_FSDP :]
    copies = weight_copies(tables, scalars, parts, weight, sem)
    for copy in copies:
        copy.start()
    for copy in copies:
        copy.wait()
    index = scalars[1]
    for lane in range(0, CS, CS // 2):
        span = pl.ds(lane, CS // 2)
        even = dot_nt(grad_ref[...], weight[1, span, :])
        first = dot_nt(grad_ref[...], weight[0, span, :])
        leading[:, span] = first
        row = lax.broadcasted_iota(jnp.int32, first.shape, 0)
        following = jnp.where(row % SEG == SEG - 1, 0.0, pltpu.roll(first, ROWS - 1, 0))
        odd = dot_nt(grad_ref[...], weight[2, span, :]) + following
        for part in range(CS // 2 // LANES):
            at = lane // LANES + part
            columns = slice(part * LANES, (part + 1) * LANES)
            mixed[at, pl.ds(0, ROWS, stride=2), :] = even[:, columns]
            mixed[at, pl.ds(1, ROWS, stride=2), :] = odd[:, columns]

    @pl.loop(0, HOLD, unroll=8)
    def _(slot):
        block = scalars[SLOTS_AT + slot]
        place, rank = block // CAP, block % CAP
        rows = pl.ds(pl.multiple_of(slot * 2 * SEG, 2 * SEG), 2 * SEG)
        for lane in range(CS // LANES):
            packed[place, rank, :, pl.ds(lane * LANES, LANES)] = mixed[lane, rows, :].astype(BF16)
        firsts[pl.ds(block, 1), :] = leading[pl.ds(slot * SEG, 1), :]

    packed[:, CAP] = firsts[...].reshape(N_FSDP, CAP, CS).astype(BF16)
    copies = [
        pltpu.make_async_copy(packed.at[place], outs[place], out_sem.at[place])
        for place in range(N_FSDP)
    ]
    for copy in copies:
        copy.start()
    for copy in copies:
        copy.wait()


def stem_payloads(scalars, parts, grad):
    tables, values = split_parts(parts)
    payload = (CAP + 1, 2 * SEG, CS)
    return call(
        lambda *refs: stem_kernel(tables, *refs), "stem_payloads",
        (shape(payload, BF16),) * N_FSDP, (1,),
        [ANY] * len(values) + [whole((ROWS, D))], (HBM,) * N_FSDP,
        [
            pltpu.VMEM((3, CS, D), BF16),
            pltpu.VMEM((CS // LANES, 2 * ROWS, LANES), F32),
            pltpu.VMEM((ROWS, CS), F32),
            pltpu.VMEM((N_FSDP,) + payload, BF16),
            pltpu.VMEM((N_FSDP * CAP, CS), F32),
            pltpu.SemaphoreType.DMA,
            pltpu.SemaphoreType.DMA((N_FSDP,)),
        ],
        vmem=18,
    )(scalars, *values, grad)


def owner_kernel(scalars, *refs):
    payloads, (out_ref, packed, firsts, sem) = refs[:N_FSDP], refs[N_FSDP:]
    step = pl.program_id(0)

    @pl.when(step == 0)
    def _():
        copies = [
            pltpu.make_async_copy(payloads[i], packed.at[place], sem.at[place])
            for i, place in enumerate(PAYLOAD_ORDER)
        ]
        for copy in copies:
            copy.start()
        for copy in copies:
            copy.wait()
        firsts[...] = packed[:, CAP].astype(F32).reshape(N_FSDP * CAP, CS)

    count = scalars[COUNT_AT]
    per_step = OWN_SEG // 4
    last_row = lax.broadcasted_iota(jnp.int32, (2 * SEG, CS), 0) == 2 * SEG - 1

    @pl.loop(0, per_step, unroll=4)
    def _(local):
        segment = step * per_step + local
        block = scalars[SEGMENTS_AT + segment]
        follower = scalars[SEGMENTS_AT + jnp.minimum(segment + 1, OWN_SEG - 1)]
        first = jnp.broadcast_to(firsts[pl.ds(follower, 1), :], (2 * SEG, CS))
        first = jnp.where(last_row & (segment + 1 < count), first, 0.0)
        rows = packed[block // CAP, block % CAP].astype(F32) + first
        to = pl.ds(pl.multiple_of(local * 2 * SEG, 2 * SEG), 2 * SEG)
        out_ref[to, :] = jnp.where(segment < count, rows, 0.0).astype(BF16)


def owner_rows(scalars, payloads):
    payload = (CAP + 1, 2 * SEG, CS)
    rows = 2 * OWN_SEG * SEG
    return call(
        owner_kernel, "owner_rows", shape((rows, CS), BF16), (4,), [ANY] * N_FSDP,
        row_block(rows // 4, CS),
        [
            pltpu.VMEM((N_FSDP,) + payload, BF16),
            pltpu.VMEM((N_FSDP * CAP, CS), F32),
            pltpu.SemaphoreType.DMA((N_FSDP,)),
        ],
    )(scalars, *payloads)


def body(held_input, held_cotangent, proj_weight, stem_weight, seg_counts):
    site, index = lax.axis_index("site"), lax.axis_index("fsdp")
    scalars = jnp.concatenate([jnp.stack([site, index]).astype(jnp.int32), seg_counts[0]])
    inputs, cotangent = held_input[0], held_cotangent[0]

    plan = plan_of(scalars)
    piece = (D // N_FSDP, QUARTER)
    half = (3, HALF, QUARTER)
    units = (UNITS, STEM_ROWS, QUARTER)
    quarters = (len(QUARTER_TAPS), STEM_ROWS, QUARTER)

    (proj_quarter,) = join(cut_proj_kernel, "cut_proj", [piece], [proj_weight])
    far = swap_z(proj_quarter, 2)
    normed_own = norm_half(scalars, inputs, [proj_quarter])
    normed_theirs = norm_half(scalars, swap_core(inputs), [normed_own])
    cotangent_theirs = swap_core(cotangent)
    proj_swapped, stem_swapped = swap_core(proj_weight), swap_core(stem_weight)
    (pair,) = join(
        pair_kernel, "pair", [(2, *piece)], [proj_quarter, far],
        [normed_theirs, cotangent_theirs, proj_swapped, stem_swapped],
    )

    near = swap_z(pair, 1)
    kept_a, sent_a, kept_b, sent_b = outer_pieces(
        scalars, normed_own, normed_theirs, cotangent, cotangent_theirs, pair
    )
    terms = (D // 4, QUARTER)
    a0, b0, sent_a, sent_b, stem_units = join(
        halves_kernel, "halves", [half, half, (2, *terms), (2, *terms), units],
        [pair, near, sent_a, sent_b, stem_weight],
    )

    a, b, stem_pair, sent_a, sent_b, own_a, own_b = join(
        site_step_kernel, "site_step", [(2, *half), (2, *half), (2, *units), terms, terms],
        [
            a0, b0, swap_site(a0, 1), swap_site(b0, 2), stem_units, swap_z(stem_units, 2),
            kept_a, swap_site(sent_a, 1), kept_b, swap_site(sent_b, 2),
        ],
        [plan],
        wide_dims=[terms, terms],
    )

    a2, b2 = swap_site(a, 2), swap_site(b, 1)
    near = swap_z(stem_pair, 1)
    kept, sent = site_sum(scalars, own_a, swap_site(sent_a, 2), own_b, swap_site(sent_b, 1))
    n = 3 * UNITS * STEM_ROWS
    others, all_others, packed = join(
        three_kernel, "three", [(3, *quarters), (3, *units), (24 * HALF + n, QUARTER)],
        [stem_pair, near, a, b, a2, b2], [kept],
    )

    over = [swap_site(others, distance) for distance in (1, 2, 3)]
    packed = swap_core(packed)
    whole_proj = [(0, 0, ("all", 0), 0, D // N_FSDP)]
    first = [half_places(0, 0) + half_places(1, 0), half_places(0, HALF) + half_places(2, HALF)]
    last = [half_places(2, 0) + half_places(3, 0), half_places(1, HALF) + half_places(3, HALF)]
    proj_parts = [
        (proj_weight, whole_proj, 0), (proj_swapped, whole_proj, 1),
        (rows_of(a), first[0], 0), (rows_of(b), first[1], 0),
        (rows_of(a2), last[0], 0), (rows_of(b2), last[1], 0),
        (packed, sum(first + last, []) + [n], 1),
    ]
    grad = input_gradient(scalars, proj_parts, inputs, cotangent)
    own, sent = near_sum(scalars, kept, swap_z(sent, 1), [grad])
    (over,) = join(collect_kernel, "collect", [(3, 3, *quarters)], over, [grad, sent])
    over = rows_of(over)
    last = sum((unit_places(d) for d in (1, 2, 3)), [])
    whole_stem = [(tap, 0, ("all", 0), 0, STEM_ROWS) for tap in range(TAPS)]
    stem_parts = [
        (stem_weight.reshape(-1, D), whole_stem, 0), (stem_swapped.reshape(-1, D), whole_stem, 1),
        (rows_of(all_others), all_places(), 0), (over, last, 0),
        (packed, [24 * HALF] + all_places(), 1), (swap_core(over), last, 1),
    ]

    payloads = stem_payloads(plan, stem_parts, grad)
    received = {0: payloads[0]}
    for d in PAYLOAD_ORDER[1:]:
        received[d] = lax.ppermute(payloads[d], "fsdp", [(i, i ^ d) for i in range(N_FSDP)])
    scale = 1.0 / math.sqrt(N_SITE * N_FSDP * ROWS)
    terms = far_sum(scalars, own, swap_z(sent, 2), scale, [received[4]])
    weight_grad = lay_columns(scalars, [terms] + [swap_site(terms, d) for d in (1, 2, 3)])
    stem_grad = owner_rows(plan, [received[d] for d in PAYLOAD_ORDER])
    return (stem_grad[None], weight_grad)


def plain_body(held_input, held_cotangent, proj_weight, stem_weight, seg_counts):
    group_size = lax.axis_size("fsdp")
    capacity = 2 * ((OWN_SEG + 2 * group_size - 1) // (2 * group_size))
    my_index = lax.axis_index("fsdp")
    cotangent = held_cotangent[0]
    normed, inverse = normalise(held_input[0])
    normed_bf = normed.astype(jnp.bfloat16)
    proj_back = dot_nt(cotangent, lax.all_gather(proj_weight, "fsdp", axis=0, tiled=True))
    input_grad = cotangent.astype(jnp.float32) + inverse * (
        proj_back
        - jnp.mean(proj_back, axis=-1, keepdims=True)
        - normed * jnp.mean(proj_back * normed, axis=-1, keepdims=True)
    )
    input_grad = input_grad.astype(jnp.bfloat16)
    counts = seg_counts[0]
    endings = jnp.cumsum(counts)
    starts = endings - counts
    slot_ids = jnp.arange(HOLD, dtype=jnp.int32)
    item_index = 2 * (slot_ids // 2 * group_size + my_index) + slot_ids % 2
    owner_ids = jnp.sum((item_index[:, None] >= endings[None, :]).astype(jnp.int32), axis=1)
    earlier = (slot_ids[None, :] < slot_ids[:, None]) & (owner_ids[None, :] == owner_ids[:, None])
    rank_ids = jnp.sum(earlier.astype(jnp.int32), axis=1)
    target = owner_ids * capacity + rank_ids
    positions = jnp.arange(group_size * capacity, dtype=jnp.int32)
    matched = target[None, :] == positions[:, None]
    filled = jnp.any(matched, axis=1)
    source = jnp.sum(jnp.where(matched, slot_ids[None, :], 0), axis=1)
    owner_hit = jnp.arange(group_size, dtype=jnp.int32) == my_index
    my_count = jnp.sum(jnp.where(owner_hit, counts, 0))
    my_start = jnp.sum(jnp.where(owner_hit, starts, 0))
    segment = jnp.arange(OWN_SEG, dtype=jnp.int32)
    is_live = segment < my_count
    holder = (my_start + segment) // 2 % group_size
    before = (
        (segment[None, :] < segment[:, None])
        & (holder[None, :] == holder[:, None])
        & is_live[None, :]
    )
    holder_rank = jnp.sum(before.astype(jnp.int32), axis=1)
    row_index = jnp.where(is_live, holder * capacity + holder_rank, 0)
    held_segments = input_grad.reshape(HOLD, SEG, D)
    zero_bf = jnp.zeros((), jnp.bfloat16)
    send_rows = jnp.where(filled[:, None, None], jnp.take(held_segments, source, axis=0), zero_bf)
    received = lax.all_to_all(
        send_rows.reshape(group_size, capacity, SEG, D), "fsdp", split_axis=0, concat_axis=0, tiled=True
    )
    picked = jnp.take(received.reshape(group_size * capacity, SEG, D), row_index, axis=0)
    frames = jnp.where(is_live[:, None, None], picked, zero_bf).reshape(OWN_SEG * SEG, D)
    tap_terms = jnp.einsum(
        "rd,kcd->krc",
        frames,
        lax.all_gather(stem_weight, "fsdp", axis=1, tiled=True),
        preferred_element_type=jnp.float32,
    )
    shifted = jnp.concatenate(
        [tap_terms[0][1:], jnp.zeros((1, tap_terms.shape[2]), jnp.float32)], 0
    )
    stem_rows = (
        jnp.stack([tap_terms[1], tap_terms[2] + shifted], 1)
        .reshape(2 * OWN_SEG * SEG, tap_terms.shape[2])
        .astype(jnp.bfloat16)
    )
    shard_sum = lax.psum_scatter(
        lax.dot_general(
            normed_bf, cotangent, (((0,), (0,)), ((), ())), preferred_element_type=jnp.float32
        ),
        "fsdp",
        scatter_dimension=0,
        tiled=True,
    )
    shard_sum = lax.psum(shard_sum, "site")
    weight_grad = shard_sum / math.sqrt(lax.axis_size("site") * group_size * ROWS)
    return (stem_rows[None], weight_grad)


def solution(mesh):
    placed = (
        P("site", "fsdp", None),
        P("site", "fsdp", None),
        P("fsdp", None),
        P(None, "fsdp", None),
        P("site", None),
    )
    fits = (mesh.shape["site"], mesh.shape["fsdp"]) == (N_SITE, N_FSDP)
    return jax.shard_map(
        body if fits else plain_body,
        mesh=mesh,
        in_specs=placed,
        out_specs=(P("site", "fsdp", None), P("fsdp", None)),
        check_vma=False,
    )
```

```python
import math

import jax
import jax.numpy as jnp
from jax import lax
from jax.experimental import pallas as pl
from jax.experimental.pallas import tpu as pltpu
from jax.sharding import PartitionSpec as P

D = 1536
SEG = 8
HOLD = 64
OWN_SEG = 128
N_SITE = 4
N_FSDP = 8
N_Z = N_FSDP // 2
QUARTER = D // N_SITE
CAP = OWN_SEG // N_FSDP
CS = 512
ROWS = HOLD * SEG
BLOCK = 128
LANES = 128
COLUMNS = 768
PAYLOAD_ORDER = (0, 4, 5, 2, 3, 6, 7, 1)
MIB = 1024 * 1024

EPSILON = 1e-05
F32 = jnp.float32
BF16 = jnp.bfloat16


def swap_core(value):
    return lax.ppermute(value, "fsdp", [(i, i ^ 1) for i in range(N_FSDP)])


def swap_z(value, distance):
    return lax.ppermute(value, "fsdp", [(i, i ^ (2 * distance)) for i in range(N_FSDP)])


def swap_site(value, distance):
    return lax.ppermute(value, "site", [(i, i ^ distance) for i in range(N_SITE)])


def hold(value, *first):
    return pl.pallas_call(
        lambda *refs: None,
        name="hold",
        out_shape=shape(value.shape, value.dtype),
        in_specs=[HBM] + [ANY] * len(first),
        out_specs=HBM,
        input_output_aliases={0: 0},
        cost_estimate=pl.CostEstimate(flops=0, bytes_accessed=0, transcendentals=0),
    )(value, *first)


Z_ORDER = (2, 1, 3)
HALF = D // N_FSDP // 2
STEM_ROWS = CS // N_FSDP
TAPS = 3


def half_places(site, low):
    return [(0, z, ("xor", site), low, HALF) for z in Z_ORDER]


SPLIT = STEM_ROWS // 2
QUARTER_BLOCKS = ((1, 0, STEM_ROWS), (0, 0, SPLIT))
WHOLE_BLOCKS = ((2, 0, STEM_ROWS), (0, SPLIT, STEM_ROWS - SPLIT))
QUARTER_ROWS = sum(count for _, _, count in QUARTER_BLOCKS)
UNIT_ROWS = QUARTER_ROWS + N_SITE * sum(count for _, _, count in WHOLE_BLOCKS)


def unit_places(site):
    return [(tap, z, ("xor", site), low, count) for z in Z_ORDER for tap, low, count in QUARTER_BLOCKS]


def all_places():
    blocks = [(tap, ("xor", 0), low, count) for tap, low, count in QUARTER_BLOCKS]
    blocks += [(tap, ("abs", j), low, count) for tap, low, count in WHOLE_BLOCKS for j in range(N_SITE)]
    return [(tap, z, kind, low, count) for z in Z_ORDER for tap, kind, low, count in blocks]


def shard_places(tap, count):
    return [(tap, 0, ("abs", j), 0, count) for j in range(N_SITE)]


def rows_of(value):
    return value.reshape(-1, QUARTER)


def call(kernel, name, out_shape, grid, in_specs, out_specs, scratch, vmem=16):
    return pl.pallas_call(
        kernel,
        name=name,
        out_shape=out_shape,
        grid_spec=pltpu.PrefetchScalarGridSpec(
            num_scalar_prefetch=1,
            grid=grid,
            in_specs=in_specs,
            out_specs=out_specs,
            scratch_shapes=scratch,
        ),
        compiler_params=pltpu.CompilerParams(
            dimension_semantics=("arbitrary",) * len(grid), vmem_limit_bytes=vmem * MIB
        ),
        cost_estimate=pl.CostEstimate(flops=0, bytes_accessed=0, transcendentals=0),
    )


ANY = pl.BlockSpec(memory_space=pl.ANY)
HBM = pl.BlockSpec(memory_space=pltpu.HBM)


def whole(shape):
    return pl.BlockSpec(shape, lambda i, scalars: (0,) * len(shape))


def row_block(rows, columns):
    return pl.BlockSpec((rows, columns), lambda i, scalars: (i, 0))


def shape(dims, dtype):
    return jax.ShapeDtypeStruct(dims, dtype)


def dot_nt(a, b):
    return lax.dot_general(a, b, (((1,), (1,)), ((), ())), preferred_element_type=F32)


def join(kernel, name, out_dims, values, first=(), wide_dims=()):
    n = len(values)

    def wrapped(*refs):
        kernel(*refs[:n], *refs[n + len(first) :])

    out = tuple(shape(dims, BF16) for dims in out_dims) + tuple(shape(dims, F32) for dims in wide_dims)
    vmem = pl.BlockSpec(memory_space=pltpu.VMEM)
    return pl.pallas_call(
        wrapped,
        name=name,
        out_shape=out,
        in_specs=[vmem] * n + [ANY] * len(first),
        out_specs=(vmem,) * len(out),
        compiler_params=pltpu.CompilerParams(vmem_limit_bytes=14 * MIB),
        cost_estimate=pl.CostEstimate(flops=0, bytes_accessed=0, transcendentals=0),
    )(*values, *first)


def cut_proj_kernel(shard, out):
    at = pl.multiple_of(lax.axis_index("site") * QUARTER, QUARTER)
    out[...] = shard[:, pl.ds(at, QUARTER)]


def halves_kernel(far, near, farthest, sent_a, sent_b, stem, a, b, units):
    for i, piece in enumerate((far, near, farthest)):
        a[i * HALF : (i + 1) * HALF, :] = piece[:HALF, :]
        b[i * HALF : (i + 1) * HALF, :] = piece[HALF:, :]
    for out, sent in ((a, sent_a), (b, sent_b)):
        out[3 * HALF : 3 * HALF + D // 4, :] = sent[0]
        out[3 * HALF + D // 4 :, :] = sent[1]
    at = pl.multiple_of(lax.axis_index("site") * QUARTER, QUARTER)
    pieces = [stem[tap, low : low + count, pl.ds(at, QUARTER)] for tap, low, count in QUARTER_BLOCKS]
    for tap, low, count in WHOLE_BLOCKS:
        pieces += column_pieces(stem[tap, low : low + count, :])
    pack_rows(units, pieces)


def pack_rows(out, pieces):
    at = 0
    for piece in pieces:
        out[at : at + piece.shape[0], :] = piece
        at += piece.shape[0]


def column_pieces(rows):
    return [rows[:, i * QUARTER : (i + 1) * QUARTER] for i in range(N_SITE)]


def site_step_kernel(
    shard, stem, a0, b0, a1, b1, units, far, kept_a, kept_b, a, b, packed, pair, own_a, own_b
):
    pair[0], pair[1] = units[...], far[...]
    n, m = 3 * HALF, D // 4
    for sent, came, kept, out, own in ((a0, a1, kept_a, a, own_a), (b0, b1, kept_b, b, own_b)):
        for j, source in enumerate((sent, came)):
            out[j * n : (j + 1) * n, :] = source[:n, :]
        own[...] = kept[0] + came[n : n + m, :].astype(F32)
        out[2 * n :, :] = (kept[1] + came[n + m :, :].astype(F32)).astype(BF16)
    pieces = column_pieces(shard[...])
    for tap in range(TAPS):
        pieces += column_pieces(stem[tap])
    pack_rows(packed, pieces + [ref[:n, :] for ref in (a0, a1, b0, b1)])


def collect_kernel(a, b, c, out):
    out[0], out[1], out[2] = a[...], b[...], c[...]


def three_kernel(pair, near, a2, b2, quarters, units, packed):
    n = 6 * HALF
    packed[:n, :], packed[n:, :] = a2[:n, :], b2[:n, :]
    for i, piece in enumerate((pair.at[1], near.at[0], near.at[1])):
        quarters[i] = piece[:QUARTER_ROWS, :]
        units[i] = piece[...]


def normalise(inputs):
    inputs = inputs.astype(F32)
    centered = inputs - jnp.mean(inputs, axis=-1, keepdims=True)
    variance = jnp.mean(centered * centered, axis=-1, keepdims=True)
    inverse = lax.rsqrt(variance + EPSILON)
    return centered * inverse, inverse


def norm_kernel(scalars, x_ref, *refs):
    out_ref, turned = refs[-2:]
    core = scalars[1] % 2
    normed, _ = normalise(x_ref[...])
    turned[...] = normed.astype(BF16).T
    shard = D // N_FSDP
    for z in range(N_Z):
        rows = pl.ds(pl.multiple_of((2 * z + core) * shard, shard), shard)
        out_ref[pl.ds(z * shard, shard), :] = turned[rows, :]


def norm_half(scalars, inputs, first=()):
    return call(
        norm_kernel, "norm_half", shape((D // 2, ROWS), BF16), (ROWS // BLOCK,),
        [row_block(BLOCK, D)] + [ANY] * len(first),
        pl.BlockSpec((D // 2, BLOCK), lambda i, scalars: (0, i)), [pltpu.VMEM((D, BLOCK), BF16)],
    )(scalars, inputs, *first)


OUTER_PLACES = (((0, 0), (0, 0)), ((1, 0), (0, 1)), ((0, 1), (1, 0)), ((1, 1), (1, 1)))


def outer_kernel(scalars, na_ref, nb_ref, ca_ref, cb_ref, ka_ref, sa_ref, kb_ref, sb_ref):
    step = pl.program_id(0)
    total = jnp.dot(na_ref[...], ca_ref[...], preferred_element_type=F32)
    total = total + jnp.dot(nb_ref[...], cb_ref[...], preferred_element_type=F32)
    low, high = total[: D // 4, :], total[D // 4 :, :]
    for at, (a, b) in enumerate(OUTER_PLACES):

        @pl.when(step == at)
        def _(a=a, b=b):
            for (ref, i), value in (((ka_ref, sa_ref)[a[0]], a[1]), low), (((kb_ref, sb_ref)[b[0]], b[1]), high):
                ref[i] = value.astype(ref.dtype)


def outer_pieces(scalars, normed_a, normed_b, cotangent_a, cotangent_b):
    dims = (2, D // 4, QUARTER)
    column = pl.BlockSpec((ROWS, QUARTER), lambda i, scalars: (0, lax.bitwise_xor(scalars[0], i)))
    return call(
        outer_kernel, "outer_pieces", (shape(dims, F32), shape(dims, BF16)) * 2, (N_SITE,),
        [whole((D // 2, ROWS))] * 2 + [column] * 2, (whole(dims),) * 4, [],
    )(scalars, normed_a, normed_b, cotangent_a, cotangent_b)


def site_sum_kernel(scalars, oa_ref, ra_ref, ob_ref, rb_ref, kept_ref, sent_ref, total):
    shard = D // N_FSDP
    z = scalars[1] // 2
    total[: D // 4, :] = oa_ref[...] + ra_ref[6 * HALF :, :].astype(F32)
    total[D // 4 :, :] = ob_ref[...] + rb_ref[6 * HALF :, :].astype(F32)
    for distance, (ref, i) in enumerate(((kept_ref, 0), (sent_ref, 0), (kept_ref, 1), (sent_ref, 1))):
        rows = pl.ds(pl.multiple_of(lax.bitwise_xor(z, distance) * shard, shard), shard)
        ref[i] = total[rows, :].astype(ref.dtype)


def site_sum(scalars, *values):
    out = (2, D // N_FSDP, QUARTER)
    return call(
        site_sum_kernel, "site_sum", (shape(out, F32), shape(out, BF16)), (1,),
        [whole(value.shape) for value in values], (whole(out),) * 2, [pltpu.VMEM((D // 2, QUARTER), F32)],
    )(scalars, *values)


def near_sum_kernel(scalars, kept_ref, came_ref, *refs):
    own_ref, sent_ref = refs[-2:]
    own_ref[...] = kept_ref[0] + came_ref[0].astype(F32)
    sent_ref[...] = (kept_ref[1] + came_ref[1].astype(F32)).astype(BF16)


def near_sum(scalars, kept, came, first):
    dims, out = (2, D // N_FSDP, QUARTER), (D // N_FSDP, QUARTER)
    return call(
        near_sum_kernel, "near_sum", (shape(out, F32), shape(out, BF16)), (1,),
        [whole(dims)] * 2 + [ANY] * len(first), (whole(out),) * 2, [],
    )(scalars, kept, came, *first)


def far_sum_kernel(scale, scalars, own_ref, came_ref, *refs):
    refs[-1][...] = (own_ref[...] + came_ref[...].astype(F32)) * scale


def far_sum(scalars, own, came, scale, first):
    dims = (D // N_FSDP, QUARTER)
    return call(
        lambda *refs: far_sum_kernel(scale, *refs), "far_sum", shape(dims, F32), (1,),
        [whole(dims)] * 2 + [ANY] * len(first), whole(dims), [],
    )(scalars, own, came, *first)


def weight_copies(tables, scalars, refs, weight, sem):
    site, index = scalars[0], scalars[1]
    shard = weight.shape[1] // N_FSDP
    copies = []
    for (places, swapped), ref in zip(tables, refs, strict=True):
        at = 0
        for place in places:
            if isinstance(place, int):
                at += place
                continue
            tap, z, (kind, quarter), low, count = place
            start = lax.bitwise_xor(index, 2 * z + swapped) * shard + low
            rows = pl.ds(pl.multiple_of(start, math.gcd(shard, low)), count)
            columns = pl.ds(quarter * QUARTER, QUARTER)
            if kind == "all":
                columns = pl.ds(0, D)
            elif kind == "xor":
                column = lax.bitwise_xor(site, quarter) * QUARTER
                columns = pl.ds(pl.multiple_of(column, QUARTER), QUARTER)
            source = ref.at[pl.ds(at, count), :]
            copies.append(pltpu.make_async_copy(source, weight.at[tap, rows, columns], sem))
            at += count
        assert at == ref.shape[0]
    return copies


def fetch(source, target, sem):
    copy = pltpu.make_async_copy(source, target, sem)
    copy.start()
    return copy


def input_grad_kernel(tables, scalars, *refs):
    n = len(tables)
    parts, (x_hbm, cot_hbm, out_ref) = refs[:n], refs[n : n + 3]
    x_ref, cot_ref, weight, normed, inverse, back, sems, sem = refs[n + 3 :]
    x_copy = fetch(x_hbm, x_ref, sems.at[0])
    cot_copy = fetch(cot_hbm, cot_ref, sems.at[1])
    copies = weight_copies(tables, scalars, parts, weight, sem)
    for copy in copies:
        copy.start()
    x_copy.wait()

    @pl.loop(0, ROWS // BLOCK)
    def _(i):
        rows = pl.ds(pl.multiple_of(i * BLOCK, BLOCK), BLOCK)
        normed[rows, :], inverse[rows, :] = normalise(x_ref[rows, :])

    cot_copy.wait()
    for copy in copies:
        copy.wait()

    @pl.loop(0, D // COLUMNS)
    def _(i):
        rows = pl.ds(pl.multiple_of(i * COLUMNS, COLUMNS), COLUMNS)
        back[:, rows] = dot_nt(cot_ref[...], weight[0, rows, :])

    @pl.loop(0, ROWS // BLOCK)
    def _(i):
        rows = pl.ds(pl.multiple_of(i * BLOCK, BLOCK), BLOCK)
        term, row_normed = back[rows, :], normed[rows, :]
        inner = term - jnp.mean(term, axis=-1, keepdims=True)
        inner = inner - row_normed * jnp.mean(term * row_normed, axis=-1, keepdims=True)
        out_ref[rows, :] = (cot_ref[rows, :].astype(F32) + inverse[rows, :] * inner).astype(BF16)


def split_parts(parts):
    return [(places, swapped) for _, places, swapped in parts], [value for value, _, _ in parts]


def input_gradient(scalars, parts, inputs, cotangent):
    tables, values = split_parts(parts)
    return call(
        lambda *refs: input_grad_kernel(tables, *refs), "input_gradient", shape((ROWS, D), BF16),
        (1,), [HBM] * (len(values) + 2), whole((ROWS, D)),
        [
            pltpu.VMEM((ROWS, D), BF16),
            pltpu.VMEM((ROWS, D), BF16),
            pltpu.VMEM((1, D, D), BF16),
            pltpu.VMEM((ROWS, D), F32),
            pltpu.VMEM((ROWS, 1), F32),
            pltpu.VMEM((ROWS, D), F32),
            pltpu.SemaphoreType.DMA((2,)),
            pltpu.SemaphoreType.DMA,
        ],
        vmem=22,
    )(scalars, *values, inputs, cotangent)


def held_before(start, holder):
    return 2 * (start // (2 * N_FSDP)) + jnp.clip(start % (2 * N_FSDP) - 2 * holder, 0, 2)


SLOTS_AT = 2
SEGMENTS_AT = SLOTS_AT + HOLD
COUNT_AT = SEGMENTS_AT + OWN_SEG


def plan_kernel(scalars, plan):
    site, index = scalars[0], scalars[1]
    plan[0], plan[1] = site, index
    starts = [jnp.int32(0)]
    for owner in range(N_FSDP):
        starts.append(starts[-1] + scalars[2 + owner])

    @pl.loop(0, HOLD)
    def _(slot):
        item = 2 * (slot // 2 * N_FSDP + index) + slot % 2
        owner = jnp.int32(0)
        start = jnp.int32(0)
        for other in range(1, N_FSDP):
            passed = item >= starts[other]
            owner = jnp.where(passed, other, owner)
            start = jnp.where(passed, starts[other], start)
        plan[SLOTS_AT + slot] = lax.bitwise_xor(owner, index) * CAP + slot - held_before(start, index)

    start = jnp.int32(0)
    for owner in range(N_FSDP):
        start = start + jnp.where(owner < index, scalars[2 + owner], 0)
    count = scalars[2 + index]
    plan[COUNT_AT] = count

    @pl.loop(0, OWN_SEG)
    def _(segment):
        item = start + jnp.minimum(segment, count - 1)
        holder = item // 2 % N_FSDP
        rank = 2 * (item // (2 * N_FSDP)) + item % 2 - held_before(start, holder)
        plan[SEGMENTS_AT + segment] = lax.bitwise_xor(holder, index) * CAP + rank


def plan_of(scalars):
    return call(
        plan_kernel, "plan", shape((COUNT_AT + 1,), jnp.int32), (1,), [],
        pl.BlockSpec(memory_space=pltpu.SMEM), [],
    )(scalars)


def stem_kernel(tables, scalars, *refs):
    n = len(tables)
    parts, grad_ref, outs = refs[:n], refs[n], refs[n + 1 : n + 1 + N_FSDP]
    weight, mixed, leading, packed, firsts, sem, out_sem = refs[n + 1 + N_FSDP :]
    copies = weight_copies(tables, scalars, parts, weight, sem)
    for copy in copies:
        copy.start()
    for copy in copies:
        copy.wait()
    index = scalars[1]
    for lane in range(0, CS, CS // 2):
        span = pl.ds(lane, CS // 2)
        even = dot_nt(grad_ref[...], weight[1, span, :])
        first = dot_nt(grad_ref[...], weight[0, span, :])
        leading[:, span] = first
        row = lax.broadcasted_iota(jnp.int32, first.shape, 0)
        following = jnp.where(row % SEG == SEG - 1, 0.0, pltpu.roll(first, ROWS - 1, 0))
        odd = dot_nt(grad_ref[...], weight[2, span, :]) + following
        for part in range(CS // 2 // LANES):
            at = lane // LANES + part
            columns = slice(part * LANES, (part + 1) * LANES)
            mixed[at, pl.ds(0, ROWS, stride=2), :] = even[:, columns]
            mixed[at, pl.ds(1, ROWS, stride=2), :] = odd[:, columns]

    @pl.loop(0, HOLD, unroll=8)
    def _(slot):
        block = scalars[SLOTS_AT + slot]
        place, rank = block // CAP, block % CAP
        rows = pl.ds(pl.multiple_of(slot * 2 * SEG, 2 * SEG), 2 * SEG)
        for lane in range(CS // LANES):
            packed[place, rank, :, pl.ds(lane * LANES, LANES)] = mixed[lane, rows, :].astype(BF16)
        firsts[pl.ds(block, 1), :] = leading[pl.ds(slot * SEG, 1), :]

    packed[:, CAP] = firsts[...].reshape(N_FSDP, CAP, CS).astype(BF16)
    copies = [
        pltpu.make_async_copy(packed.at[place], outs[place], out_sem.at[place])
        for place in range(N_FSDP)
    ]
    for copy in copies:
        copy.start()
    for copy in copies:
        copy.wait()


def stem_payloads(scalars, parts, grad):
    tables, values = split_parts(parts)
    payload = (CAP + 1, 2 * SEG, CS)
    return call(
        lambda *refs: stem_kernel(tables, *refs), "stem_payloads",
        (shape(payload, BF16),) * N_FSDP, (1,),
        [ANY] * len(values) + [whole((ROWS, D))], (HBM,) * N_FSDP,
        [
            pltpu.VMEM((3, CS, D), BF16),
            pltpu.VMEM((CS // LANES, 2 * ROWS, LANES), F32),
            pltpu.VMEM((ROWS, CS), F32),
            pltpu.VMEM((N_FSDP,) + payload, BF16),
            pltpu.VMEM((N_FSDP * CAP, CS), F32),
            pltpu.SemaphoreType.DMA,
            pltpu.SemaphoreType.DMA((N_FSDP,)),
        ],
        vmem=18,
    )(scalars, *values, grad)


def owner_kernel(scalars, *refs):
    payloads, terms, (out_ref, total), (packed, firsts, sem, total_sem) = (
        refs[:N_FSDP], refs[N_FSDP : N_FSDP + N_SITE], refs[-6:-4], refs[-4:]
    )
    step = pl.program_id(0)
    total_copies = []
    for distance, term in enumerate(terms):
        at = pl.multiple_of(lax.bitwise_xor(scalars[0], distance) * QUARTER, QUARTER)
        total_copies.append(
            pltpu.make_async_copy(term, total.at[:, pl.ds(at, QUARTER)], total_sem.at[distance])
        )

    @pl.when(step == 0)
    def _():
        for copy in total_copies:
            copy.start()

    @pl.when(step == 0)
    def _():
        copies = [
            pltpu.make_async_copy(payloads[i], packed.at[place], sem.at[place])
            for i, place in enumerate(PAYLOAD_ORDER)
        ]
        for copy in copies:
            copy.start()
        for copy in copies:
            copy.wait()
        firsts[...] = packed[:, CAP].astype(F32).reshape(N_FSDP * CAP, CS)

    count = scalars[COUNT_AT]
    per_step = OWN_SEG // 4
    last_row = lax.broadcasted_iota(jnp.int32, (2 * SEG, CS), 0) == 2 * SEG - 1

    @pl.loop(0, per_step, unroll=4)
    def _(local):
        segment = step * per_step + local
        block = scalars[SEGMENTS_AT + segment]
        follower = scalars[SEGMENTS_AT + jnp.minimum(segment + 1, OWN_SEG - 1)]
        first = jnp.broadcast_to(firsts[pl.ds(follower, 1), :], (2 * SEG, CS))
        first = jnp.where(last_row & (segment + 1 < count), first, 0.0)
        rows = packed[block // CAP, block % CAP].astype(F32) + first
        to = pl.ds(pl.multiple_of(local * 2 * SEG, 2 * SEG), 2 * SEG)
        out_ref[to, :] = jnp.where(segment < count, rows, 0.0).astype(BF16)

    @pl.when(step == pl.num_programs(0) - 1)
    def _():
        for copy in total_copies:
            copy.wait()


def owner_rows(scalars, payloads, terms):
    payload = (CAP + 1, 2 * SEG, CS)
    rows = 2 * OWN_SEG * SEG
    return call(
        owner_kernel, "owner_rows", (shape((rows, CS), BF16), shape((D // N_FSDP, D), F32)), (4,),
        [ANY] * (N_FSDP + N_SITE), (row_block(rows // 4, CS), HBM),
        [
            pltpu.VMEM((N_FSDP,) + payload, BF16),
            pltpu.VMEM((N_FSDP * CAP, CS), F32),
            pltpu.SemaphoreType.DMA((N_FSDP,)),
            pltpu.SemaphoreType.DMA((N_SITE,)),
        ],
    )(scalars, *payloads, *terms)


def body(held_input, held_cotangent, proj_weight, stem_weight, seg_counts):
    site, index = lax.axis_index("site"), lax.axis_index("fsdp")
    scalars = jnp.concatenate([jnp.stack([site, index]).astype(jnp.int32), seg_counts[0]])
    inputs, cotangent = held_input[0], held_cotangent[0]

    plan = plan_of(scalars)
    piece = (D // N_FSDP, QUARTER)
    half = (3, HALF, QUARTER)
    units = (UNIT_ROWS, QUARTER)
    quarters = (QUARTER_ROWS, QUARTER)

    (proj_quarter,) = join(cut_proj_kernel, "cut_proj", [piece], [proj_weight])
    around = [swap_z(proj_quarter, distance) for distance in Z_ORDER]
    normed_own = norm_half(scalars, inputs, [proj_quarter])
    normed_theirs = norm_half(scalars, swap_core(inputs), [normed_own])
    kept_a, sent_a, kept_b, sent_b = outer_pieces(
        scalars, normed_own, normed_theirs, cotangent, swap_core(cotangent)
    )
    n, m = 3 * HALF, D // 4
    a0, b0, stem_units = join(
        halves_kernel, "halves", [(n + 2 * m, QUARTER)] * 2 + [units],
        [*around, sent_a, sent_b, stem_weight],
    )

    a, b, packed, stem_pair, own_a, own_b = join(
        site_step_kernel, "site_step", [(2 * n + m, QUARTER)] * 2 + [(D + 4 * n, QUARTER), (2, *units)],
        [
            proj_weight, stem_weight, a0, b0, swap_site(a0, 1), swap_site(b0, 2),
            stem_units, swap_z(stem_units, 2), kept_a, kept_b,
        ],
        [plan],
        wide_dims=[(m, QUARTER)] * 2,
    )

    a2, b2 = swap_site(a, 2), swap_site(b, 1)
    near = swap_z(stem_pair, 1)
    packed = swap_core(packed)
    kept, sent = site_sum(scalars, own_a, a2, own_b, b2)
    others, all_others, late = join(
        three_kernel, "three", [(3, *quarters), (3, *units), (4 * n, QUARTER)],
        [stem_pair, near, a2, b2], [kept, packed],
    )

    over = [swap_site(others, distance) for distance in (1, 2, 3)]
    late, late_stem = swap_core(late), swap_core(rows_of(all_others))
    whole_proj = [(0, 0, ("all", 0), 0, D // N_FSDP)]
    first = [half_places(0, 0) + half_places(1, 0), half_places(0, HALF) + half_places(2, HALF)]
    last = [half_places(2, 0) + half_places(3, 0), half_places(1, HALF) + half_places(3, HALF)]
    proj_parts = [
        (proj_weight, whole_proj, 0),
        (a, first[0] + [m], 0), (b, first[1] + [m], 0),
        (a2, last[0] + [m], 0), (b2, last[1] + [m], 0),
        (packed, shard_places(0, D // N_FSDP) + [D // 2] + sum(first, []), 1), (late, sum(last, []), 1),
    ]
    grad = input_gradient(scalars, proj_parts, inputs, cotangent)
    own, sent = near_sum(scalars, kept, swap_z(sent, 1), [grad])
    (over,) = join(collect_kernel, "collect", [(3, 3, *quarters)], over, [grad, sent, late_stem])
    over = rows_of(over)
    last = sum((unit_places(d) for d in (1, 2, 3)), [])
    whole_stem = [(tap, 0, ("all", 0), 0, STEM_ROWS) for tap in range(TAPS)]
    stem_parts = [
        (stem_weight.reshape(-1, D), whole_stem, 0),
        (
            packed,
            [D // 2] + sum((shard_places(tap, STEM_ROWS) for tap in range(TAPS)), []) + [4 * n], 1,
        ),
        (rows_of(all_others), all_places(), 0), (over, last, 0),
        (late_stem, all_places(), 1), (swap_core(over), last, 1),
    ]

    payloads = stem_payloads(plan, stem_parts, grad)
    received = {0: payloads[0]}
    for d in PAYLOAD_ORDER[1:]:
        received[d] = lax.ppermute(payloads[d], "fsdp", [(i, i ^ d) for i in range(N_FSDP)])
    scale = 1.0 / math.sqrt(N_SITE * N_FSDP * ROWS)
    terms = far_sum(scalars, own, swap_z(sent, 2), scale, [received[4]])
    terms = [terms] + [swap_site(terms, d) for d in (1, 2, 3)]
    stem_grad, weight_grad = owner_rows(plan, [received[d] for d in PAYLOAD_ORDER], terms)
    return (stem_grad[None], weight_grad)


def plain_body(held_input, held_cotangent, proj_weight, stem_weight, seg_counts):
    group_size = lax.axis_size("fsdp")
    capacity = 2 * ((OWN_SEG + 2 * group_size - 1) // (2 * group_size))
    my_index = lax.axis_index("fsdp")
    cotangent = held_cotangent[0]
    normed, inverse = normalise(held_input[0])
    normed_bf = normed.astype(jnp.bfloat16)
    proj_back = dot_nt(cotangent, lax.all_gather(proj_weight, "fsdp", axis=0, tiled=True))
    input_grad = cotangent.astype(jnp.float32) + inverse * (
        proj_back
        - jnp.mean(proj_back, axis=-1, keepdims=True)
        - normed * jnp.mean(proj_back * normed, axis=-1, keepdims=True)
    )
    input_grad = input_grad.astype(jnp.bfloat16)
    counts = seg_counts[0]
    endings = jnp.cumsum(counts)
    starts = endings - counts
    slot_ids = jnp.arange(HOLD, dtype=jnp.int32)
    item_index = 2 * (slot_ids // 2 * group_size + my_index) + slot_ids % 2
    owner_ids = jnp.sum((item_index[:, None] >= endings[None, :]).astype(jnp.int32), axis=1)
    earlier = (slot_ids[None, :] < slot_ids[:, None]) & (owner_ids[None, :] == owner_ids[:, None])
    rank_ids = jnp.sum(earlier.astype(jnp.int32), axis=1)
    target = owner_ids * capacity + rank_ids
    positions = jnp.arange(group_size * capacity, dtype=jnp.int32)
    matched = target[None, :] == positions[:, None]
    filled = jnp.any(matched, axis=1)
    source = jnp.sum(jnp.where(matched, slot_ids[None, :], 0), axis=1)
    owner_hit = jnp.arange(group_size, dtype=jnp.int32) == my_index
    my_count = jnp.sum(jnp.where(owner_hit, counts, 0))
    my_start = jnp.sum(jnp.where(owner_hit, starts, 0))
    segment = jnp.arange(OWN_SEG, dtype=jnp.int32)
    is_live = segment < my_count
    holder = (my_start + segment) // 2 % group_size
    before = (
        (segment[None, :] < segment[:, None])
        & (holder[None, :] == holder[:, None])
        & is_live[None, :]
    )
    holder_rank = jnp.sum(before.astype(jnp.int32), axis=1)
    row_index = jnp.where(is_live, holder * capacity + holder_rank, 0)
    held_segments = input_grad.reshape(HOLD, SEG, D)
    zero_bf = jnp.zeros((), jnp.bfloat16)
    send_rows = jnp.where(filled[:, None, None], jnp.take(held_segments, source, axis=0), zero_bf)
    received = lax.all_to_all(
        send_rows.reshape(group_size, capacity, SEG, D), "fsdp", split_axis=0, concat_axis=0, tiled=True
    )
    picked = jnp.take(received.reshape(group_size * capacity, SEG, D), row_index, axis=0)
    frames = jnp.where(is_live[:, None, None], picked, zero_bf).reshape(OWN_SEG * SEG, D)
    tap_terms = jnp.einsum(
        "rd,kcd->krc",
        frames,
        lax.all_gather(stem_weight, "fsdp", axis=1, tiled=True),
        preferred_element_type=jnp.float32,
    )
    shifted = jnp.concatenate(
        [tap_terms[0][1:], jnp.zeros((1, tap_terms.shape[2]), jnp.float32)], 0
    )
    stem_rows = (
        jnp.stack([tap_terms[1], tap_terms[2] + shifted], 1)
        .reshape(2 * OWN_SEG * SEG, tap_terms.shape[2])
        .astype(jnp.bfloat16)
    )
    shard_sum = lax.psum_scatter(
        lax.dot_general(
            normed_bf, cotangent, (((0,), (0,)), ((), ())), preferred_element_type=jnp.float32
        ),
        "fsdp",
        scatter_dimension=0,
        tiled=True,
    )
    shard_sum = lax.psum(shard_sum, "site")
    weight_grad = shard_sum / math.sqrt(lax.axis_size("site") * group_size * ROWS)
    return (stem_rows[None], weight_grad)


def solution(mesh):
    placed = (
        P("site", "fsdp", None),
        P("site", "fsdp", None),
        P("fsdp", None),
        P(None, "fsdp", None),
        P("site", None),
    )
    fits = (mesh.shape["site"], mesh.shape["fsdp"]) == (N_SITE, N_FSDP)
    return jax.shard_map(
        body if fits else plain_body,
        mesh=mesh,
        in_specs=placed,
        out_specs=(P("site", "fsdp", None), P("fsdp", None)),
        check_vma=False,
    )
```

```python
import math

import jax
import jax.numpy as jnp
from jax import lax
from jax.experimental import pallas as pl
from jax.experimental.pallas import tpu as pltpu
from jax.sharding import PartitionSpec as P

D = 1536
SEG = 8
HOLD = 64
OWN_SEG = 128
N_SITE = 4
N_FSDP = 8
N_Z = N_FSDP // 2
QUARTER = D // N_SITE
CAP = OWN_SEG // N_FSDP
CS = 512
ROWS = HOLD * SEG
BLOCK = 256
LANES = 128
COLUMNS = 512
PAYLOAD_ORDER = (0, 4, 5, 2, 3, 6, 7, 1)
MIB = 1024 * 1024

EPSILON = 1e-05
F32 = jnp.float32
BF16 = jnp.bfloat16


def swap_core(value):
    return lax.ppermute(value, "fsdp", [(i, i ^ 1) for i in range(N_FSDP)])


def swap_z(value, distance):
    return lax.ppermute(value, "fsdp", [(i, i ^ (2 * distance)) for i in range(N_FSDP)])


def swap_site(value, distance):
    return lax.ppermute(value, "site", [(i, i ^ distance) for i in range(N_SITE)])


def hold(value, *first):
    return pl.pallas_call(
        lambda *refs: None,
        name="hold",
        out_shape=shape(value.shape, value.dtype),
        in_specs=[HBM] + [ANY] * len(first),
        out_specs=HBM,
        input_output_aliases={0: 0},
        cost_estimate=pl.CostEstimate(flops=0, bytes_accessed=0, transcendentals=0),
    )(value, *first)


Z_ORDER = (2, 1, 3)
HALF = D // N_FSDP // 2
STEM_ROWS = CS // N_FSDP
TAPS = 3


def half_places(site, low):
    return [(0, z, ("xor", site), low, HALF) for z in Z_ORDER]


SPLIT = STEM_ROWS // 2
QUARTER_BLOCKS = ((1, 0, STEM_ROWS), (0, 0, SPLIT))
WHOLE_BLOCKS = ((2, 0, STEM_ROWS), (0, SPLIT, STEM_ROWS - SPLIT))
QUARTER_ROWS = sum(count for _, _, count in QUARTER_BLOCKS)
UNIT_ROWS = QUARTER_ROWS + N_SITE * sum(count for _, _, count in WHOLE_BLOCKS)


def unit_places(site):
    return [(tap, z, ("xor", site), low, count) for z in Z_ORDER for tap, low, count in QUARTER_BLOCKS]


def all_places():
    blocks = [(tap, ("xor", 0), low, count) for tap, low, count in QUARTER_BLOCKS]
    blocks += [(tap, ("abs", j), low, count) for tap, low, count in WHOLE_BLOCKS for j in range(N_SITE)]
    return [(tap, z, kind, low, count) for z in Z_ORDER for tap, kind, low, count in blocks]


def shard_places(tap, count):
    return [(tap, 0, ("abs", j), 0, count) for j in range(N_SITE)]


def rows_of(value):
    return value.reshape(-1, QUARTER)


def call(kernel, name, out_shape, grid, in_specs, out_specs, scratch, vmem=16):
    return pl.pallas_call(
        kernel,
        name=name,
        out_shape=out_shape,
        grid_spec=pltpu.PrefetchScalarGridSpec(
            num_scalar_prefetch=1,
            grid=grid,
            in_specs=in_specs,
            out_specs=out_specs,
            scratch_shapes=scratch,
        ),
        compiler_params=pltpu.CompilerParams(
            dimension_semantics=("arbitrary",) * len(grid), vmem_limit_bytes=vmem * MIB
        ),
        cost_estimate=pl.CostEstimate(flops=0, bytes_accessed=0, transcendentals=0),
    )


ANY = pl.BlockSpec(memory_space=pl.ANY)
HBM = pl.BlockSpec(memory_space=pltpu.HBM)


def whole(shape):
    return pl.BlockSpec(shape, lambda i, scalars: (0,) * len(shape))


def row_block(rows, columns):
    return pl.BlockSpec((rows, columns), lambda i, scalars: (i, 0))


def shape(dims, dtype):
    return jax.ShapeDtypeStruct(dims, dtype)


def dot_nt(a, b):
    return lax.dot_general(a, b, (((1,), (1,)), ((), ())), preferred_element_type=F32)


def join(kernel, name, out_dims, values, first=(), wide_dims=(), aliases=None):
    n = len(values)

    def wrapped(*refs):
        kernel(*refs[:n], *refs[n + len(first) :])

    out = tuple(shape(dims, BF16) for dims in out_dims) + tuple(shape(dims, F32) for dims in wide_dims)
    vmem = pl.BlockSpec(memory_space=pltpu.VMEM)
    return pl.pallas_call(
        wrapped,
        name=name,
        out_shape=out,
        in_specs=[vmem] * n + [ANY] * len(first),
        out_specs=(vmem,) * len(out),
        input_output_aliases=aliases or {},
        compiler_params=pltpu.CompilerParams(vmem_limit_bytes=14 * MIB),
        cost_estimate=pl.CostEstimate(flops=0, bytes_accessed=0, transcendentals=0),
    )(*values, *first)


def cut_proj_kernel(shard, out):
    at = pl.multiple_of(lax.axis_index("site") * QUARTER, QUARTER)
    out[...] = shard[:, pl.ds(at, QUARTER)]


def halves_kernel(_, __, far, near, farthest, stem, a, b, units):
    for i, piece in enumerate((far, near, farthest)):
        a[i * HALF : (i + 1) * HALF, :] = piece[:HALF, :]
        b[i * HALF : (i + 1) * HALF, :] = piece[HALF:, :]
    at = pl.multiple_of(lax.axis_index("site") * QUARTER, QUARTER)
    pieces = [stem[tap, low : low + count, pl.ds(at, QUARTER)] for tap, low, count in QUARTER_BLOCKS]
    for tap, low, count in WHOLE_BLOCKS:
        pieces += column_pieces(stem[tap, low : low + count, :])
    pack_rows(units, pieces)


def pack_rows(out, pieces):
    at = 0
    for piece in pieces:
        out[at : at + piece.shape[0], :] = piece
        at += piece.shape[0]


def column_pieces(rows):
    return [rows[:, i * QUARTER : (i + 1) * QUARTER] for i in range(N_SITE)]


def site_step_kernel(
    shard, stem, a0, b0, a1, b1, units, far, kept_a, kept_b, a, b, packed, pair, own_a, own_b
):
    pair[0], pair[1] = units[...], far[...]
    n, m = 3 * HALF, D // 4
    for sent, came, kept, out, own in ((a0, a1, kept_a, a, own_a), (b0, b1, kept_b, b, own_b)):
        for j, source in enumerate((sent, came)):
            out[j * n : (j + 1) * n, :] = source[:n, :]
        own[...] = kept[0] + came[n : n + m, :].astype(F32)
        out[2 * n :, :] = (kept[1] + came[n + m :, :].astype(F32)).astype(BF16)
    pieces = column_pieces(shard[...])
    for tap in range(TAPS):
        pieces += column_pieces(stem[tap])
    pack_rows(packed, pieces + [ref[:n, :] for ref in (a0, a1, b0, b1)])


def collect_kernel(a, b, c, out):
    out[0], out[1], out[2] = a[...], b[...], c[...]


def three_kernel(pair, near, a2, b2, quarters, units, packed):
    n = 6 * HALF
    packed[:n, :], packed[n:, :] = a2[:n, :], b2[:n, :]
    for i, piece in enumerate((pair.at[1], near.at[0], near.at[1])):
        quarters[i] = piece[:QUARTER_ROWS, :]
        units[i] = piece[...]


def normalise(inputs):
    inputs = inputs.astype(F32)
    centered = inputs - jnp.mean(inputs, axis=-1, keepdims=True)
    variance = jnp.mean(centered * centered, axis=-1, keepdims=True)
    inverse = lax.rsqrt(variance + EPSILON)
    return centered * inverse, inverse


def norm_kernel(scalars, x_ref, *refs):
    out_ref, turned = refs[-2:]
    core = scalars[1] % 2
    normed, _ = normalise(x_ref[...])
    turned[...] = normed.astype(BF16).T
    shard = D // N_FSDP
    for z in range(N_Z):
        rows = pl.ds(pl.multiple_of((2 * z + core) * shard, shard), shard)
        out_ref[pl.ds(z * shard, shard), :] = turned[rows, :]


def norm_half(scalars, inputs, first=()):
    return call(
        norm_kernel, "norm_half", shape((D // 2, ROWS), BF16), (ROWS // BLOCK,),
        [row_block(BLOCK, D)] + [ANY] * len(first),
        pl.BlockSpec((D // 2, BLOCK), lambda i, scalars: (0, i)), [pltpu.VMEM((D, BLOCK), BF16)],
    )(scalars, inputs, *first)


OUTER_PLACES = (((0, 0), (0, 0)), ((1, 0), (0, 1)), ((0, 1), (1, 0)), ((1, 1), (1, 1)))


def outer_kernel(scalars, na_ref, nb_ref, ca_ref, cb_ref, ka_ref, a_ref, kb_ref, b_ref):
    site = scalars[0]
    n, m = 3 * HALF, D // 4
    for half in range(2):
        start = lax.bitwise_xor(site // 2, half) * 2 * QUARTER
        columns = pl.ds(pl.multiple_of(start, 2 * QUARTER), 2 * QUARTER)
        total = jnp.dot(na_ref[...], ca_ref[:, columns], preferred_element_type=F32)
        total = total + jnp.dot(nb_ref[...], cb_ref[:, columns], preferred_element_type=F32)
        low, high = total[:, :QUARTER], total[:, QUARTER:]
        odd = site % 2 == 1
        for at, value in ((2 * half, jnp.where(odd, high, low)), (2 * half + 1, jnp.where(odd, low, high))):
            for (goes, i), kept, sent, rows in zip(
                OUTER_PLACES[at], (ka_ref, kb_ref), (a_ref, b_ref), (value[:m, :], value[m:, :]), strict=True
            ):
                if goes:
                    sent[n + i * m : n + (i + 1) * m, :] = rows.astype(BF16)
                else:
                    kept[i] = rows


def outer_pieces(scalars, normed_a, normed_b, cotangent_a, cotangent_b):
    kept, sent = (2, D // 4, QUARTER), (3 * HALF + D // 2, QUARTER)
    values = (normed_a, normed_b, cotangent_a, cotangent_b)
    return call(
        outer_kernel, "outer_pieces", (shape(kept, F32), shape(sent, BF16)) * 2, (1,),
        [whole(value.shape) for value in values], (whole(kept), whole(sent)) * 2, [], vmem=24,
    )(scalars, *values)


def site_sum_kernel(scalars, oa_ref, ra_ref, ob_ref, rb_ref, kept_ref, sent_ref, total):
    shard = D // N_FSDP
    z = scalars[1] // 2
    total[: D // 4, :] = oa_ref[...] + ra_ref[6 * HALF :, :].astype(F32)
    total[D // 4 :, :] = ob_ref[...] + rb_ref[6 * HALF :, :].astype(F32)
    for distance, (ref, i) in enumerate(((kept_ref, 0), (sent_ref, 0), (kept_ref, 1), (sent_ref, 1))):
        rows = pl.ds(pl.multiple_of(lax.bitwise_xor(z, distance) * shard, shard), shard)
        ref[i] = total[rows, :].astype(ref.dtype)


def site_sum(scalars, *values):
    out = (2, D // N_FSDP, QUARTER)
    return call(
        site_sum_kernel, "site_sum", (shape(out, F32), shape(out, BF16)), (1,),
        [whole(value.shape) for value in values], (whole(out),) * 2, [pltpu.VMEM((D // 2, QUARTER), F32)],
    )(scalars, *values)


def near_sum_kernel(scalars, kept_ref, came_ref, *refs):
    own_ref, sent_ref = refs[-2:]
    own_ref[...] = kept_ref[0] + came_ref[0].astype(F32)
    sent_ref[...] = (kept_ref[1] + came_ref[1].astype(F32)).astype(BF16)


def near_sum(scalars, kept, came, first):
    dims, out = (2, D // N_FSDP, QUARTER), (D // N_FSDP, QUARTER)
    return call(
        near_sum_kernel, "near_sum", (shape(out, F32), shape(out, BF16)), (1,),
        [whole(dims)] * 2 + [ANY] * len(first), (whole(out),) * 2, [],
    )(scalars, kept, came, *first)


def far_sum_kernel(scale, scalars, own_ref, came_ref, *refs):
    refs[-1][...] = (own_ref[...] + came_ref[...].astype(F32)) * scale


def far_sum(scalars, own, came, scale, first):
    dims = (D // N_FSDP, QUARTER)
    return call(
        lambda *refs: far_sum_kernel(scale, *refs), "far_sum", shape(dims, F32), (1,),
        [whole(dims)] * 2 + [ANY] * len(first), whole(dims), [],
    )(scalars, own, came, *first)


def weight_copies(tables, scalars, refs, weight, sem):
    site, index = scalars[0], scalars[1]
    shard = weight.shape[1] // N_FSDP
    copies = []
    for (places, swapped), ref in zip(tables, refs, strict=True):
        at = 0
        for place in places:
            if isinstance(place, int):
                at += place
                continue
            tap, z, (kind, quarter), low, count = place
            start = lax.bitwise_xor(index, 2 * z + swapped) * shard + low
            rows = pl.ds(pl.multiple_of(start, math.gcd(shard, low)), count)
            columns = pl.ds(quarter * QUARTER, QUARTER)
            if kind == "all":
                columns = pl.ds(0, D)
            elif kind == "xor":
                column = lax.bitwise_xor(site, quarter) * QUARTER
                columns = pl.ds(pl.multiple_of(column, QUARTER), QUARTER)
            source = ref.at[pl.ds(at, count), :]
            copies.append(pltpu.make_async_copy(source, weight.at[tap, rows, columns], sem))
            at += count
        assert at == ref.shape[0]
    return copies


def fetch(source, target, sem):
    copy = pltpu.make_async_copy(source, target, sem)
    copy.start()
    return copy


def input_grad_kernel(tables, scalars, *refs):
    n = len(tables)
    parts, (x_hbm, cot_hbm, out_ref) = refs[:n], refs[n : n + 3]
    x_ref, cot_ref, weight, normed, inverse, back, sems, sem = refs[n + 3 :]
    x_copy = fetch(x_hbm, x_ref, sems.at[0])
    cot_copy = fetch(cot_hbm, cot_ref, sems.at[1])
    copies = weight_copies(tables, scalars, parts, weight, sem)
    for copy in copies:
        copy.start()
    x_copy.wait()

    @pl.loop(0, ROWS // BLOCK)
    def _(i):
        rows = pl.ds(pl.multiple_of(i * BLOCK, BLOCK), BLOCK)
        normed[rows, :], inverse[rows, :] = normalise(x_ref[rows, :])

    cot_copy.wait()
    for copy in copies:
        copy.wait()

    def finish(rows):
        term, row_normed = back[rows, :], normed[rows, :]
        inner = term - jnp.mean(term, axis=-1, keepdims=True)
        inner = inner - row_normed * jnp.mean(term * row_normed, axis=-1, keepdims=True)
        out_ref[rows, :] = (cot_ref[rows, :].astype(F32) + inverse[rows, :] * inner).astype(BF16)

    half = ROWS // 2
    for i in range(3):
        if i < 2:
            rows = slice(i * half, (i + 1) * half)
            for j in range(D // COLUMNS):
                columns = slice(j * COLUMNS, (j + 1) * COLUMNS)
                back[rows, columns] = dot_nt(cot_ref[rows, :], weight[0, columns, :])
        if i > 0:
            for j in range(4):
                start = (i - 1) * half + j * half // 4
                finish(slice(start, start + half // 4))


def split_parts(parts):
    return [(places, swapped) for _, places, swapped in parts], [value for value, _, _ in parts]


def input_gradient(scalars, parts, inputs, cotangent):
    tables, values = split_parts(parts)
    return call(
        lambda *refs: input_grad_kernel(tables, *refs), "input_gradient", shape((ROWS, D), BF16),
        (1,), [HBM] * (len(values) + 2), whole((ROWS, D)),
        [
            pltpu.VMEM((ROWS, D), BF16),
            pltpu.VMEM((ROWS, D), BF16),
            pltpu.VMEM((1, D, D), BF16),
            pltpu.VMEM((ROWS, D), F32),
            pltpu.VMEM((ROWS, 1), F32),
            pltpu.VMEM((ROWS, D), F32),
            pltpu.SemaphoreType.DMA((2,)),
            pltpu.SemaphoreType.DMA,
        ],
        vmem=22,
    )(scalars, *values, inputs, cotangent)


def held_before(start, holder):
    return 2 * (start // (2 * N_FSDP)) + jnp.clip(start % (2 * N_FSDP) - 2 * holder, 0, 2)


SLOTS_AT = 2
SEGMENTS_AT = SLOTS_AT + HOLD
COUNT_AT = SEGMENTS_AT + OWN_SEG


def plan_kernel(scalars, plan):
    site, index = scalars[0], scalars[1]
    plan[0], plan[1] = site, index
    starts = [jnp.int32(0)]
    for owner in range(N_FSDP):
        starts.append(starts[-1] + scalars[2 + owner])

    @pl.loop(0, HOLD)
    def _(slot):
        item = 2 * (slot // 2 * N_FSDP + index) + slot % 2
        owner = jnp.int32(0)
        start = jnp.int32(0)
        for other in range(1, N_FSDP):
            passed = item >= starts[other]
            owner = jnp.where(passed, other, owner)
            start = jnp.where(passed, starts[other], start)
        plan[SLOTS_AT + slot] = lax.bitwise_xor(owner, index) * CAP + slot - held_before(start, index)

    start = jnp.int32(0)
    for owner in range(N_FSDP):
        start = start + jnp.where(owner < index, scalars[2 + owner], 0)
    count = scalars[2 + index]
    plan[COUNT_AT] = count

    @pl.loop(0, OWN_SEG)
    def _(segment):
        item = start + jnp.minimum(segment, count - 1)
        holder = item // 2 % N_FSDP
        rank = 2 * (item // (2 * N_FSDP)) + item % 2 - held_before(start, holder)
        plan[SEGMENTS_AT + segment] = lax.bitwise_xor(holder, index) * CAP + rank


def plan_of(scalars):
    return call(
        plan_kernel, "plan", shape((COUNT_AT + 1,), jnp.int32), (1,), [],
        pl.BlockSpec(memory_space=pltpu.SMEM), [],
    )(scalars)


def stem_kernel(tables, scalars, *refs):
    n = len(tables)
    parts, grad_ref, outs = refs[:n], refs[n], refs[n + 1 : n + 1 + N_FSDP]
    weight, mixed, leading, packed, firsts, sem, out_sem = refs[n + 1 + N_FSDP :]
    copies = weight_copies(tables, scalars, parts, weight, sem)
    for copy in copies:
        copy.start()
    for copy in copies:
        copy.wait()
    index = scalars[1]
    for lane in range(0, CS, CS // 2):
        span = pl.ds(lane, CS // 2)
        even = dot_nt(grad_ref[...], weight[1, span, :])
        first = dot_nt(grad_ref[...], weight[0, span, :])
        leading[:, span] = first
        row = lax.broadcasted_iota(jnp.int32, first.shape, 0)
        following = jnp.where(row % SEG == SEG - 1, 0.0, pltpu.roll(first, ROWS - 1, 0))
        odd = dot_nt(grad_ref[...], weight[2, span, :]) + following
        for part in range(CS // 2 // LANES):
            at = lane // LANES + part
            columns = slice(part * LANES, (part + 1) * LANES)
            mixed[at, pl.ds(0, ROWS, stride=2), :] = even[:, columns]
            mixed[at, pl.ds(1, ROWS, stride=2), :] = odd[:, columns]

    @pl.loop(0, HOLD, unroll=8)
    def _(slot):
        block = scalars[SLOTS_AT + slot]
        place, rank = block // CAP, block % CAP
        rows = pl.ds(pl.multiple_of(slot * 2 * SEG, 2 * SEG), 2 * SEG)
        for lane in range(CS // LANES):
            packed[place, rank, :, pl.ds(lane * LANES, LANES)] = mixed[lane, rows, :].astype(BF16)
        firsts[pl.ds(block, 1), :] = leading[pl.ds(slot * SEG, 1), :]

    packed[:, CAP] = firsts[...].reshape(N_FSDP, CAP, CS).astype(BF16)
    copies = [
        pltpu.make_async_copy(packed.at[place], outs[place], out_sem.at[place])
        for place in range(N_FSDP)
    ]
    for copy in copies:
        copy.start()
    for copy in copies:
        copy.wait()


def stem_payloads(scalars, parts, grad):
    tables, values = split_parts(parts)
    payload = (CAP + 1, 2 * SEG, CS)
    return call(
        lambda *refs: stem_kernel(tables, *refs), "stem_payloads",
        (shape(payload, BF16),) * N_FSDP, (1,),
        [ANY] * len(values) + [whole((ROWS, D))], (HBM,) * N_FSDP,
        [
            pltpu.VMEM((3, CS, D), BF16),
            pltpu.VMEM((CS // LANES, 2 * ROWS, LANES), F32),
            pltpu.VMEM((ROWS, CS), F32),
            pltpu.VMEM((N_FSDP,) + payload, BF16),
            pltpu.VMEM((N_FSDP * CAP, CS), F32),
            pltpu.SemaphoreType.DMA,
            pltpu.SemaphoreType.DMA((N_FSDP,)),
        ],
        vmem=18,
    )(scalars, *values, grad)


def owner_kernel(scalars, *refs):
    payloads, terms, (out_ref, total), (packed, firsts, sem, total_sem) = (
        refs[:N_FSDP], refs[N_FSDP : N_FSDP + N_SITE], refs[-6:-4], refs[-4:]
    )
    step = pl.program_id(0)
    total_copies = []
    for distance, term in enumerate(terms):
        at = pl.multiple_of(lax.bitwise_xor(scalars[0], distance) * QUARTER, QUARTER)
        total_copies.append(
            pltpu.make_async_copy(term, total.at[:, pl.ds(at, QUARTER)], total_sem.at[distance])
        )

    @pl.when(step == 0)
    def _():
        for copy in total_copies:
            copy.start()

    @pl.when(step == 0)
    def _():
        copies = [
            pltpu.make_async_copy(payloads[i], packed.at[place], sem.at[place])
            for i, place in enumerate(PAYLOAD_ORDER)
        ]
        for copy in copies:
            copy.start()
        for copy in copies:
            copy.wait()
        firsts[...] = packed[:, CAP].astype(F32).reshape(N_FSDP * CAP, CS)

    count = scalars[COUNT_AT]
    per_step = OWN_SEG // 4
    last_row = lax.broadcasted_iota(jnp.int32, (2 * SEG, CS), 0) == 2 * SEG - 1

    @pl.loop(0, per_step, unroll=4)
    def _(local):
        segment = step * per_step + local
        block = scalars[SEGMENTS_AT + segment]
        follower = scalars[SEGMENTS_AT + jnp.minimum(segment + 1, OWN_SEG - 1)]
        first = jnp.broadcast_to(firsts[pl.ds(follower, 1), :], (2 * SEG, CS))
        first = jnp.where(last_row & (segment + 1 < count), first, 0.0)
        rows = packed[block // CAP, block % CAP].astype(F32) + first
        to = pl.ds(pl.multiple_of(local * 2 * SEG, 2 * SEG), 2 * SEG)
        out_ref[to, :] = jnp.where(segment < count, rows, 0.0).astype(BF16)

    @pl.when(step == pl.num_programs(0) - 1)
    def _():
        for copy in total_copies:
            copy.wait()


def owner_rows(scalars, payloads, terms):
    payload = (CAP + 1, 2 * SEG, CS)
    rows = 2 * OWN_SEG * SEG
    return call(
        owner_kernel, "owner_rows", (shape((rows, CS), BF16), shape((D // N_FSDP, D), F32)), (4,),
        [ANY] * (N_FSDP + N_SITE), (row_block(rows // 4, CS), HBM),
        [
            pltpu.VMEM((N_FSDP,) + payload, BF16),
            pltpu.VMEM((N_FSDP * CAP, CS), F32),
            pltpu.SemaphoreType.DMA((N_FSDP,)),
            pltpu.SemaphoreType.DMA((N_SITE,)),
        ],
    )(scalars, *payloads, *terms)


def body(held_input, held_cotangent, proj_weight, stem_weight, seg_counts):
    site, index = lax.axis_index("site"), lax.axis_index("fsdp")
    scalars = jnp.concatenate([jnp.stack([site, index]).astype(jnp.int32), seg_counts[0]])
    inputs, cotangent = held_input[0], held_cotangent[0]

    plan = plan_of(scalars)
    piece = (D // N_FSDP, QUARTER)
    half = (3, HALF, QUARTER)
    units = (UNIT_ROWS, QUARTER)
    quarters = (QUARTER_ROWS, QUARTER)

    (proj_quarter,) = join(cut_proj_kernel, "cut_proj", [piece], [proj_weight])
    around = [swap_z(proj_quarter, distance) for distance in Z_ORDER]
    normed_own = norm_half(scalars, inputs, [proj_quarter])
    normed_theirs = norm_half(scalars, swap_core(inputs), [normed_own])
    kept_a, sent_a, kept_b, sent_b = outer_pieces(
        scalars, normed_own, normed_theirs, cotangent, swap_core(cotangent)
    )
    n, m = 3 * HALF, D // 4
    a0, b0, stem_units = join(
        halves_kernel, "halves", [(n + 2 * m, QUARTER)] * 2 + [units],
        [sent_a, sent_b, *around, stem_weight], aliases={0: 0, 1: 1},
    )

    a, b, packed, stem_pair, own_a, own_b = join(
        site_step_kernel, "site_step", [(2 * n + m, QUARTER)] * 2 + [(D + 4 * n, QUARTER), (2, *units)],
        [
            proj_weight, stem_weight, a0, b0, swap_site(a0, 1), swap_site(b0, 2),
            stem_units, swap_z(stem_units, 2), kept_a, kept_b,
        ],
        [plan],
        wide_dims=[(m, QUARTER)] * 2,
    )

    a2, b2 = swap_site(a, 2), swap_site(b, 1)
    near = swap_z(stem_pair, 1)
    packed = swap_core(packed)
    kept, sent = site_sum(scalars, own_a, a2, own_b, b2)
    others, all_others, late = join(
        three_kernel, "three", [(3, *quarters), (3, *units), (4 * n, QUARTER)],
        [stem_pair, near, a2, b2], [kept, packed],
    )

    over = [swap_site(others, distance) for distance in (1, 2, 3)]
    late, late_stem = swap_core(late), swap_core(rows_of(all_others))
    whole_proj = [(0, 0, ("all", 0), 0, D // N_FSDP)]
    first = [half_places(0, 0) + half_places(1, 0), half_places(0, HALF) + half_places(2, HALF)]
    last = [half_places(2, 0) + half_places(3, 0), half_places(1, HALF) + half_places(3, HALF)]
    proj_parts = [
        (proj_weight, whole_proj, 0),
        (a, first[0] + [m], 0), (b, first[1] + [m], 0),
        (a2, last[0] + [m], 0), (b2, last[1] + [m], 0),
        (packed, shard_places(0, D // N_FSDP) + [D // 2] + sum(first, []), 1), (late, sum(last, []), 1),
    ]
    grad = input_gradient(scalars, proj_parts, inputs, cotangent)
    own, sent = near_sum(scalars, kept, swap_z(sent, 1), [grad])
    (over,) = join(collect_kernel, "collect", [(3, 3, *quarters)], over, [grad, sent, late_stem])
    over = rows_of(over)
    last = sum((unit_places(d) for d in (1, 2, 3)), [])
    whole_stem = [(tap, 0, ("all", 0), 0, STEM_ROWS) for tap in range(TAPS)]
    stem_parts = [
        (stem_weight.reshape(-1, D), whole_stem, 0),
        (
            packed,
            [D // 2] + sum((shard_places(tap, STEM_ROWS) for tap in range(TAPS)), []) + [4 * n], 1,
        ),
        (rows_of(all_others), all_places(), 0), (over, last, 0),
        (late_stem, all_places(), 1), (swap_core(over), last, 1),
    ]

    payloads = stem_payloads(plan, stem_parts, grad)
    received = {0: payloads[0]}
    for d in PAYLOAD_ORDER[1:]:
        received[d] = lax.ppermute(payloads[d], "fsdp", [(i, i ^ d) for i in range(N_FSDP)])
    scale = 1.0 / math.sqrt(N_SITE * N_FSDP * ROWS)
    terms = far_sum(scalars, own, swap_z(sent, 2), scale, [received[4]])
    terms = [terms] + [swap_site(terms, d) for d in (1, 2, 3)]
    stem_grad, weight_grad = owner_rows(plan, [received[d] for d in PAYLOAD_ORDER], terms)
    return (stem_grad[None], weight_grad)


def plain_body(held_input, held_cotangent, proj_weight, stem_weight, seg_counts):
    group_size = lax.axis_size("fsdp")
    capacity = 2 * ((OWN_SEG + 2 * group_size - 1) // (2 * group_size))
    my_index = lax.axis_index("fsdp")
    cotangent = held_cotangent[0]
    normed, inverse = normalise(held_input[0])
    normed_bf = normed.astype(jnp.bfloat16)
    proj_back = dot_nt(cotangent, lax.all_gather(proj_weight, "fsdp", axis=0, tiled=True))
    input_grad = cotangent.astype(jnp.float32) + inverse * (
        proj_back
        - jnp.mean(proj_back, axis=-1, keepdims=True)
        - normed * jnp.mean(proj_back * normed, axis=-1, keepdims=True)
    )
    input_grad = input_grad.astype(jnp.bfloat16)
    counts = seg_counts[0]
    endings = jnp.cumsum(counts)
    starts = endings - counts
    slot_ids = jnp.arange(HOLD, dtype=jnp.int32)
    item_index = 2 * (slot_ids // 2 * group_size + my_index) + slot_ids % 2
    owner_ids = jnp.sum((item_index[:, None] >= endings[None, :]).astype(jnp.int32), axis=1)
    earlier = (slot_ids[None, :] < slot_ids[:, None]) & (owner_ids[None, :] == owner_ids[:, None])
    rank_ids = jnp.sum(earlier.astype(jnp.int32), axis=1)
    target = owner_ids * capacity + rank_ids
    positions = jnp.arange(group_size * capacity, dtype=jnp.int32)
    matched = target[None, :] == positions[:, None]
    filled = jnp.any(matched, axis=1)
    source = jnp.sum(jnp.where(matched, slot_ids[None, :], 0), axis=1)
    owner_hit = jnp.arange(group_size, dtype=jnp.int32) == my_index
    my_count = jnp.sum(jnp.where(owner_hit, counts, 0))
    my_start = jnp.sum(jnp.where(owner_hit, starts, 0))
    segment = jnp.arange(OWN_SEG, dtype=jnp.int32)
    is_live = segment < my_count
    holder = (my_start + segment) // 2 % group_size
    before = (
        (segment[None, :] < segment[:, None])
        & (holder[None, :] == holder[:, None])
        & is_live[None, :]
    )
    holder_rank = jnp.sum(before.astype(jnp.int32), axis=1)
    row_index = jnp.where(is_live, holder * capacity + holder_rank, 0)
    held_segments = input_grad.reshape(HOLD, SEG, D)
    zero_bf = jnp.zeros((), jnp.bfloat16)
    send_rows = jnp.where(filled[:, None, None], jnp.take(held_segments, source, axis=0), zero_bf)
    received = lax.all_to_all(
        send_rows.reshape(group_size, capacity, SEG, D), "fsdp", split_axis=0, concat_axis=0, tiled=True
    )
    picked = jnp.take(received.reshape(group_size * capacity, SEG, D), row_index, axis=0)
    frames = jnp.where(is_live[:, None, None], picked, zero_bf).reshape(OWN_SEG * SEG, D)
    tap_terms = jnp.einsum(
        "rd,kcd->krc",
        frames,
        lax.all_gather(stem_weight, "fsdp", axis=1, tiled=True),
        preferred_element_type=jnp.float32,
    )
    shifted = jnp.concatenate(
        [tap_terms[0][1:], jnp.zeros((1, tap_terms.shape[2]), jnp.float32)], 0
    )
    stem_rows = (
        jnp.stack([tap_terms[1], tap_terms[2] + shifted], 1)
        .reshape(2 * OWN_SEG * SEG, tap_terms.shape[2])
        .astype(jnp.bfloat16)
    )
    shard_sum = lax.psum_scatter(
        lax.dot_general(
            normed_bf, cotangent, (((0,), (0,)), ((), ())), preferred_element_type=jnp.float32
        ),
        "fsdp",
        scatter_dimension=0,
        tiled=True,
    )
    shard_sum = lax.psum(shard_sum, "site")
    weight_grad = shard_sum / math.sqrt(lax.axis_size("site") * group_size * ROWS)
    return (stem_rows[None], weight_grad)


def solution(mesh):
    placed = (
        P("site", "fsdp", None),
        P("site", "fsdp", None),
        P("fsdp", None),
        P(None, "fsdp", None),
        P("site", None),
    )
    fits = (mesh.shape["site"], mesh.shape["fsdp"]) == (N_SITE, N_FSDP)
    return jax.shard_map(
        body if fits else plain_body,
        mesh=mesh,
        in_specs=placed,
        out_specs=(P("site", "fsdp", None), P("fsdp", None)),
        check_vma=False,
    )
```

```python
import math

import jax
import jax.numpy as jnp
from jax import lax
from jax.experimental import pallas as pl
from jax.experimental.pallas import tpu as pltpu
from jax.sharding import PartitionSpec as P

D = 1536
SEG = 8
HOLD = 64
OWN_SEG = 128
N_SITE = 4
N_FSDP = 8
N_Z = N_FSDP // 2
QUARTER = D // N_SITE
CAP = OWN_SEG // N_FSDP
CS = 512
ROWS = HOLD * SEG
BLOCK = 256
LANES = 128
COLUMNS = 512
PAYLOAD_ORDER = (0, 4, 5, 2, 3, 6, 7, 1)
MIB = 1024 * 1024

EPSILON = 1e-05
F32 = jnp.float32
BF16 = jnp.bfloat16


def swap_core(value):
    return lax.ppermute(value, "fsdp", [(i, i ^ 1) for i in range(N_FSDP)])


def swap_z(value, distance):
    return lax.ppermute(value, "fsdp", [(i, i ^ (2 * distance)) for i in range(N_FSDP)])


def swap_site(value, distance):
    return lax.ppermute(value, "site", [(i, i ^ distance) for i in range(N_SITE)])


def hold(value, *first):
    return pl.pallas_call(
        lambda *refs: None,
        name="hold",
        out_shape=shape(value.shape, value.dtype),
        in_specs=[HBM] + [ANY] * len(first),
        out_specs=HBM,
        input_output_aliases={0: 0},
        cost_estimate=pl.CostEstimate(flops=0, bytes_accessed=0, transcendentals=0),
    )(value, *first)


Z_ORDER = (2, 1, 3)
HALF = D // N_FSDP // 2
STEM_ROWS = CS // N_FSDP
TAPS = 3


def half_places(site, low):
    return [(0, z, ("xor", site), low, HALF) for z in Z_ORDER]


SPLIT = STEM_ROWS // 2
QUARTER_BLOCKS = ((1, 0, STEM_ROWS), (0, 0, SPLIT))
WHOLE_BLOCKS = ((2, 0, STEM_ROWS), (0, SPLIT, STEM_ROWS - SPLIT))
QUARTER_ROWS = sum(count for _, _, count in QUARTER_BLOCKS)
UNIT_ROWS = QUARTER_ROWS + N_SITE * sum(count for _, _, count in WHOLE_BLOCKS)


def unit_places(site):
    return [(tap, z, ("xor", site), low, count) for z in Z_ORDER for tap, low, count in QUARTER_BLOCKS]


def all_places():
    blocks = [(tap, ("xor", 0), low, count) for tap, low, count in QUARTER_BLOCKS]
    blocks += [(tap, ("abs", j), low, count) for tap, low, count in WHOLE_BLOCKS for j in range(N_SITE)]
    return [(tap, z, kind, low, count) for z in Z_ORDER for tap, kind, low, count in blocks]


def shard_places(tap, count):
    return [(tap, 0, ("abs", j), 0, count) for j in range(N_SITE)]


def rows_of(value):
    return value.reshape(-1, QUARTER)


def call(kernel, name, out_shape, grid, in_specs, out_specs, scratch, vmem=16):
    return pl.pallas_call(
        kernel,
        name=name,
        out_shape=out_shape,
        grid_spec=pltpu.PrefetchScalarGridSpec(
            num_scalar_prefetch=1,
            grid=grid,
            in_specs=in_specs,
            out_specs=out_specs,
            scratch_shapes=scratch,
        ),
        compiler_params=pltpu.CompilerParams(
            dimension_semantics=("arbitrary",) * len(grid), vmem_limit_bytes=vmem * MIB
        ),
        cost_estimate=pl.CostEstimate(flops=0, bytes_accessed=0, transcendentals=0),
    )


ANY = pl.BlockSpec(memory_space=pl.ANY)
HBM = pl.BlockSpec(memory_space=pltpu.HBM)


def whole(shape):
    return pl.BlockSpec(shape, lambda i, scalars: (0,) * len(shape))


def row_block(rows, columns):
    return pl.BlockSpec((rows, columns), lambda i, scalars: (i, 0))


def shape(dims, dtype):
    return jax.ShapeDtypeStruct(dims, dtype)


def dot_nt(a, b):
    return lax.dot_general(a, b, (((1,), (1,)), ((), ())), preferred_element_type=F32)


def join(kernel, name, out_dims, values, first=(), wide_dims=(), aliases=None):
    n = len(values)

    def wrapped(*refs):
        kernel(*refs[:n], *refs[n + len(first) :])

    out = tuple(shape(dims, BF16) for dims in out_dims) + tuple(shape(dims, F32) for dims in wide_dims)
    vmem = pl.BlockSpec(memory_space=pltpu.VMEM)
    return pl.pallas_call(
        wrapped,
        name=name,
        out_shape=out,
        in_specs=[vmem] * n + [ANY] * len(first),
        out_specs=(vmem,) * len(out),
        input_output_aliases=aliases or {},
        compiler_params=pltpu.CompilerParams(vmem_limit_bytes=14 * MIB),
        cost_estimate=pl.CostEstimate(flops=0, bytes_accessed=0, transcendentals=0),
    )(*values, *first)


def cut_proj_kernel(shard, out):
    at = pl.multiple_of(lax.axis_index("site") * QUARTER, QUARTER)
    out[...] = shard[:, pl.ds(at, QUARTER)]


def halves_kernel(_, __, far, near, farthest, stem, a, b, units):
    for i, piece in enumerate((far, near, farthest)):
        a[i * HALF : (i + 1) * HALF, :] = piece[:HALF, :]
        b[i * HALF : (i + 1) * HALF, :] = piece[HALF:, :]
    at = pl.multiple_of(lax.axis_index("site") * QUARTER, QUARTER)
    pieces = [stem[tap, low : low + count, pl.ds(at, QUARTER)] for tap, low, count in QUARTER_BLOCKS]
    for tap, low, count in WHOLE_BLOCKS:
        pieces += column_pieces(stem[tap, low : low + count, :])
    pack_rows(units, pieces)


def pack_rows(out, pieces):
    at = 0
    for piece in pieces:
        out[at : at + piece.shape[0], :] = piece
        at += piece.shape[0]


def column_pieces(rows):
    return [rows[:, i * QUARTER : (i + 1) * QUARTER] for i in range(N_SITE)]


def site_step_kernel(
    shard, stem, a0, b0, a1, b1, units, far, kept_a, kept_b, a, b, packed, pair, own_a, own_b
):
    pair[0], pair[1] = units[...], far[...]
    n, m = 3 * HALF, D // 4
    for sent, came, kept, out, own in ((a0, a1, kept_a, a, own_a), (b0, b1, kept_b, b, own_b)):
        for j, source in enumerate((sent, came)):
            out[j * n : (j + 1) * n, :] = source[:n, :]
        own[...] = kept[0] + came[n : n + m, :].astype(F32)
        out[2 * n :, :] = (kept[1] + came[n + m :, :].astype(F32)).astype(BF16)
    pieces = column_pieces(shard[...])
    for tap in range(TAPS):
        pieces += column_pieces(stem[tap])
    pack_rows(packed, pieces + [ref[:n, :] for ref in (a0, a1, b0, b1)])


def collect_kernel(a, b, c, out):
    out[0], out[1], out[2] = a[...], b[...], c[...]


def three_kernel(pair, near, a2, b2, quarters, units, packed):
    n = 6 * HALF
    packed[:n, :], packed[n:, :] = a2[:n, :], b2[:n, :]
    for i, piece in enumerate((pair.at[1], near.at[0], near.at[1])):
        quarters[i] = piece[:QUARTER_ROWS, :]
        units[i] = piece[...]


def normalise(inputs):
    inputs = inputs.astype(F32)
    centered = inputs - jnp.mean(inputs, axis=-1, keepdims=True)
    variance = jnp.mean(centered * centered, axis=-1, keepdims=True)
    inverse = lax.rsqrt(variance + EPSILON)
    return centered * inverse, inverse


def norm_kernel(scalars, x_ref, *refs):
    out_ref, turned = refs[-2:]
    core = scalars[1] % 2
    normed, _ = normalise(x_ref[...])
    turned[...] = normed.astype(BF16).T
    shard = D // N_FSDP
    for z in range(N_Z):
        rows = pl.ds(pl.multiple_of((2 * z + core) * shard, shard), shard)
        out_ref[pl.ds(z * shard, shard), :] = turned[rows, :]


def norm_half(scalars, inputs, first=()):
    return call(
        norm_kernel, "norm_half", shape((D // 2, ROWS), BF16), (ROWS // BLOCK,),
        [row_block(BLOCK, D)] + [ANY] * len(first),
        pl.BlockSpec((D // 2, BLOCK), lambda i, scalars: (0, i)), [pltpu.VMEM((D, BLOCK), BF16)],
    )(scalars, inputs, *first)


OUTER_PLACES = (((0, 0), (0, 0)), ((1, 0), (0, 1)), ((0, 1), (1, 0)), ((1, 1), (1, 1)))


def outer_kernel(scalars, na_ref, nb_ref, ca_ref, cb_ref, ka_ref, a_ref, kb_ref, b_ref):
    site = scalars[0]
    n, m = 3 * HALF, D // 4
    for half in range(2):
        start = lax.bitwise_xor(site // 2, half) * 2 * QUARTER
        columns = pl.ds(pl.multiple_of(start, 2 * QUARTER), 2 * QUARTER)
        total = jnp.dot(na_ref[...], ca_ref[:, columns], preferred_element_type=F32)
        total = total + jnp.dot(nb_ref[...], cb_ref[:, columns], preferred_element_type=F32)
        low, high = total[:, :QUARTER], total[:, QUARTER:]
        odd = site % 2 == 1
        for at, value in ((2 * half, jnp.where(odd, high, low)), (2 * half + 1, jnp.where(odd, low, high))):
            for (goes, i), kept, sent, rows in zip(
                OUTER_PLACES[at], (ka_ref, kb_ref), (a_ref, b_ref), (value[:m, :], value[m:, :]), strict=True
            ):
                if goes:
                    sent[n + i * m : n + (i + 1) * m, :] = rows.astype(BF16)
                else:
                    kept[i] = rows


def outer_pieces(scalars, normed_a, normed_b, cotangent_a, cotangent_b):
    kept, sent = (2, D // 4, QUARTER), (3 * HALF + D // 2, QUARTER)
    values = (normed_a, normed_b, cotangent_a, cotangent_b)
    return call(
        outer_kernel, "outer_pieces", (shape(kept, F32), shape(sent, BF16)) * 2, (1,),
        [whole(value.shape) for value in values], (whole(kept), whole(sent)) * 2, [], vmem=24,
    )(scalars, *values)


def site_sum_kernel(scalars, oa_ref, ra_ref, ob_ref, rb_ref, kept_ref, sent_ref, total):
    shard = D // N_FSDP
    z = scalars[1] // 2
    total[: D // 4, :] = oa_ref[...] + ra_ref[6 * HALF :, :].astype(F32)
    total[D // 4 :, :] = ob_ref[...] + rb_ref[6 * HALF :, :].astype(F32)
    for distance, (ref, i) in enumerate(((kept_ref, 0), (sent_ref, 0), (kept_ref, 1), (sent_ref, 1))):
        rows = pl.ds(pl.multiple_of(lax.bitwise_xor(z, distance) * shard, shard), shard)
        ref[i] = total[rows, :].astype(ref.dtype)


def site_sum(scalars, *values):
    out = (2, D // N_FSDP, QUARTER)
    return call(
        site_sum_kernel, "site_sum", (shape(out, F32), shape(out, BF16)), (1,),
        [whole(value.shape) for value in values], (whole(out),) * 2, [pltpu.VMEM((D // 2, QUARTER), F32)],
    )(scalars, *values)


def near_sum_kernel(scalars, kept_ref, came_ref, *refs):
    own_ref, sent_ref = refs[-2:]
    own_ref[...] = kept_ref[0] + came_ref[0].astype(F32)
    sent_ref[...] = (kept_ref[1] + came_ref[1].astype(F32)).astype(BF16)


def near_sum(scalars, kept, came, first):
    dims, out = (2, D // N_FSDP, QUARTER), (D // N_FSDP, QUARTER)
    return call(
        near_sum_kernel, "near_sum", (shape(out, F32), shape(out, BF16)), (1,),
        [whole(dims)] * 2 + [ANY] * len(first), (whole(out),) * 2, [],
    )(scalars, kept, came, *first)


def far_sum_kernel(scale, scalars, own_ref, came_ref, *refs):
    refs[-1][...] = (own_ref[...] + came_ref[...].astype(F32)) * scale


def far_sum(scalars, own, came, scale, first):
    dims = (D // N_FSDP, QUARTER)
    return call(
        lambda *refs: far_sum_kernel(scale, *refs), "far_sum", shape(dims, F32), (1,),
        [whole(dims)] * 2 + [ANY] * len(first), whole(dims), [],
    )(scalars, own, came, *first)


def weight_copies(tables, scalars, refs, weight, sem):
    site, index = scalars[0], scalars[1]
    shard = weight.shape[1] // N_FSDP
    copies = []
    for (places, swapped), ref in zip(tables, refs, strict=True):
        at = 0
        for place in places:
            if isinstance(place, int):
                at += place
                continue
            tap, z, (kind, quarter), low, count = place
            start = lax.bitwise_xor(index, 2 * z + swapped) * shard + low
            rows = pl.ds(pl.multiple_of(start, math.gcd(shard, low)), count)
            columns = pl.ds(quarter * QUARTER, QUARTER)
            if kind == "all":
                columns = pl.ds(0, D)
            elif kind == "xor":
                column = lax.bitwise_xor(site, quarter) * QUARTER
                columns = pl.ds(pl.multiple_of(column, QUARTER), QUARTER)
            source = ref.at[pl.ds(at, count), :]
            copies.append(pltpu.make_async_copy(source, weight.at[tap, rows, columns], sem))
            at += count
        assert at == ref.shape[0]
    return copies


def fetch(source, target, sem):
    copy = pltpu.make_async_copy(source, target, sem)
    copy.start()
    return copy


def input_grad_kernel(tables, scalars, *refs):
    n = len(tables)
    parts, (x_hbm, cot_hbm, out_ref) = refs[:n], refs[n : n + 3]
    x_ref, cot_ref, weight, normed, inverse, back, sems, sem = refs[n + 3 :]
    x_copy = fetch(x_hbm, x_ref, sems.at[0])
    cot_copy = fetch(cot_hbm, cot_ref, sems.at[1])
    copies = weight_copies(tables, scalars, parts, weight, sem)
    for copy in copies:
        copy.start()
    x_copy.wait()

    @pl.loop(0, ROWS // BLOCK)
    def _(i):
        rows = pl.ds(pl.multiple_of(i * BLOCK, BLOCK), BLOCK)
        normed[rows, :], inverse[rows, :] = normalise(x_ref[rows, :])

    cot_copy.wait()
    for copy in copies:
        copy.wait()

    def finish(rows):
        term, row_normed = back[rows, :], normed[rows, :]
        inner = term - jnp.mean(term, axis=-1, keepdims=True)
        inner = inner - row_normed * jnp.mean(term * row_normed, axis=-1, keepdims=True)
        out_ref[rows, :] = (cot_ref[rows, :].astype(F32) + inverse[rows, :] * inner).astype(BF16)

    half = ROWS // 2
    for i in range(3):
        if i < 2:
            rows = slice(i * half, (i + 1) * half)
            for j in range(D // COLUMNS):
                columns = slice(j * COLUMNS, (j + 1) * COLUMNS)
                back[rows, columns] = dot_nt(cot_ref[rows, :], weight[0, columns, :])
        if i > 0:
            for j in range(4):
                start = (i - 1) * half + j * half // 4
                finish(slice(start, start + half // 4))


def split_parts(parts):
    return [(places, swapped) for _, places, swapped in parts], [value for value, _, _ in parts]


def input_gradient(scalars, parts, inputs, cotangent):
    tables, values = split_parts(parts)
    return call(
        lambda *refs: input_grad_kernel(tables, *refs), "input_gradient", shape((ROWS, D), BF16),
        (1,), [HBM] * (len(values) + 2), whole((ROWS, D)),
        [
            pltpu.VMEM((ROWS, D), BF16),
            pltpu.VMEM((ROWS, D), BF16),
            pltpu.VMEM((1, D, D), BF16),
            pltpu.VMEM((ROWS, D), F32),
            pltpu.VMEM((ROWS, 1), F32),
            pltpu.VMEM((ROWS, D), F32),
            pltpu.SemaphoreType.DMA((2,)),
            pltpu.SemaphoreType.DMA,
        ],
        vmem=22,
    )(scalars, *values, inputs, cotangent)


def held_before(start, holder):
    return 2 * (start // (2 * N_FSDP)) + jnp.clip(start % (2 * N_FSDP) - 2 * holder, 0, 2)


BASES_AT = 2
SEGMENTS_AT = BASES_AT + N_FSDP
BEFORE_AT = SEGMENTS_AT + N_FSDP * CAP
COUNT_AT = BEFORE_AT + N_FSDP * CAP


def plan_kernel(scalars, plan):
    site, index = scalars[0], scalars[1]
    plan[0], plan[1] = site, index
    count = scalars[2 + index]
    plan[COUNT_AT] = count
    starts = [jnp.int32(0)]
    for owner in range(N_FSDP):
        starts.append(starts[-1] + scalars[2 + owner])
    my_start = jnp.int32(0)
    for owner in range(N_FSDP):
        place = lax.bitwise_xor(index, owner)
        plan[BASES_AT + place] = held_before(starts[owner], index)
        my_start = my_start + jnp.where(owner < index, scalars[2 + owner], 0)

    @pl.loop(0, N_FSDP * CAP)
    def _(block):
        holder = lax.bitwise_xor(index, block // CAP)
        slot = held_before(my_start, holder) + block % CAP
        segment = 2 * (slot // 2 * N_FSDP + holder) + slot % 2 - my_start
        held = (segment >= 0) & (segment < count)
        plan[SEGMENTS_AT + block] = jnp.where(held, segment, OWN_SEG)
        plan[BEFORE_AT + block] = jnp.where(held & (segment > 0), segment - 1, OWN_SEG)


def plan_of(scalars):
    return call(
        plan_kernel, "plan", shape((COUNT_AT + 1,), jnp.int32), (1,), [],
        pl.BlockSpec(memory_space=pltpu.SMEM), [],
    )(scalars)


def stem_kernel(tables, scalars, *refs):
    n = len(tables)
    parts, grad_ref, outs = refs[:n], refs[n], refs[n + 1 : n + 1 + N_FSDP]
    weight, mixed, leading, firsts, sem = refs[n + 1 + N_FSDP :]
    copies = weight_copies(tables, scalars, parts, weight, sem)
    for copy in copies:
        copy.start()
    for copy in copies:
        copy.wait()
    index = scalars[1]
    for lane in range(0, CS, CS // 2):
        span = pl.ds(lane, CS // 2)
        even = dot_nt(grad_ref[...], weight[1, span, :])
        first = dot_nt(grad_ref[...], weight[0, span, :])
        leading[:, span] = first
        row = lax.broadcasted_iota(jnp.int32, first.shape, 0)
        following = jnp.where(row % SEG == SEG - 1, 0.0, pltpu.roll(first, ROWS - 1, 0))
        odd = dot_nt(grad_ref[...], weight[2, span, :]) + following
        for part in range(CS // 2 // LANES):
            at = lane // LANES + part
            columns = slice(part * LANES, (part + 1) * LANES)
            mixed[at, pl.ds(0, ROWS, stride=2), :] = even[:, columns]
            mixed[at, pl.ds(1, ROWS, stride=2), :] = odd[:, columns]

    for place, out in enumerate(outs):
        base = scalars[BASES_AT + place]
        for rank in range(CAP):
            slot = jnp.minimum(base + rank, HOLD - 1)
            rows = pl.ds(pl.multiple_of(slot * 2 * SEG, 2 * SEG), 2 * SEG)
            for lane in range(CS // LANES):
                out[rank, :, lane * LANES : (lane + 1) * LANES] = mixed[lane, rows, :].astype(BF16)
            firsts[rank : rank + 1, :] = leading[pl.ds(slot * SEG, 1), :]
        out[CAP] = firsts[...].astype(BF16)


VMEM = pl.BlockSpec(memory_space=pltpu.VMEM)


def stem_payloads(scalars, parts, grad):
    tables, values = split_parts(parts)
    payload = (CAP + 1, 2 * SEG, CS)
    return call(
        lambda *refs: stem_kernel(tables, *refs), "stem_payloads",
        (shape(payload, BF16),) * N_FSDP, (1,),
        [ANY] * len(values) + [whole((ROWS, D))], (VMEM,) * N_FSDP,
        [
            pltpu.VMEM((3, CS, D), BF16),
            pltpu.VMEM((CS // LANES, 2 * ROWS, LANES), F32),
            pltpu.VMEM((ROWS, CS), F32),
            pltpu.VMEM((CAP, CS), F32),
            pltpu.SemaphoreType.DMA,
        ],
        vmem=18,
    )(scalars, *values, grad)


def owner_kernel(scalars, *refs):
    payloads, terms, (out_hbm, total), (out, sem, total_sem) = (
        refs[:N_FSDP], refs[N_FSDP : N_FSDP + N_SITE], refs[-5:-3], refs[-3:]
    )
    copies = []
    for distance, term in enumerate(terms):
        at = pl.multiple_of(lax.bitwise_xor(scalars[0], distance) * QUARTER, QUARTER)
        copies.append(
            pltpu.make_async_copy(term, total.at[:, pl.ds(at, QUARTER)], total_sem.at[distance])
        )
    for copy in copies:
        copy.start()

    def rows_of_segment(segment):
        return pl.ds(pl.multiple_of(segment * 2 * SEG, 2 * SEG), 2 * SEG)

    @pl.loop(scalars[COUNT_AT], OWN_SEG)
    def _(segment):
        out[rows_of_segment(segment), :] = jnp.zeros((2 * SEG, CS), BF16)

    for i, place in enumerate(PAYLOAD_ORDER):
        for rank in range(CAP):
            segment = scalars[SEGMENTS_AT + place * CAP + rank]
            out[rows_of_segment(segment), :] = payloads[i][rank]
    last_row = lax.broadcasted_iota(jnp.int32, (2 * SEG, CS), 0) == 2 * SEG - 1
    for i, place in enumerate(PAYLOAD_ORDER):
        firsts = payloads[i][CAP].astype(F32)
        for rank in range(CAP):
            rows = rows_of_segment(scalars[BEFORE_AT + place * CAP + rank])
            first = jnp.broadcast_to(firsts[rank : rank + 1, :], (2 * SEG, CS))
            term = jnp.where(last_row, first, 0.0)
            out[rows, :] = (out[rows, :].astype(F32) + term).astype(BF16)
    copies.append(fetch(out.at[pl.ds(0, out_hbm.shape[0]), :], out_hbm, sem))
    for copy in copies:
        copy.wait()


def owner_rows(scalars, payloads, terms):
    rows = 2 * OWN_SEG * SEG
    return call(
        owner_kernel, "owner_rows", (shape((rows, CS), BF16), shape((D // N_FSDP, D), F32)), (1,),
        [VMEM] * N_FSDP + [ANY] * N_SITE, (HBM, HBM),
        [
            pltpu.VMEM((rows + 2 * SEG, CS), BF16),
            pltpu.SemaphoreType.DMA,
            pltpu.SemaphoreType.DMA((N_SITE,)),
        ],
    )(scalars, *payloads, *terms)


def body(held_input, held_cotangent, proj_weight, stem_weight, seg_counts):
    site, index = lax.axis_index("site"), lax.axis_index("fsdp")
    scalars = jnp.concatenate([jnp.stack([site, index]).astype(jnp.int32), seg_counts[0]])
    inputs, cotangent = held_input[0], held_cotangent[0]

    plan = plan_of(scalars)
    piece = (D // N_FSDP, QUARTER)
    half = (3, HALF, QUARTER)
    units = (UNIT_ROWS, QUARTER)
    quarters = (QUARTER_ROWS, QUARTER)

    (proj_quarter,) = join(cut_proj_kernel, "cut_proj", [piece], [proj_weight])
    around = [swap_z(proj_quarter, distance) for distance in Z_ORDER]
    normed_own = norm_half(scalars, inputs, [proj_quarter])
    normed_theirs = norm_half(scalars, swap_core(inputs), [normed_own])
    kept_a, sent_a, kept_b, sent_b = outer_pieces(
        scalars, normed_own, normed_theirs, cotangent, swap_core(cotangent)
    )
    n, m = 3 * HALF, D // 4
    a0, b0, stem_units = join(
        halves_kernel, "halves", [(n + 2 * m, QUARTER)] * 2 + [units],
        [sent_a, sent_b, *around, stem_weight], aliases={0: 0, 1: 1},
    )

    a, b, packed, stem_pair, own_a, own_b = join(
        site_step_kernel, "site_step", [(2 * n + m, QUARTER)] * 2 + [(D + 4 * n, QUARTER), (2, *units)],
        [
            proj_weight, stem_weight, a0, b0, swap_site(a0, 1), swap_site(b0, 2),
            stem_units, swap_z(stem_units, 2), kept_a, kept_b,
        ],
        [plan],
        wide_dims=[(m, QUARTER)] * 2,
    )

    a2, b2 = swap_site(a, 2), swap_site(b, 1)
    near = swap_z(stem_pair, 1)
    packed = swap_core(packed)
    kept, sent = site_sum(scalars, own_a, a2, own_b, b2)
    others, all_others, late = join(
        three_kernel, "three", [(3, *quarters), (3, *units), (4 * n, QUARTER)],
        [stem_pair, near, a2, b2], [kept, packed],
    )

    over = [swap_site(others, distance) for distance in (1, 2, 3)]
    late, late_stem = swap_core(late), swap_core(rows_of(all_others))
    whole_proj = [(0, 0, ("all", 0), 0, D // N_FSDP)]
    first = [half_places(0, 0) + half_places(1, 0), half_places(0, HALF) + half_places(2, HALF)]
    last = [half_places(2, 0) + half_places(3, 0), half_places(1, HALF) + half_places(3, HALF)]
    proj_parts = [
        (proj_weight, whole_proj, 0),
        (a, first[0] + [m], 0), (b, first[1] + [m], 0),
        (a2, last[0] + [m], 0), (b2, last[1] + [m], 0),
        (packed, shard_places(0, D // N_FSDP) + [D // 2] + sum(first, []), 1), (late, sum(last, []), 1),
    ]
    grad = input_gradient(scalars, proj_parts, inputs, cotangent)
    own, sent = near_sum(scalars, kept, swap_z(sent, 1), [grad])
    (over,) = join(collect_kernel, "collect", [(3, 3, *quarters)], over, [grad, sent, late_stem])
    over = rows_of(over)
    last = sum((unit_places(d) for d in (1, 2, 3)), [])
    whole_stem = [(tap, 0, ("all", 0), 0, STEM_ROWS) for tap in range(TAPS)]
    stem_parts = [
        (stem_weight.reshape(-1, D), whole_stem, 0),
        (
            packed,
            [D // 2] + sum((shard_places(tap, STEM_ROWS) for tap in range(TAPS)), []) + [4 * n], 1,
        ),
        (rows_of(all_others), all_places(), 0), (over, last, 0),
        (late_stem, all_places(), 1), (swap_core(over), last, 1),
    ]

    payloads = stem_payloads(plan, stem_parts, grad)
    received = {0: payloads[0]}
    for d in PAYLOAD_ORDER[1:]:
        received[d] = lax.ppermute(payloads[d], "fsdp", [(i, i ^ d) for i in range(N_FSDP)])
    scale = 1.0 / math.sqrt(N_SITE * N_FSDP * ROWS)
    terms = far_sum(scalars, own, swap_z(sent, 2), scale, [received[4]])
    terms = [terms] + [swap_site(terms, d) for d in (1, 2, 3)]
    stem_grad, weight_grad = owner_rows(plan, [received[d] for d in PAYLOAD_ORDER], terms)
    return (stem_grad[None], weight_grad)


def plain_body(held_input, held_cotangent, proj_weight, stem_weight, seg_counts):
    group_size = lax.axis_size("fsdp")
    capacity = 2 * ((OWN_SEG + 2 * group_size - 1) // (2 * group_size))
    my_index = lax.axis_index("fsdp")
    cotangent = held_cotangent[0]
    normed, inverse = normalise(held_input[0])
    normed_bf = normed.astype(jnp.bfloat16)
    proj_back = dot_nt(cotangent, lax.all_gather(proj_weight, "fsdp", axis=0, tiled=True))
    input_grad = cotangent.astype(jnp.float32) + inverse * (
        proj_back
        - jnp.mean(proj_back, axis=-1, keepdims=True)
        - normed * jnp.mean(proj_back * normed, axis=-1, keepdims=True)
    )
    input_grad = input_grad.astype(jnp.bfloat16)
    counts = seg_counts[0]
    endings = jnp.cumsum(counts)
    starts = endings - counts
    slot_ids = jnp.arange(HOLD, dtype=jnp.int32)
    item_index = 2 * (slot_ids // 2 * group_size + my_index) + slot_ids % 2
    owner_ids = jnp.sum((item_index[:, None] >= endings[None, :]).astype(jnp.int32), axis=1)
    earlier = (slot_ids[None, :] < slot_ids[:, None]) & (owner_ids[None, :] == owner_ids[:, None])
    rank_ids = jnp.sum(earlier.astype(jnp.int32), axis=1)
    target = owner_ids * capacity + rank_ids
    positions = jnp.arange(group_size * capacity, dtype=jnp.int32)
    matched = target[None, :] == positions[:, None]
    filled = jnp.any(matched, axis=1)
    source = jnp.sum(jnp.where(matched, slot_ids[None, :], 0), axis=1)
    owner_hit = jnp.arange(group_size, dtype=jnp.int32) == my_index
    my_count = jnp.sum(jnp.where(owner_hit, counts, 0))
    my_start = jnp.sum(jnp.where(owner_hit, starts, 0))
    segment = jnp.arange(OWN_SEG, dtype=jnp.int32)
    is_live = segment < my_count
    holder = (my_start + segment) // 2 % group_size
    before = (
        (segment[None, :] < segment[:, None])
        & (holder[None, :] == holder[:, None])
        & is_live[None, :]
    )
    holder_rank = jnp.sum(before.astype(jnp.int32), axis=1)
    row_index = jnp.where(is_live, holder * capacity + holder_rank, 0)
    held_segments = input_grad.reshape(HOLD, SEG, D)
    zero_bf = jnp.zeros((), jnp.bfloat16)
    send_rows = jnp.where(filled[:, None, None], jnp.take(held_segments, source, axis=0), zero_bf)
    received = lax.all_to_all(
        send_rows.reshape(group_size, capacity, SEG, D), "fsdp", split_axis=0, concat_axis=0, tiled=True
    )
    picked = jnp.take(received.reshape(group_size * capacity, SEG, D), row_index, axis=0)
    frames = jnp.where(is_live[:, None, None], picked, zero_bf).reshape(OWN_SEG * SEG, D)
    tap_terms = jnp.einsum(
        "rd,kcd->krc",
        frames,
        lax.all_gather(stem_weight, "fsdp", axis=1, tiled=True),
        preferred_element_type=jnp.float32,
    )
    shifted = jnp.concatenate(
        [tap_terms[0][1:], jnp.zeros((1, tap_terms.shape[2]), jnp.float32)], 0
    )
    stem_rows = (
        jnp.stack([tap_terms[1], tap_terms[2] + shifted], 1)
        .reshape(2 * OWN_SEG * SEG, tap_terms.shape[2])
        .astype(jnp.bfloat16)
    )
    shard_sum = lax.psum_scatter(
        lax.dot_general(
            normed_bf, cotangent, (((0,), (0,)), ((), ())), preferred_element_type=jnp.float32
        ),
        "fsdp",
        scatter_dimension=0,
        tiled=True,
    )
    shard_sum = lax.psum(shard_sum, "site")
    weight_grad = shard_sum / math.sqrt(lax.axis_size("site") * group_size * ROWS)
    return (stem_rows[None], weight_grad)


def solution(mesh):
    placed = (
        P("site", "fsdp", None),
        P("site", "fsdp", None),
        P("fsdp", None),
        P(None, "fsdp", None),
        P("site", None),
    )
    fits = (mesh.shape["site"], mesh.shape["fsdp"]) == (N_SITE, N_FSDP)
    return jax.shard_map(
        body if fits else plain_body,
        mesh=mesh,
        in_specs=placed,
        out_specs=(P("site", "fsdp", None), P("fsdp", None)),
        check_vma=False,
    )
```

```python
import math

import jax
import jax.numpy as jnp
from jax import lax
from jax.experimental import pallas as pl
from jax.experimental.pallas import tpu as pltpu
from jax.sharding import PartitionSpec as P

D = 1536
SEG = 8
HOLD = 64
OWN_SEG = 128
N_SITE = 4
N_FSDP = 8
N_Z = N_FSDP // 2
QUARTER = D // N_SITE
CAP = OWN_SEG // N_FSDP
CS = 512
ROWS = HOLD * SEG
BLOCK = 256
LANES = 128
COLUMNS = 512
PAYLOAD_ORDER = (0, 4, 5, 2, 3, 6, 7, 1)
MIB = 1024 * 1024

EPSILON = 1e-05
F32 = jnp.float32
BF16 = jnp.bfloat16


def swap_core(value):
    return lax.ppermute(value, "fsdp", [(i, i ^ 1) for i in range(N_FSDP)])


def swap_z(value, distance):
    return lax.ppermute(value, "fsdp", [(i, i ^ (2 * distance)) for i in range(N_FSDP)])


def swap_site(value, distance):
    return lax.ppermute(value, "site", [(i, i ^ distance) for i in range(N_SITE)])


def hold(value, *first):
    return pl.pallas_call(
        lambda *refs: None,
        name="hold",
        out_shape=shape(value.shape, value.dtype),
        in_specs=[HBM] + [ANY] * len(first),
        out_specs=HBM,
        input_output_aliases={0: 0},
        cost_estimate=pl.CostEstimate(flops=0, bytes_accessed=0, transcendentals=0),
    )(value, *first)


Z_ORDER = (2, 1, 3)
HALF = D // N_FSDP // 2
STEM_ROWS = CS // N_FSDP
TAPS = 3


def half_places(site, low):
    return [(0, z, ("xor", site), low, HALF) for z in Z_ORDER]


SPLIT = STEM_ROWS // 2
QUARTER_BLOCKS = ((1, 0, STEM_ROWS), (0, 0, SPLIT))
WHOLE_BLOCKS = ((2, 0, STEM_ROWS), (0, SPLIT, STEM_ROWS - SPLIT))
QUARTER_ROWS = sum(count for _, _, count in QUARTER_BLOCKS)
UNIT_ROWS = QUARTER_ROWS + N_SITE * sum(count for _, _, count in WHOLE_BLOCKS)


def unit_places(site):
    return [(tap, z, ("xor", site), low, count) for z in Z_ORDER for tap, low, count in QUARTER_BLOCKS]


def all_places():
    blocks = [(tap, ("xor", 0), low, count) for tap, low, count in QUARTER_BLOCKS]
    blocks += [(tap, ("abs", j), low, count) for tap, low, count in WHOLE_BLOCKS for j in range(N_SITE)]
    return [(tap, z, kind, low, count) for z in Z_ORDER for tap, kind, low, count in blocks]


def shard_places(tap, count):
    return [(tap, 0, ("abs", j), 0, count) for j in range(N_SITE)]


def rows_of(value):
    return value.reshape(-1, QUARTER)


def call(kernel, name, out_shape, grid, in_specs, out_specs, scratch, vmem=16):
    return pl.pallas_call(
        kernel,
        name=name,
        out_shape=out_shape,
        grid_spec=pltpu.PrefetchScalarGridSpec(
            num_scalar_prefetch=1,
            grid=grid,
            in_specs=in_specs,
            out_specs=out_specs,
            scratch_shapes=scratch,
        ),
        compiler_params=pltpu.CompilerParams(
            dimension_semantics=("arbitrary",) * len(grid), vmem_limit_bytes=vmem * MIB
        ),
        cost_estimate=pl.CostEstimate(flops=0, bytes_accessed=0, transcendentals=0),
    )


ANY = pl.BlockSpec(memory_space=pl.ANY)
HBM = pl.BlockSpec(memory_space=pltpu.HBM)


def whole(shape):
    return pl.BlockSpec(shape, lambda i, scalars: (0,) * len(shape))


def row_block(rows, columns):
    return pl.BlockSpec((rows, columns), lambda i, scalars: (i, 0))


def shape(dims, dtype):
    return jax.ShapeDtypeStruct(dims, dtype)


def dot_nt(a, b):
    return lax.dot_general(a, b, (((1,), (1,)), ((), ())), preferred_element_type=F32)


def join(kernel, name, out_dims, values, first=(), wide_dims=(), aliases=None):
    n = len(values)

    def wrapped(*refs):
        kernel(*refs[:n], *refs[n + len(first) :])

    out = tuple(shape(dims, BF16) for dims in out_dims) + tuple(shape(dims, F32) for dims in wide_dims)
    vmem = pl.BlockSpec(memory_space=pltpu.VMEM)
    return pl.pallas_call(
        wrapped,
        name=name,
        out_shape=out,
        in_specs=[vmem] * n + [ANY] * len(first),
        out_specs=(vmem,) * len(out),
        input_output_aliases=aliases or {},
        compiler_params=pltpu.CompilerParams(vmem_limit_bytes=14 * MIB),
        cost_estimate=pl.CostEstimate(flops=0, bytes_accessed=0, transcendentals=0),
    )(*values, *first)


def cut_proj_kernel(shard, out):
    at = pl.multiple_of(lax.axis_index("site") * QUARTER, QUARTER)
    out[...] = shard[:, pl.ds(at, QUARTER)]


def halves_kernel(_, __, far, near, farthest, stem, a, b, units):
    for i, piece in enumerate((far, near, farthest)):
        a[i * HALF : (i + 1) * HALF, :] = piece[:HALF, :]
        b[i * HALF : (i + 1) * HALF, :] = piece[HALF:, :]
    at = pl.multiple_of(lax.axis_index("site") * QUARTER, QUARTER)
    pieces = [stem[tap, low : low + count, pl.ds(at, QUARTER)] for tap, low, count in QUARTER_BLOCKS]
    for tap, low, count in WHOLE_BLOCKS:
        pieces += column_pieces(stem[tap, low : low + count, :])
    pack_rows(units, pieces)


def pack_rows(out, pieces):
    at = 0
    for piece in pieces:
        out[at : at + piece.shape[0], :] = piece
        at += piece.shape[0]


def column_pieces(rows):
    return [rows[:, i * QUARTER : (i + 1) * QUARTER] for i in range(N_SITE)]


def site_step_kernel(
    shard, stem, a0, b0, a1, b1, units, far, kept_a, kept_b, a, b, packed, pair, own_a, own_b
):
    pair[0], pair[1] = units[...], far[...]
    n, m = 3 * HALF, D // 4
    for sent, came, kept, out, own in ((a0, a1, kept_a, a, own_a), (b0, b1, kept_b, b, own_b)):
        for j, source in enumerate((sent, came)):
            out[j * n : (j + 1) * n, :] = source[:n, :]
        own[...] = kept[0] + came[n : n + m, :].astype(F32)
        out[2 * n :, :] = (kept[1] + came[n + m :, :].astype(F32)).astype(BF16)
    pieces = column_pieces(shard[...])
    for tap in range(TAPS):
        pieces += column_pieces(stem[tap])
    pack_rows(packed, pieces + [ref[:n, :] for ref in (a0, a1, b0, b1)])


def collect_kernel(a, b, c, out):
    out[0], out[1], out[2] = a[...], b[...], c[...]


def three_kernel(pair, near, a2, b2, quarters, units, packed):
    n = 6 * HALF
    packed[:n, :], packed[n:, :] = a2[:n, :], b2[:n, :]
    for i, piece in enumerate((pair.at[1], near.at[0], near.at[1])):
        quarters[i] = piece[:QUARTER_ROWS, :]
        units[i] = piece[...]


def normalise(inputs):
    inputs = inputs.astype(F32)
    centered = inputs - jnp.mean(inputs, axis=-1, keepdims=True)
    variance = jnp.mean(centered * centered, axis=-1, keepdims=True)
    inverse = lax.rsqrt(variance + EPSILON)
    return centered * inverse, inverse


def norm_kernel(scalars, x_ref, *refs):
    out_ref, turned = refs[-2:]
    core = scalars[1] % 2
    normed, _ = normalise(x_ref[...])
    turned[...] = normed.astype(BF16).T
    shard = D // N_FSDP
    for z in range(N_Z):
        rows = pl.ds(pl.multiple_of((2 * z + core) * shard, shard), shard)
        out_ref[pl.ds(z * shard, shard), :] = turned[rows, :]


def norm_half(scalars, inputs, first=()):
    return call(
        norm_kernel, "norm_half", shape((D // 2, ROWS), BF16), (ROWS // BLOCK,),
        [row_block(BLOCK, D)] + [ANY] * len(first),
        pl.BlockSpec((D // 2, BLOCK), lambda i, scalars: (0, i)), [pltpu.VMEM((D, BLOCK), BF16)],
    )(scalars, inputs, *first)


OUTER_PLACES = (((0, 0), (0, 0)), ((1, 0), (0, 1)), ((0, 1), (1, 0)), ((1, 1), (1, 1)))


def outer_kernel(scalars, na_ref, nb_ref, ca_ref, cb_ref, ka_ref, a_ref, kb_ref, b_ref):
    site = scalars[0]
    n, m = 3 * HALF, D // 4
    for half in range(2):
        start = lax.bitwise_xor(site // 2, half) * 2 * QUARTER
        columns = pl.ds(pl.multiple_of(start, 2 * QUARTER), 2 * QUARTER)
        total = jnp.dot(na_ref[...], ca_ref[:, columns], preferred_element_type=F32)
        total = total + jnp.dot(nb_ref[...], cb_ref[:, columns], preferred_element_type=F32)
        low, high = total[:, :QUARTER], total[:, QUARTER:]
        odd = site % 2 == 1
        for at, value in ((2 * half, jnp.where(odd, high, low)), (2 * half + 1, jnp.where(odd, low, high))):
            for (goes, i), kept, sent, rows in zip(
                OUTER_PLACES[at], (ka_ref, kb_ref), (a_ref, b_ref), (value[:m, :], value[m:, :]), strict=True
            ):
                if goes:
                    sent[n + i * m : n + (i + 1) * m, :] = rows.astype(BF16)
                else:
                    kept[i] = rows


def outer_pieces(scalars, normed_a, normed_b, cotangent_a, cotangent_b):
    kept, sent = (2, D // 4, QUARTER), (3 * HALF + D // 2, QUARTER)
    values = (normed_a, normed_b, cotangent_a, cotangent_b)
    return call(
        outer_kernel, "outer_pieces", (shape(kept, F32), shape(sent, BF16)) * 2, (1,),
        [whole(value.shape) for value in values], (whole(kept), whole(sent)) * 2, [], vmem=24,
    )(scalars, *values)


def site_sum_kernel(scalars, oa_ref, ra_ref, ob_ref, rb_ref, kept_ref, sent_ref, total):
    shard = D // N_FSDP
    z = scalars[1] // 2
    total[: D // 4, :] = oa_ref[...] + ra_ref[6 * HALF :, :].astype(F32)
    total[D // 4 :, :] = ob_ref[...] + rb_ref[6 * HALF :, :].astype(F32)
    for distance, (ref, i) in enumerate(((kept_ref, 0), (sent_ref, 0), (kept_ref, 1), (sent_ref, 1))):
        rows = pl.ds(pl.multiple_of(lax.bitwise_xor(z, distance) * shard, shard), shard)
        ref[i] = total[rows, :].astype(ref.dtype)


def site_sum(scalars, *values):
    out = (2, D // N_FSDP, QUARTER)
    return call(
        site_sum_kernel, "site_sum", (shape(out, F32), shape(out, BF16)), (1,),
        [whole(value.shape) for value in values], (whole(out),) * 2, [pltpu.VMEM((D // 2, QUARTER), F32)],
    )(scalars, *values)


def near_sum_kernel(scalars, kept_ref, came_ref, *refs):
    own_ref, sent_ref = refs[-2:]
    own_ref[...] = kept_ref[0] + came_ref[0].astype(F32)
    sent_ref[...] = (kept_ref[1] + came_ref[1].astype(F32)).astype(BF16)


def near_sum(scalars, kept, came, first):
    dims, out = (2, D // N_FSDP, QUARTER), (D // N_FSDP, QUARTER)
    return call(
        near_sum_kernel, "near_sum", (shape(out, F32), shape(out, BF16)), (1,),
        [whole(dims)] * 2 + [ANY] * len(first), (whole(out),) * 2, [],
    )(scalars, kept, came, *first)


def far_sum_kernel(scale, scalars, own_ref, came_ref, *refs):
    refs[-1][...] = (own_ref[...] + came_ref[...].astype(F32)) * scale


def far_sum(scalars, own, came, scale, first):
    dims = (D // N_FSDP, QUARTER)
    return call(
        lambda *refs: far_sum_kernel(scale, *refs), "far_sum", shape(dims, F32), (1,),
        [whole(dims)] * 2 + [ANY] * len(first), whole(dims), [],
    )(scalars, own, came, *first)


def weight_copies(tables, scalars, refs, weight, sem):
    site, index = scalars[0], scalars[1]
    shard = weight.shape[1] // N_FSDP
    copies = []
    for (places, swapped), ref in zip(tables, refs, strict=True):
        at = 0
        for place in places:
            if isinstance(place, int):
                at += place
                continue
            tap, z, (kind, quarter), low, count = place
            start = lax.bitwise_xor(index, 2 * z + swapped) * shard + low
            rows = pl.ds(pl.multiple_of(start, math.gcd(shard, low)), count)
            columns = pl.ds(quarter * QUARTER, QUARTER)
            if kind == "all":
                columns = pl.ds(0, D)
            elif kind == "xor":
                column = lax.bitwise_xor(site, quarter) * QUARTER
                columns = pl.ds(pl.multiple_of(column, QUARTER), QUARTER)
            source = ref.at[pl.ds(at, count), :]
            copies.append(pltpu.make_async_copy(source, weight.at[tap, rows, columns], sem))
            at += count
        assert at == ref.shape[0]
    return copies


def fetch(source, target, sem):
    copy = pltpu.make_async_copy(source, target, sem)
    copy.start()
    return copy


def input_grad_kernel(tables, scalars, *refs):
    n = len(tables)
    parts, (x_hbm, cot_hbm, out_ref) = refs[:n], refs[n : n + 3]
    x_ref, cot_ref, weight, normed, inverse, back, sems, sem = refs[n + 3 :]
    x_copy = fetch(x_hbm, x_ref, sems.at[0])
    cot_copy = fetch(cot_hbm, cot_ref, sems.at[1])
    copies = weight_copies(tables, scalars, parts, weight, sem)
    for copy in copies:
        copy.start()
    x_copy.wait()

    @pl.loop(0, ROWS // BLOCK)
    def _(i):
        rows = pl.ds(pl.multiple_of(i * BLOCK, BLOCK), BLOCK)
        normed[rows, :], inverse[rows, :] = normalise(x_ref[rows, :])

    cot_copy.wait()
    for copy in copies:
        copy.wait()

    def finish(rows):
        term, row_normed = back[rows, :], normed[rows, :]
        inner = term - jnp.mean(term, axis=-1, keepdims=True)
        inner = inner - row_normed * jnp.mean(term * row_normed, axis=-1, keepdims=True)
        out_ref[rows, :] = (cot_ref[rows, :].astype(F32) + inverse[rows, :] * inner).astype(BF16)

    half = ROWS // 2
    for i in range(3):
        if i < 2:
            rows = slice(i * half, (i + 1) * half)
            for j in range(D // COLUMNS):
                columns = slice(j * COLUMNS, (j + 1) * COLUMNS)
                back[rows, columns] = dot_nt(cot_ref[rows, :], weight[0, columns, :])
        if i > 0:
            for j in range(4):
                start = (i - 1) * half + j * half // 4
                finish(slice(start, start + half // 4))


def split_parts(parts):
    return [(places, swapped) for _, places, swapped in parts], [value for value, _, _ in parts]


def input_gradient(scalars, parts, inputs, cotangent):
    tables, values = split_parts(parts)
    return call(
        lambda *refs: input_grad_kernel(tables, *refs), "input_gradient", shape((ROWS, D), BF16),
        (1,), [HBM] * (len(values) + 2), whole((ROWS, D)),
        [
            pltpu.VMEM((ROWS, D), BF16),
            pltpu.VMEM((ROWS, D), BF16),
            pltpu.VMEM((1, D, D), BF16),
            pltpu.VMEM((ROWS, D), F32),
            pltpu.VMEM((ROWS, 1), F32),
            pltpu.VMEM((ROWS, D), F32),
            pltpu.SemaphoreType.DMA((2,)),
            pltpu.SemaphoreType.DMA,
        ],
        vmem=22,
    )(scalars, *values, inputs, cotangent)


def held_before(start, holder):
    return 2 * (start // (2 * N_FSDP)) + jnp.clip(start % (2 * N_FSDP) - 2 * holder, 0, 2)


PAIRS = CAP // 2
BASES_AT = 2
SPLITS_AT = BASES_AT + N_FSDP
SEGMENTS_AT = SPLITS_AT + N_FSDP
BEFORE_AT = SEGMENTS_AT + N_FSDP * CAP
COUNT_AT = BEFORE_AT + N_FSDP * PAIRS


def plan_kernel(scalars, plan):
    site, index = scalars[0], scalars[1]
    plan[0], plan[1] = site, index
    count = scalars[2 + index]
    plan[COUNT_AT] = count
    starts = [jnp.int32(0)]
    for owner in range(N_FSDP):
        starts.append(starts[-1] + scalars[2 + owner])
    my_start = jnp.int32(0)
    for owner in range(N_FSDP):
        start = starts[owner]
        plan[BASES_AT + lax.bitwise_xor(index, owner)] = held_before(start, index)
        my_start = my_start + jnp.where(owner < index, scalars[2 + owner], 0)
        splits = (start % 2 == 1) & (start // 2 % N_FSDP == index)
        plan[SPLITS_AT + owner] = jnp.where(splits, 2 * (start // (2 * N_FSDP)) * SEG + SEG - 1, -1)

    @pl.loop(0, N_FSDP * CAP)
    def _(block):
        holder = lax.bitwise_xor(index, block // CAP)
        slot = held_before(my_start, holder) + block % CAP
        segment = 2 * (slot // 2 * N_FSDP + holder) + slot % 2 - my_start
        held = (segment >= 0) & (segment < count)
        plan[SEGMENTS_AT + block] = jnp.where(held, segment, OWN_SEG)

    @pl.loop(0, N_FSDP * PAIRS)
    def _(block):
        holder = lax.bitwise_xor(index, block // PAIRS)
        segment = 2 * (even_slot(held_before(my_start, holder), block % PAIRS) // 2 * N_FSDP + holder) - my_start
        held = (segment > 0) & (segment < count)
        plan[BEFORE_AT + block] = jnp.where(held, segment - 1, OWN_SEG)


def even_slot(base, i):
    return base + base % 2 + 2 * i


def plan_of(scalars):
    return call(
        plan_kernel, "plan", shape((COUNT_AT + 1,), jnp.int32), (1,), [],
        pl.BlockSpec(memory_space=pltpu.SMEM), [],
    )(scalars)


def stem_kernel(tables, scalars, *refs):
    n = len(tables)
    parts, grad_ref, outs = refs[:n], refs[n], refs[n + 1 : n + 1 + N_FSDP]
    weight, mixed, leading, firsts, sem = refs[n + 1 + N_FSDP :]
    copies = weight_copies(tables, scalars, parts, weight, sem)
    for copy in copies:
        copy.start()
    for copy in copies:
        copy.wait()
    row = lax.broadcasted_iota(jnp.int32, (ROWS, LANES), 0)
    inside = row % (2 * SEG) == SEG - 1
    for owner in range(1, N_FSDP):
        inside = inside & (row != scalars[SPLITS_AT + owner])
    inside = inside | (row % SEG != SEG - 1)
    for lane in range(0, CS, CS // 2):
        span = pl.ds(lane, CS // 2)
        even = dot_nt(grad_ref[...], weight[1, span, :])
        first = dot_nt(grad_ref[...], weight[0, span, :])
        leading[:, span] = first
        following = pltpu.roll(first, ROWS - 1, 0)
        odd = dot_nt(grad_ref[...], weight[2, span, :])
        for part in range(CS // 2 // LANES):
            at = lane // LANES + part
            columns = slice(part * LANES, (part + 1) * LANES)
            mixed[at, pl.ds(0, ROWS, stride=2), :] = even[:, columns]
            mixed[at, pl.ds(1, ROWS, stride=2), :] = odd[:, columns] + jnp.where(
                inside, following[:, columns], 0.0
            )

    for place, out in enumerate(outs):
        base = scalars[BASES_AT + place]
        for rank in range(CAP):
            slot = jnp.minimum(base + rank, HOLD - 1)
            rows = pl.ds(pl.multiple_of(slot * 2 * SEG, 2 * SEG), 2 * SEG)
            for lane in range(CS // LANES):
                at, columns = divmod(lane * LANES, CS // 2)
                out[2 * rank + at, :, columns : columns + LANES] = mixed[lane, rows, :].astype(BF16)
        for i in range(PAIRS):
            slot = jnp.minimum(even_slot(base, i), HOLD - 1)
            first = leading[pl.ds(slot * SEG, 1), :]
            for at in range(2):
                firsts[at * PAIRS + i : at * PAIRS + i + 1, :] = first[:, at * CS // 2 : (at + 1) * CS // 2]
        out[2 * CAP] = firsts[...].astype(BF16)


VMEM = pl.BlockSpec(memory_space=pltpu.VMEM)


def stem_payloads(scalars, parts, grad):
    tables, values = split_parts(parts)
    payload = (2 * CAP + 1, 2 * PAIRS, CS // 2)
    return call(
        lambda *refs: stem_kernel(tables, *refs), "stem_payloads",
        (shape(payload, BF16),) * N_FSDP, (1,),
        [ANY] * len(values) + [whole((ROWS, D))], (VMEM,) * N_FSDP,
        [
            pltpu.VMEM((3, CS, D), BF16),
            pltpu.VMEM((CS // LANES, 2 * ROWS, LANES), F32),
            pltpu.VMEM((ROWS, CS), F32),
            pltpu.VMEM((2 * PAIRS, CS // 2), F32),
            pltpu.SemaphoreType.DMA,
        ],
        vmem=18,
    )(scalars, *values, grad)


def owner_kernel(scalars, *refs):
    payloads, terms, (out_hbm, total), (out, sem, total_sem) = (
        refs[:N_FSDP], refs[N_FSDP : N_FSDP + N_SITE], refs[-5:-3], refs[-3:]
    )
    copies = []
    for distance, term in enumerate(terms):
        at = pl.multiple_of(lax.bitwise_xor(scalars[0], distance) * QUARTER, QUARTER)
        copies.append(
            pltpu.make_async_copy(term, total.at[:, pl.ds(at, QUARTER)], total_sem.at[distance])
        )
    for copy in copies:
        copy.start()

    def rows_of_segment(segment):
        return pl.ds(pl.multiple_of(segment * 2 * SEG, 2 * SEG), 2 * SEG)

    @pl.loop(scalars[COUNT_AT], OWN_SEG)
    def _(segment):
        out[rows_of_segment(segment), :] = jnp.zeros((2 * SEG, CS), BF16)

    halves = [slice(0, CS // 2), slice(CS // 2, CS)]
    for i, place in enumerate(PAYLOAD_ORDER):
        for rank in range(CAP):
            rows = rows_of_segment(scalars[SEGMENTS_AT + place * CAP + rank])
            for at, columns in enumerate(halves):
                out[rows, columns] = payloads[i][2 * rank + at]
    last_row = lax.broadcasted_iota(jnp.int32, (2 * SEG, CS // 2), 0) == 2 * SEG - 1
    for i, place in enumerate(PAYLOAD_ORDER):
        firsts = payloads[i][2 * CAP].astype(F32)
        for pair in range(PAIRS):
            rows = rows_of_segment(scalars[BEFORE_AT + place * PAIRS + pair])
            for at, columns in enumerate(halves):
                first = firsts[at * PAIRS + pair : at * PAIRS + pair + 1, :]
                term = jnp.where(last_row, jnp.broadcast_to(first, last_row.shape), 0.0)
                out[rows, columns] = (out[rows, columns].astype(F32) + term).astype(BF16)
    copies.append(fetch(out.at[pl.ds(0, out_hbm.shape[0]), :], out_hbm, sem))
    for copy in copies:
        copy.wait()


def owner_rows(scalars, payloads, terms):
    rows = 2 * OWN_SEG * SEG
    return call(
        owner_kernel, "owner_rows", (shape((rows, CS), BF16), shape((D // N_FSDP, D), F32)), (1,),
        [VMEM] * N_FSDP + [ANY] * N_SITE, (HBM, HBM),
        [
            pltpu.VMEM((rows + 2 * SEG, CS), BF16),
            pltpu.SemaphoreType.DMA,
            pltpu.SemaphoreType.DMA((N_SITE,)),
        ],
    )(scalars, *payloads, *terms)


def body(held_input, held_cotangent, proj_weight, stem_weight, seg_counts):
    site, index = lax.axis_index("site"), lax.axis_index("fsdp")
    scalars = jnp.concatenate([jnp.stack([site, index]).astype(jnp.int32), seg_counts[0]])
    inputs, cotangent = held_input[0], held_cotangent[0]

    plan = plan_of(scalars)
    piece = (D // N_FSDP, QUARTER)
    half = (3, HALF, QUARTER)
    units = (UNIT_ROWS, QUARTER)
    quarters = (QUARTER_ROWS, QUARTER)

    (proj_quarter,) = join(cut_proj_kernel, "cut_proj", [piece], [proj_weight])
    around = [swap_z(proj_quarter, distance) for distance in Z_ORDER]
    normed_own = norm_half(scalars, inputs, [proj_quarter])
    normed_theirs = norm_half(scalars, swap_core(inputs), [normed_own])
    kept_a, sent_a, kept_b, sent_b = outer_pieces(
        scalars, normed_own, normed_theirs, cotangent, swap_core(cotangent)
    )
    n, m = 3 * HALF, D // 4
    a0, b0, stem_units = join(
        halves_kernel, "halves", [(n + 2 * m, QUARTER)] * 2 + [units],
        [sent_a, sent_b, *around, stem_weight], aliases={0: 0, 1: 1},
    )

    a, b, packed, stem_pair, own_a, own_b = join(
        site_step_kernel, "site_step", [(2 * n + m, QUARTER)] * 2 + [(D + 4 * n, QUARTER), (2, *units)],
        [
            proj_weight, stem_weight, a0, b0, swap_site(a0, 1), swap_site(b0, 2),
            stem_units, swap_z(stem_units, 2), kept_a, kept_b,
        ],
        [plan],
        wide_dims=[(m, QUARTER)] * 2,
    )

    a2, b2 = swap_site(a, 2), swap_site(b, 1)
    near = swap_z(stem_pair, 1)
    packed = swap_core(packed)
    kept, sent = site_sum(scalars, own_a, a2, own_b, b2)
    others, all_others, late = join(
        three_kernel, "three", [(3, *quarters), (3, *units), (4 * n, QUARTER)],
        [stem_pair, near, a2, b2], [kept, packed],
    )

    over = [swap_site(others, distance) for distance in (1, 2, 3)]
    late, late_stem = swap_core(late), swap_core(rows_of(all_others))
    whole_proj = [(0, 0, ("all", 0), 0, D // N_FSDP)]
    first = [half_places(0, 0) + half_places(1, 0), half_places(0, HALF) + half_places(2, HALF)]
    last = [half_places(2, 0) + half_places(3, 0), half_places(1, HALF) + half_places(3, HALF)]
    proj_parts = [
        (proj_weight, whole_proj, 0),
        (a, first[0] + [m], 0), (b, first[1] + [m], 0),
        (a2, last[0] + [m], 0), (b2, last[1] + [m], 0),
        (packed, shard_places(0, D // N_FSDP) + [D // 2] + sum(first, []), 1), (late, sum(last, []), 1),
    ]
    grad = input_gradient(scalars, proj_parts, inputs, cotangent)
    own, sent = near_sum(scalars, kept, swap_z(sent, 1), [grad])
    (over,) = join(collect_kernel, "collect", [(3, 3, *quarters)], over, [grad, sent, late_stem])
    over = rows_of(over)
    last = sum((unit_places(d) for d in (1, 2, 3)), [])
    whole_stem = [(tap, 0, ("all", 0), 0, STEM_ROWS) for tap in range(TAPS)]
    stem_parts = [
        (stem_weight.reshape(-1, D), whole_stem, 0),
        (
            packed,
            [D // 2] + sum((shard_places(tap, STEM_ROWS) for tap in range(TAPS)), []) + [4 * n], 1,
        ),
        (rows_of(all_others), all_places(), 0), (over, last, 0),
        (late_stem, all_places(), 1), (swap_core(over), last, 1),
    ]

    payloads = stem_payloads(plan, stem_parts, grad)
    received = {0: payloads[0]}
    for d in PAYLOAD_ORDER[1:]:
        received[d] = lax.ppermute(payloads[d], "fsdp", [(i, i ^ d) for i in range(N_FSDP)])
    scale = 1.0 / math.sqrt(N_SITE * N_FSDP * ROWS)
    terms = far_sum(scalars, own, swap_z(sent, 2), scale, [received[4]])
    terms = [terms] + [swap_site(terms, d) for d in (1, 2, 3)]
    stem_grad, weight_grad = owner_rows(plan, [received[d] for d in PAYLOAD_ORDER], terms)
    return (stem_grad[None], weight_grad)


def plain_body(held_input, held_cotangent, proj_weight, stem_weight, seg_counts):
    group_size = lax.axis_size("fsdp")
    capacity = 2 * ((OWN_SEG + 2 * group_size - 1) // (2 * group_size))
    my_index = lax.axis_index("fsdp")
    cotangent = held_cotangent[0]
    normed, inverse = normalise(held_input[0])
    normed_bf = normed.astype(jnp.bfloat16)
    proj_back = dot_nt(cotangent, lax.all_gather(proj_weight, "fsdp", axis=0, tiled=True))
    input_grad = cotangent.astype(jnp.float32) + inverse * (
        proj_back
        - jnp.mean(proj_back, axis=-1, keepdims=True)
        - normed * jnp.mean(proj_back * normed, axis=-1, keepdims=True)
    )
    input_grad = input_grad.astype(jnp.bfloat16)
    counts = seg_counts[0]
    endings = jnp.cumsum(counts)
    starts = endings - counts
    slot_ids = jnp.arange(HOLD, dtype=jnp.int32)
    item_index = 2 * (slot_ids // 2 * group_size + my_index) + slot_ids % 2
    owner_ids = jnp.sum((item_index[:, None] >= endings[None, :]).astype(jnp.int32), axis=1)
    earlier = (slot_ids[None, :] < slot_ids[:, None]) & (owner_ids[None, :] == owner_ids[:, None])
    rank_ids = jnp.sum(earlier.astype(jnp.int32), axis=1)
    target = owner_ids * capacity + rank_ids
    positions = jnp.arange(group_size * capacity, dtype=jnp.int32)
    matched = target[None, :] == positions[:, None]
    filled = jnp.any(matched, axis=1)
    source = jnp.sum(jnp.where(matched, slot_ids[None, :], 0), axis=1)
    owner_hit = jnp.arange(group_size, dtype=jnp.int32) == my_index
    my_count = jnp.sum(jnp.where(owner_hit, counts, 0))
    my_start = jnp.sum(jnp.where(owner_hit, starts, 0))
    segment = jnp.arange(OWN_SEG, dtype=jnp.int32)
    is_live = segment < my_count
    holder = (my_start + segment) // 2 % group_size
    before = (
        (segment[None, :] < segment[:, None])
        & (holder[None, :] == holder[:, None])
        & is_live[None, :]
    )
    holder_rank = jnp.sum(before.astype(jnp.int32), axis=1)
    row_index = jnp.where(is_live, holder * capacity + holder_rank, 0)
    held_segments = input_grad.reshape(HOLD, SEG, D)
    zero_bf = jnp.zeros((), jnp.bfloat16)
    send_rows = jnp.where(filled[:, None, None], jnp.take(held_segments, source, axis=0), zero_bf)
    received = lax.all_to_all(
        send_rows.reshape(group_size, capacity, SEG, D), "fsdp", split_axis=0, concat_axis=0, tiled=True
    )
    picked = jnp.take(received.reshape(group_size * capacity, SEG, D), row_index, axis=0)
    frames = jnp.where(is_live[:, None, None], picked, zero_bf).reshape(OWN_SEG * SEG, D)
    tap_terms = jnp.einsum(
        "rd,kcd->krc",
        frames,
        lax.all_gather(stem_weight, "fsdp", axis=1, tiled=True),
        preferred_element_type=jnp.float32,
    )
    shifted = jnp.concatenate(
        [tap_terms[0][1:], jnp.zeros((1, tap_terms.shape[2]), jnp.float32)], 0
    )
    stem_rows = (
        jnp.stack([tap_terms[1], tap_terms[2] + shifted], 1)
        .reshape(2 * OWN_SEG * SEG, tap_terms.shape[2])
        .astype(jnp.bfloat16)
    )
    shard_sum = lax.psum_scatter(
        lax.dot_general(
            normed_bf, cotangent, (((0,), (0,)), ((), ())), preferred_element_type=jnp.float32
        ),
        "fsdp",
        scatter_dimension=0,
        tiled=True,
    )
    shard_sum = lax.psum(shard_sum, "site")
    weight_grad = shard_sum / math.sqrt(lax.axis_size("site") * group_size * ROWS)
    return (stem_rows[None], weight_grad)


def solution(mesh):
    placed = (
        P("site", "fsdp", None),
        P("site", "fsdp", None),
        P("fsdp", None),
        P(None, "fsdp", None),
        P("site", None),
    )
    fits = (mesh.shape["site"], mesh.shape["fsdp"]) == (N_SITE, N_FSDP)
    return jax.shard_map(
        body if fits else plain_body,
        mesh=mesh,
        in_specs=placed,
        out_specs=(P("site", "fsdp", None), P("fsdp", None)),
        check_vma=False,
    )
```

```python
import math

import jax
import jax.numpy as jnp
from jax import lax
from jax.experimental import pallas as pl
from jax.experimental.pallas import tpu as pltpu
from jax.sharding import PartitionSpec as P

D = 1536
SEG = 8
HOLD = 64
OWN_SEG = 128
N_SITE = 4
N_FSDP = 8
N_Z = N_FSDP // 2
QUARTER = D // N_SITE
CAP = OWN_SEG // N_FSDP
CS = 512
ROWS = HOLD * SEG
BLOCK = 256
LANES = 128
COLUMNS = 512
PAYLOAD_ORDER = (0, 4, 5, 2, 3, 6, 7, 1)
MIB = 1024 * 1024

EPSILON = 1e-05
F32 = jnp.float32
BF16 = jnp.bfloat16


def swap_core(value):
    return lax.ppermute(value, "fsdp", [(i, i ^ 1) for i in range(N_FSDP)])


def swap_z(value, distance):
    return lax.ppermute(value, "fsdp", [(i, i ^ (2 * distance)) for i in range(N_FSDP)])


def swap_site(value, distance):
    return lax.ppermute(value, "site", [(i, i ^ distance) for i in range(N_SITE)])


def hold(value, *first):
    return pl.pallas_call(
        lambda *refs: None,
        name="hold",
        out_shape=shape(value.shape, value.dtype),
        in_specs=[HBM] + [ANY] * len(first),
        out_specs=HBM,
        input_output_aliases={0: 0},
        cost_estimate=pl.CostEstimate(flops=0, bytes_accessed=0, transcendentals=0),
    )(value, *first)


Z_ORDER = (2, 1, 3)
HALF = D // N_FSDP // 2
STEM_ROWS = CS // N_FSDP
TAPS = 3


def half_places(site, low):
    return [(0, z, ("xor", site), low, HALF) for z in Z_ORDER]


SPLIT = STEM_ROWS // 4
QUARTER_BLOCKS = ((1, 0, STEM_ROWS), (0, 0, SPLIT))
WHOLE_BLOCKS = ((2, 0, STEM_ROWS), (0, SPLIT, STEM_ROWS - SPLIT))
QUARTER_ROWS = sum(count for _, _, count in QUARTER_BLOCKS)
UNIT_ROWS = QUARTER_ROWS + N_SITE * sum(count for _, _, count in WHOLE_BLOCKS)


def unit_places(site):
    return [(tap, z, ("xor", site), low, count) for z in Z_ORDER for tap, low, count in QUARTER_BLOCKS]


def all_places():
    blocks = [(tap, ("xor", 0), low, count) for tap, low, count in QUARTER_BLOCKS]
    blocks += [(tap, ("abs", j), low, count) for tap, low, count in WHOLE_BLOCKS for j in range(N_SITE)]
    return [(tap, z, kind, low, count) for z in Z_ORDER for tap, kind, low, count in blocks]


def shard_places(tap, count):
    return [(tap, 0, ("abs", j), 0, count) for j in range(N_SITE)]


def rows_of(value):
    return value.reshape(-1, QUARTER)


def call(kernel, name, out_shape, grid, in_specs, out_specs, scratch, vmem=16):
    return pl.pallas_call(
        kernel,
        name=name,
        out_shape=out_shape,
        grid_spec=pltpu.PrefetchScalarGridSpec(
            num_scalar_prefetch=1,
            grid=grid,
            in_specs=in_specs,
            out_specs=out_specs,
            scratch_shapes=scratch,
        ),
        compiler_params=pltpu.CompilerParams(
            dimension_semantics=("arbitrary",) * len(grid), vmem_limit_bytes=vmem * MIB
        ),
        cost_estimate=pl.CostEstimate(flops=0, bytes_accessed=0, transcendentals=0),
    )


ANY = pl.BlockSpec(memory_space=pl.ANY)
HBM = pl.BlockSpec(memory_space=pltpu.HBM)


def whole(shape):
    return pl.BlockSpec(shape, lambda i, scalars: (0,) * len(shape))


def row_block(rows, columns):
    return pl.BlockSpec((rows, columns), lambda i, scalars: (i, 0))


def shape(dims, dtype):
    return jax.ShapeDtypeStruct(dims, dtype)


def dot_nt(a, b):
    return lax.dot_general(a, b, (((1,), (1,)), ((), ())), preferred_element_type=F32)


def join(kernel, name, out_dims, values, first=(), wide_dims=(), aliases=None):
    n = len(values)

    def wrapped(*refs):
        kernel(*refs[:n], *refs[n + len(first) :])

    out = tuple(shape(dims, BF16) for dims in out_dims) + tuple(shape(dims, F32) for dims in wide_dims)
    vmem = pl.BlockSpec(memory_space=pltpu.VMEM)
    return pl.pallas_call(
        wrapped,
        name=name,
        out_shape=out,
        in_specs=[vmem] * n + [ANY] * len(first),
        out_specs=(vmem,) * len(out),
        input_output_aliases=aliases or {},
        compiler_params=pltpu.CompilerParams(vmem_limit_bytes=14 * MIB),
        cost_estimate=pl.CostEstimate(flops=0, bytes_accessed=0, transcendentals=0),
    )(*values, *first)


def cut_proj_kernel(shard, out):
    at = pl.multiple_of(lax.axis_index("site") * QUARTER, QUARTER)
    out[...] = shard[:, pl.ds(at, QUARTER)]


def halves_kernel(_, __, far, near, farthest, stem, a, b, units):
    for i, piece in enumerate((far, near, farthest)):
        a[i * HALF : (i + 1) * HALF, :] = piece[:HALF, :]
        b[i * HALF : (i + 1) * HALF, :] = piece[HALF:, :]
    at = pl.multiple_of(lax.axis_index("site") * QUARTER, QUARTER)
    pieces = [stem[tap, low : low + count, pl.ds(at, QUARTER)] for tap, low, count in QUARTER_BLOCKS]
    for tap, low, count in WHOLE_BLOCKS:
        pieces += column_pieces(stem[tap, low : low + count, :])
    pack_rows(units, pieces)


def pack_rows(out, pieces):
    at = 0
    for piece in pieces:
        out[at : at + piece.shape[0], :] = piece
        at += piece.shape[0]


def column_pieces(rows):
    return [rows[:, i * QUARTER : (i + 1) * QUARTER] for i in range(N_SITE)]


def site_step_kernel(
    shard, stem, a0, b0, a1, b1, units, far, kept_a, kept_b, a, b, packed, pair, own_a, own_b
):
    pair[0], pair[1] = units[...], far[...]
    n, m = 3 * HALF, D // 4
    for sent, came, kept, out, own in ((a0, a1, kept_a, a, own_a), (b0, b1, kept_b, b, own_b)):
        for j, source in enumerate((sent, came)):
            out[j * n : (j + 1) * n, :] = source[:n, :]
        own[...] = kept[0] + came[n : n + m, :].astype(F32)
        out[2 * n :, :] = (kept[1] + came[n + m :, :].astype(F32)).astype(BF16)
    pieces = column_pieces(shard[...])
    for tap in range(TAPS):
        pieces += column_pieces(stem[tap])
    pack_rows(packed, pieces + [ref[:n, :] for ref in (a0, a1, b0, b1)])


def collect_kernel(a, b, c, out):
    out[0], out[1], out[2] = a[...], b[...], c[...]


def three_kernel(pair, near, a2, b2, quarters, units, packed):
    n = 6 * HALF
    packed[:n, :], packed[n:, :] = a2[:n, :], b2[:n, :]
    for i, piece in enumerate((pair.at[1], near.at[0], near.at[1])):
        quarters[i] = piece[:QUARTER_ROWS, :]
        units[i] = piece[...]


def normalise(inputs):
    inputs = inputs.astype(F32)
    centered = inputs - jnp.mean(inputs, axis=-1, keepdims=True)
    variance = jnp.mean(centered * centered, axis=-1, keepdims=True)
    inverse = lax.rsqrt(variance + EPSILON)
    return centered * inverse, inverse


def norm_kernel(scalars, x_ref, *refs):
    out_ref, turned = refs[-2:]
    core = scalars[1] % 2
    normed, _ = normalise(x_ref[...])
    turned[...] = normed.astype(BF16).T
    shard = D // N_FSDP
    for z in range(N_Z):
        rows = pl.ds(pl.multiple_of((2 * z + core) * shard, shard), shard)
        out_ref[pl.ds(z * shard, shard), :] = turned[rows, :]


def norm_half(scalars, inputs, first=()):
    return call(
        norm_kernel, "norm_half", shape((D // 2, ROWS), BF16), (ROWS // BLOCK,),
        [row_block(BLOCK, D)] + [ANY] * len(first),
        pl.BlockSpec((D // 2, BLOCK), lambda i, scalars: (0, i)), [pltpu.VMEM((D, BLOCK), BF16)],
    )(scalars, inputs, *first)


OUTER_PLACES = (((0, 0), (0, 0)), ((1, 0), (0, 1)), ((0, 1), (1, 0)), ((1, 1), (1, 1)))


def outer_kernel(scalars, na_ref, nb_ref, ca_ref, cb_ref, ka_ref, a_ref, kb_ref, b_ref):
    site = scalars[0]
    n, m = 3 * HALF, D // 4
    for half in range(2):
        start = lax.bitwise_xor(site // 2, half) * 2 * QUARTER
        columns = pl.ds(pl.multiple_of(start, 2 * QUARTER), 2 * QUARTER)
        total = jnp.dot(na_ref[...], ca_ref[:, columns], preferred_element_type=F32)
        total = total + jnp.dot(nb_ref[...], cb_ref[:, columns], preferred_element_type=F32)
        low, high = total[:, :QUARTER], total[:, QUARTER:]
        odd = site % 2 == 1
        for at, value in ((2 * half, jnp.where(odd, high, low)), (2 * half + 1, jnp.where(odd, low, high))):
            for (goes, i), kept, sent, rows in zip(
                OUTER_PLACES[at], (ka_ref, kb_ref), (a_ref, b_ref), (value[:m, :], value[m:, :]), strict=True
            ):
                if goes:
                    sent[n + i * m : n + (i + 1) * m, :] = rows.astype(BF16)
                else:
                    kept[i] = rows


def outer_pieces(scalars, normed_a, normed_b, cotangent_a, cotangent_b):
    kept, sent = (2, D // 4, QUARTER), (3 * HALF + D // 2, QUARTER)
    values = (normed_a, normed_b, cotangent_a, cotangent_b)
    return call(
        outer_kernel, "outer_pieces", (shape(kept, F32), shape(sent, BF16)) * 2, (1,),
        [whole(value.shape) for value in values], (whole(kept), whole(sent)) * 2, [], vmem=24,
    )(scalars, *values)


def site_sum_kernel(scalars, oa_ref, ra_ref, ob_ref, rb_ref, kept_ref, sent_ref, total):
    shard = D // N_FSDP
    z = scalars[1] // 2
    total[: D // 4, :] = oa_ref[...] + ra_ref[6 * HALF :, :].astype(F32)
    total[D // 4 :, :] = ob_ref[...] + rb_ref[6 * HALF :, :].astype(F32)
    for distance, (ref, i) in enumerate(((kept_ref, 0), (sent_ref, 0), (kept_ref, 1), (sent_ref, 1))):
        rows = pl.ds(pl.multiple_of(lax.bitwise_xor(z, distance) * shard, shard), shard)
        ref[i] = total[rows, :].astype(ref.dtype)


def site_sum(scalars, *values):
    out = (2, D // N_FSDP, QUARTER)
    return call(
        site_sum_kernel, "site_sum", (shape(out, F32), shape(out, BF16)), (1,),
        [whole(value.shape) for value in values], (whole(out),) * 2, [pltpu.VMEM((D // 2, QUARTER), F32)],
    )(scalars, *values)


def near_sum_kernel(scalars, kept_ref, came_ref, *refs):
    own_ref, sent_ref = refs[-2:]
    own_ref[...] = kept_ref[0] + came_ref[0].astype(F32)
    sent_ref[...] = (kept_ref[1] + came_ref[1].astype(F32)).astype(BF16)


def near_sum(scalars, kept, came, first):
    dims, out = (2, D // N_FSDP, QUARTER), (D // N_FSDP, QUARTER)
    return call(
        near_sum_kernel, "near_sum", (shape(out, F32), shape(out, BF16)), (1,),
        [whole(dims)] * 2 + [ANY] * len(first), (whole(out),) * 2, [],
    )(scalars, kept, came, *first)


def far_sum_kernel(scale, scalars, own_ref, came_ref, *refs):
    refs[-1][...] = (own_ref[...] + came_ref[...].astype(F32)) * scale


def far_sum(scalars, own, came, scale, first):
    dims = (D // N_FSDP, QUARTER)
    return call(
        lambda *refs: far_sum_kernel(scale, *refs), "far_sum", shape(dims, F32), (1,),
        [whole(dims)] * 2 + [ANY] * len(first), whole(dims), [],
    )(scalars, own, came, *first)


def weight_copies(tables, scalars, refs, weight, sem):
    site, index = scalars[0], scalars[1]
    shard = weight.shape[1] // N_FSDP
    copies = []
    for (places, swapped), ref in zip(tables, refs, strict=True):
        at = 0
        for place in places:
            if isinstance(place, int):
                at += place
                continue
            tap, z, (kind, quarter), low, count = place
            start = lax.bitwise_xor(index, 2 * z + swapped) * shard + low
            rows = pl.ds(pl.multiple_of(start, math.gcd(shard, low)), count)
            columns = pl.ds(quarter * QUARTER, QUARTER)
            if kind == "all":
                columns = pl.ds(0, D)
            elif kind == "xor":
                column = lax.bitwise_xor(site, quarter) * QUARTER
                columns = pl.ds(pl.multiple_of(column, QUARTER), QUARTER)
            source = ref.at[pl.ds(at, count), :]
            copies.append(pltpu.make_async_copy(source, weight.at[tap, rows, columns], sem))
            at += count
        assert at == ref.shape[0]
    return copies


def fetch(source, target, sem):
    copy = pltpu.make_async_copy(source, target, sem)
    copy.start()
    return copy


def input_grad_kernel(tables, scalars, *refs):
    n = len(tables)
    parts, (x_hbm, cot_hbm, out_ref) = refs[:n], refs[n : n + 3]
    x_ref, cot_ref, weight, normed, inverse, back, sems, sem = refs[n + 3 :]
    x_copy = fetch(x_hbm, x_ref, sems.at[0])
    cot_copy = fetch(cot_hbm, cot_ref, sems.at[1])
    copies = weight_copies(tables, scalars, parts, weight, sem)
    for copy in copies:
        copy.start()
    x_copy.wait()

    @pl.loop(0, ROWS // BLOCK)
    def _(i):
        rows = pl.ds(pl.multiple_of(i * BLOCK, BLOCK), BLOCK)
        normed[rows, :], inverse[rows, :] = normalise(x_ref[rows, :])

    cot_copy.wait()
    for copy in copies:
        copy.wait()

    def finish(rows):
        term, row_normed = back[rows, :], normed[rows, :]
        inner = term - jnp.mean(term, axis=-1, keepdims=True)
        inner = inner - row_normed * jnp.mean(term * row_normed, axis=-1, keepdims=True)
        out_ref[rows, :] = (cot_ref[rows, :].astype(F32) + inverse[rows, :] * inner).astype(BF16)

    half = ROWS // 2
    for i in range(3):
        if i < 2:
            rows = slice(i * half, (i + 1) * half)
            for j in range(D // COLUMNS):
                columns = slice(j * COLUMNS, (j + 1) * COLUMNS)
                back[rows, columns] = dot_nt(cot_ref[rows, :], weight[0, columns, :])
        if i > 0:
            for j in range(4):
                start = (i - 1) * half + j * half // 4
                finish(slice(start, start + half // 4))


def split_parts(parts):
    return [(places, swapped) for _, places, swapped in parts], [value for value, _, _ in parts]


def input_gradient(scalars, parts, inputs, cotangent):
    tables, values = split_parts(parts)
    return call(
        lambda *refs: input_grad_kernel(tables, *refs), "input_gradient", shape((ROWS, D), BF16),
        (1,), [HBM] * (len(values) + 2), whole((ROWS, D)),
        [
            pltpu.VMEM((ROWS, D), BF16),
            pltpu.VMEM((ROWS, D), BF16),
            pltpu.VMEM((1, D, D), BF16),
            pltpu.VMEM((ROWS, D), F32),
            pltpu.VMEM((ROWS, 1), F32),
            pltpu.VMEM((ROWS, D), F32),
            pltpu.SemaphoreType.DMA((2,)),
            pltpu.SemaphoreType.DMA,
        ],
        vmem=22,
    )(scalars, *values, inputs, cotangent)


def held_before(start, holder):
    return 2 * (start // (2 * N_FSDP)) + jnp.clip(start % (2 * N_FSDP) - 2 * holder, 0, 2)


PAIRS = CAP // 2
BASES_AT = 2
SPLITS_AT = BASES_AT + N_FSDP
SEGMENTS_AT = SPLITS_AT + N_FSDP
BEFORE_AT = SEGMENTS_AT + N_FSDP * CAP
COUNT_AT = BEFORE_AT + N_FSDP * PAIRS


def plan_kernel(scalars, plan):
    site, index = scalars[0], scalars[1]
    plan[0], plan[1] = site, index
    count = scalars[2 + index]
    plan[COUNT_AT] = count
    starts = [jnp.int32(0)]
    for owner in range(N_FSDP):
        starts.append(starts[-1] + scalars[2 + owner])
    my_start = jnp.int32(0)
    for owner in range(N_FSDP):
        start = starts[owner]
        plan[BASES_AT + lax.bitwise_xor(index, owner)] = held_before(start, index)
        my_start = my_start + jnp.where(owner < index, scalars[2 + owner], 0)
        splits = (start % 2 == 1) & (start // 2 % N_FSDP == index)
        plan[SPLITS_AT + owner] = jnp.where(splits, 2 * (start // (2 * N_FSDP)) * SEG + SEG - 1, -1)

    @pl.loop(0, N_FSDP * CAP)
    def _(block):
        holder = lax.bitwise_xor(index, block // CAP)
        slot = held_before(my_start, holder) + block % CAP
        segment = 2 * (slot // 2 * N_FSDP + holder) + slot % 2 - my_start
        held = (segment >= 0) & (segment < count)
        plan[SEGMENTS_AT + block] = jnp.where(held, segment, OWN_SEG)

    @pl.loop(0, N_FSDP * PAIRS)
    def _(block):
        holder = lax.bitwise_xor(index, block // PAIRS)
        segment = 2 * (even_slot(held_before(my_start, holder), block % PAIRS) // 2 * N_FSDP + holder) - my_start
        held = (segment > 0) & (segment < count)
        plan[BEFORE_AT + block] = jnp.where(held, segment - 1, OWN_SEG)


def even_slot(base, i):
    return base + base % 2 + 2 * i


def plan_of(scalars):
    return call(
        plan_kernel, "plan", shape((COUNT_AT + 1,), jnp.int32), (1,), [],
        pl.BlockSpec(memory_space=pltpu.SMEM), [],
    )(scalars)


def stem_kernel(tables, scalars, *refs):
    n = len(tables)
    parts, grad_ref, outs = refs[:n], refs[n], refs[n + 1 : n + 1 + N_FSDP]
    weight, mixed, leading, firsts, sem = refs[n + 1 + N_FSDP :]
    copies = weight_copies(tables, scalars, parts, weight, sem)
    for copy in copies:
        copy.start()
    for copy in copies:
        copy.wait()
    row = lax.broadcasted_iota(jnp.int32, (ROWS, LANES), 0)
    inside = row % (2 * SEG) == SEG - 1
    for owner in range(1, N_FSDP):
        inside = inside & (row != scalars[SPLITS_AT + owner])
    inside = inside | (row % SEG != SEG - 1)
    for lane in range(0, CS, CS // 2):
        span = pl.ds(lane, CS // 2)
        even = dot_nt(grad_ref[...], weight[1, span, :])
        first = dot_nt(grad_ref[...], weight[0, span, :])
        leading[:, span] = first
        following = pltpu.roll(first, ROWS - 1, 0)
        odd = dot_nt(grad_ref[...], weight[2, span, :])
        for part in range(CS // 2 // LANES):
            at = lane // LANES + part
            columns = slice(part * LANES, (part + 1) * LANES)
            mixed[at, pl.ds(0, ROWS, stride=2), :] = even[:, columns]
            mixed[at, pl.ds(1, ROWS, stride=2), :] = odd[:, columns] + jnp.where(
                inside, following[:, columns], 0.0
            )

    for place, out in enumerate(outs):
        base = scalars[BASES_AT + place]
        for rank in range(CAP):
            slot = jnp.minimum(base + rank, HOLD - 1)
            rows = pl.ds(pl.multiple_of(slot * 2 * SEG, 2 * SEG), 2 * SEG)
            for lane in range(CS // LANES):
                at, columns = divmod(lane * LANES, CS // 2)
                out[2 * rank + at, :, columns : columns + LANES] = mixed[lane, rows, :].astype(BF16)
        for i in range(PAIRS):
            slot = jnp.minimum(even_slot(base, i), HOLD - 1)
            first = leading[pl.ds(slot * SEG, 1), :]
            for at in range(2):
                firsts[at * PAIRS + i : at * PAIRS + i + 1, :] = first[:, at * CS // 2 : (at + 1) * CS // 2]
        out[2 * CAP] = firsts[...].astype(BF16)


VMEM = pl.BlockSpec(memory_space=pltpu.VMEM)


def stem_payloads(scalars, parts, grad):
    tables, values = split_parts(parts)
    payload = (2 * CAP + 1, 2 * PAIRS, CS // 2)
    return call(
        lambda *refs: stem_kernel(tables, *refs), "stem_payloads",
        (shape(payload, BF16),) * N_FSDP, (1,),
        [ANY] * len(values) + [whole((ROWS, D))], (VMEM,) * N_FSDP,
        [
            pltpu.VMEM((3, CS, D), BF16),
            pltpu.VMEM((CS // LANES, 2 * ROWS, LANES), F32),
            pltpu.VMEM((ROWS, CS), F32),
            pltpu.VMEM((2 * PAIRS, CS // 2), F32),
            pltpu.SemaphoreType.DMA,
        ],
        vmem=18,
    )(scalars, *values, grad)


def owner_kernel(scalars, *refs):
    payloads, terms, (out_hbm, total), (out, sem, total_sem) = (
        refs[:N_FSDP], refs[N_FSDP : N_FSDP + N_SITE], refs[-5:-3], refs[-3:]
    )
    copies = []
    for distance, term in enumerate(terms):
        at = pl.multiple_of(lax.bitwise_xor(scalars[0], distance) * QUARTER, QUARTER)
        copies.append(
            pltpu.make_async_copy(term, total.at[:, pl.ds(at, QUARTER)], total_sem.at[distance])
        )
    for copy in copies:
        copy.start()

    def rows_of_segment(segment):
        return pl.ds(pl.multiple_of(segment * 2 * SEG, 2 * SEG), 2 * SEG)

    @pl.loop(scalars[COUNT_AT], OWN_SEG)
    def _(segment):
        out[rows_of_segment(segment), :] = jnp.zeros((2 * SEG, CS), BF16)

    halves = [slice(0, CS // 2), slice(CS // 2, CS)]
    for i, place in enumerate(PAYLOAD_ORDER):
        for rank in range(CAP):
            rows = rows_of_segment(scalars[SEGMENTS_AT + place * CAP + rank])
            for at, columns in enumerate(halves):
                out[rows, columns] = payloads[i][2 * rank + at]
    last_row = lax.broadcasted_iota(jnp.int32, (2 * SEG, CS // 2), 0) == 2 * SEG - 1
    for i, place in enumerate(PAYLOAD_ORDER):
        firsts = payloads[i][2 * CAP].astype(F32)
        for pair in range(PAIRS):
            rows = rows_of_segment(scalars[BEFORE_AT + place * PAIRS + pair])
            for at, columns in enumerate(halves):
                first = firsts[at * PAIRS + pair : at * PAIRS + pair + 1, :]
                term = jnp.where(last_row, jnp.broadcast_to(first, last_row.shape), 0.0)
                out[rows, columns] = (out[rows, columns].astype(F32) + term).astype(BF16)
    copies.append(fetch(out.at[pl.ds(0, out_hbm.shape[0]), :], out_hbm, sem))
    for copy in copies:
        copy.wait()


def owner_rows(scalars, payloads, terms):
    rows = 2 * OWN_SEG * SEG
    return call(
        owner_kernel, "owner_rows", (shape((rows, CS), BF16), shape((D // N_FSDP, D), F32)), (1,),
        [VMEM] * N_FSDP + [ANY] * N_SITE, (HBM, HBM),
        [
            pltpu.VMEM((rows + 2 * SEG, CS), BF16),
            pltpu.SemaphoreType.DMA,
            pltpu.SemaphoreType.DMA((N_SITE,)),
        ],
    )(scalars, *payloads, *terms)


def body(held_input, held_cotangent, proj_weight, stem_weight, seg_counts):
    site, index = lax.axis_index("site"), lax.axis_index("fsdp")
    scalars = jnp.concatenate([jnp.stack([site, index]).astype(jnp.int32), seg_counts[0]])
    inputs, cotangent = held_input[0], held_cotangent[0]

    plan = plan_of(scalars)
    piece = (D // N_FSDP, QUARTER)
    half = (3, HALF, QUARTER)
    units = (UNIT_ROWS, QUARTER)
    quarters = (QUARTER_ROWS, QUARTER)

    (proj_quarter,) = join(cut_proj_kernel, "cut_proj", [piece], [proj_weight])
    around = [swap_z(proj_quarter, distance) for distance in Z_ORDER]
    normed_own = norm_half(scalars, inputs, [proj_quarter])
    normed_theirs = norm_half(scalars, swap_core(inputs), [normed_own])
    kept_a, sent_a, kept_b, sent_b = outer_pieces(
        scalars, normed_own, normed_theirs, cotangent, swap_core(cotangent)
    )
    n, m = 3 * HALF, D // 4
    a0, b0, stem_units = join(
        halves_kernel, "halves", [(n + 2 * m, QUARTER)] * 2 + [units],
        [sent_a, sent_b, *around, stem_weight], aliases={0: 0, 1: 1},
    )

    a, b, packed, stem_pair, own_a, own_b = join(
        site_step_kernel, "site_step", [(2 * n + m, QUARTER)] * 2 + [(D + 4 * n, QUARTER), (2, *units)],
        [
            proj_weight, stem_weight, a0, b0, swap_site(a0, 1), swap_site(b0, 2),
            stem_units, swap_z(stem_units, 2), kept_a, kept_b,
        ],
        [plan],
        wide_dims=[(m, QUARTER)] * 2,
    )

    a2, b2 = swap_site(a, 2), swap_site(b, 1)
    near = swap_z(stem_pair, 1)
    packed = swap_core(packed)
    kept, sent = site_sum(scalars, own_a, a2, own_b, b2)
    others, all_others, late = join(
        three_kernel, "three", [(3, *quarters), (3, *units), (4 * n, QUARTER)],
        [stem_pair, near, a2, b2], [kept, packed],
    )

    over = [swap_site(others, distance) for distance in (1, 2, 3)]
    late, late_stem = swap_core(late), swap_core(rows_of(all_others))
    whole_proj = [(0, 0, ("all", 0), 0, D // N_FSDP)]
    first = [half_places(0, 0) + half_places(1, 0), half_places(0, HALF) + half_places(2, HALF)]
    last = [half_places(2, 0) + half_places(3, 0), half_places(1, HALF) + half_places(3, HALF)]
    proj_parts = [
        (proj_weight, whole_proj, 0),
        (a, first[0] + [m], 0), (b, first[1] + [m], 0),
        (a2, last[0] + [m], 0), (b2, last[1] + [m], 0),
        (packed, shard_places(0, D // N_FSDP) + [D // 2] + sum(first, []), 1), (late, sum(last, []), 1),
    ]
    grad = input_gradient(scalars, proj_parts, inputs, cotangent)
    own, sent = near_sum(scalars, kept, swap_z(sent, 1), [grad])
    (over,) = join(collect_kernel, "collect", [(3, 3, *quarters)], over, [grad, sent, late_stem])
    over = rows_of(over)
    last = sum((unit_places(d) for d in (1, 2, 3)), [])
    whole_stem = [(tap, 0, ("all", 0), 0, STEM_ROWS) for tap in range(TAPS)]
    stem_parts = [
        (stem_weight.reshape(-1, D), whole_stem, 0),
        (
            packed,
            [D // 2] + sum((shard_places(tap, STEM_ROWS) for tap in range(TAPS)), []) + [4 * n], 1,
        ),
        (rows_of(all_others), all_places(), 0), (over, last, 0),
        (late_stem, all_places(), 1), (swap_core(over), last, 1),
    ]

    payloads = stem_payloads(plan, stem_parts, grad)
    received = {0: payloads[0]}
    for d in PAYLOAD_ORDER[1:]:
        received[d] = lax.ppermute(payloads[d], "fsdp", [(i, i ^ d) for i in range(N_FSDP)])
    scale = 1.0 / math.sqrt(N_SITE * N_FSDP * ROWS)
    terms = far_sum(scalars, own, swap_z(sent, 2), scale, [received[4]])
    terms = [terms] + [swap_site(terms, d) for d in (1, 2, 3)]
    stem_grad, weight_grad = owner_rows(plan, [received[d] for d in PAYLOAD_ORDER], terms)
    return (stem_grad[None], weight_grad)


def plain_body(held_input, held_cotangent, proj_weight, stem_weight, seg_counts):
    group_size = lax.axis_size("fsdp")
    capacity = 2 * ((OWN_SEG + 2 * group_size - 1) // (2 * group_size))
    my_index = lax.axis_index("fsdp")
    cotangent = held_cotangent[0]
    normed, inverse = normalise(held_input[0])
    normed_bf = normed.astype(jnp.bfloat16)
    proj_back = dot_nt(cotangent, lax.all_gather(proj_weight, "fsdp", axis=0, tiled=True))
    input_grad = cotangent.astype(jnp.float32) + inverse * (
        proj_back
        - jnp.mean(proj_back, axis=-1, keepdims=True)
        - normed * jnp.mean(proj_back * normed, axis=-1, keepdims=True)
    )
    input_grad = input_grad.astype(jnp.bfloat16)
    counts = seg_counts[0]
    endings = jnp.cumsum(counts)
    starts = endings - counts
    slot_ids = jnp.arange(HOLD, dtype=jnp.int32)
    item_index = 2 * (slot_ids // 2 * group_size + my_index) + slot_ids % 2
    owner_ids = jnp.sum((item_index[:, None] >= endings[None, :]).astype(jnp.int32), axis=1)
    earlier = (slot_ids[None, :] < slot_ids[:, None]) & (owner_ids[None, :] == owner_ids[:, None])
    rank_ids = jnp.sum(earlier.astype(jnp.int32), axis=1)
    target = owner_ids * capacity + rank_ids
    positions = jnp.arange(group_size * capacity, dtype=jnp.int32)
    matched = target[None, :] == positions[:, None]
    filled = jnp.any(matched, axis=1)
    source = jnp.sum(jnp.where(matched, slot_ids[None, :], 0), axis=1)
    owner_hit = jnp.arange(group_size, dtype=jnp.int32) == my_index
    my_count = jnp.sum(jnp.where(owner_hit, counts, 0))
    my_start = jnp.sum(jnp.where(owner_hit, starts, 0))
    segment = jnp.arange(OWN_SEG, dtype=jnp.int32)
    is_live = segment < my_count
    holder = (my_start + segment) // 2 % group_size
    before = (
        (segment[None, :] < segment[:, None])
        & (holder[None, :] == holder[:, None])
        & is_live[None, :]
    )
    holder_rank = jnp.sum(before.astype(jnp.int32), axis=1)
    row_index = jnp.where(is_live, holder * capacity + holder_rank, 0)
    held_segments = input_grad.reshape(HOLD, SEG, D)
    zero_bf = jnp.zeros((), jnp.bfloat16)
    send_rows = jnp.where(filled[:, None, None], jnp.take(held_segments, source, axis=0), zero_bf)
    received = lax.all_to_all(
        send_rows.reshape(group_size, capacity, SEG, D), "fsdp", split_axis=0, concat_axis=0, tiled=True
    )
    picked = jnp.take(received.reshape(group_size * capacity, SEG, D), row_index, axis=0)
    frames = jnp.where(is_live[:, None, None], picked, zero_bf).reshape(OWN_SEG * SEG, D)
    tap_terms = jnp.einsum(
        "rd,kcd->krc",
        frames,
        lax.all_gather(stem_weight, "fsdp", axis=1, tiled=True),
        preferred_element_type=jnp.float32,
    )
    shifted = jnp.concatenate(
        [tap_terms[0][1:], jnp.zeros((1, tap_terms.shape[2]), jnp.float32)], 0
    )
    stem_rows = (
        jnp.stack([tap_terms[1], tap_terms[2] + shifted], 1)
        .reshape(2 * OWN_SEG * SEG, tap_terms.shape[2])
        .astype(jnp.bfloat16)
    )
    shard_sum = lax.psum_scatter(
        lax.dot_general(
            normed_bf, cotangent, (((0,), (0,)), ((), ())), preferred_element_type=jnp.float32
        ),
        "fsdp",
        scatter_dimension=0,
        tiled=True,
    )
    shard_sum = lax.psum(shard_sum, "site")
    weight_grad = shard_sum / math.sqrt(lax.axis_size("site") * group_size * ROWS)
    return (stem_rows[None], weight_grad)


def solution(mesh):
    placed = (
        P("site", "fsdp", None),
        P("site", "fsdp", None),
        P("fsdp", None),
        P(None, "fsdp", None),
        P("site", None),
    )
    fits = (mesh.shape["site"], mesh.shape["fsdp"]) == (N_SITE, N_FSDP)
    return jax.shard_map(
        body if fits else plain_body,
        mesh=mesh,
        in_specs=placed,
        out_specs=(P("site", "fsdp", None), P("fsdp", None)),
        check_vma=False,
    )
```
